32 devices in a mesh: batch: 4 (over z), gran: 4 (over y, x), ffn: 2 (over core).
Axes of the slice: x: 2, y: 2, z: 4, core: 2. Of those that a mesh axis runs over, the one named last changes fastest.
Arguments:
- tokens: bfloat16 [4096, 1536], P(('batch', 'gran', 'ffn')), may hold values from -26 to 26
- seq_ids: int32 [4096], P(('batch', 'gran', 'ffn')), may hold values from 0 to 3, as said below
- granularity: int32 [128], P(('batch', 'gran', 'ffn')), may hold values from 0 to 3
- w_qkv: bfloat16 [1536, 4608], P('batch'), may hold values from -0.15625 to 0.15625
- w_out: bfloat16 [1536, 1536], P('batch'), may hold values from -1.75 to 1.75
- gain_attn: bfloat16 [1536], P('batch'), may hold values from 0.5 to 1.5
- gain_ffn: bfloat16 [1536], P('batch'), may hold values from 0.5 to 1.5
- w_gate: bfloat16 [1536, 2, 3072], P('batch', 'ffn'), may hold values from -0.15625 to 0.15625
- w_up: bfloat16 [1536, 2, 3072], P('batch', 'ffn'), may hold values from -0.15625 to 0.15625
- w_down: bfloat16 [3072, 2, 1536], P('batch', 'ffn'), may hold values from -0.21875 to 0.21875
- out_cotangent: bfloat16 [4096, 1536], P(('batch', 'gran', 'ffn')), may hold values from -6 to 6
Outputs:
- outputs: bfloat16 [4096, 1536], P(('batch', 'gran', 'ffn'))
- input_grad: bfloat16 [4096, 1536], P(('batch', 'gran', 'ffn'))
- grad_w_qkv: float32 [1536, 4608], P('batch')
- grad_w_out: float32 [1536, 1536], P('batch')
- grad_gain_attn: float32 [1536], P('batch')
- grad_gain_ffn: float32 [1536], P('batch')
- grad_w_gate: float32 [1536, 2, 3072], P('batch', 'ffn')
- grad_w_up: float32 [1536, 2, 3072], P('batch', 'ffn')
- grad_w_down: float32 [3072, 2, 1536], P('batch', 'ffn')
The draws below stay inside these ranges and needn't reach their ends.
Inputs may be any that keep to these rules, and one draw needn't show every extreme that they name: `seq_ids`: within each device's block of 128 rows the ids never fall; a sequence may have no rows; on some device one sequence fills all 128 rows, and on some device every sequence has rows. `granularity`: entry i is the group of sequence i mod 4 of the device holding the sequence ids of block i // 4.
All inputs are finite; a program needn't handle non-finite values.
Results may differ from the reference program's by a relative error of at most 0.02.
Values may be sent and summed in bfloat16 or wider, within the bound.
No kernel may reach another device: no remote copies, remote signals or barrier semaphores. Data moves between devices by JAX's collectives and lax.ppermute only.
A program may use at most 256 MiB of HBM per device.

```python
import functools
import math
import jax
import jax.numpy as jnp
from jax import lax

D = 1536
H = 12
FF = 6144
TOK_DEV = 128
SEQ_DEV = 4
TOKENS = 4096
SEQS = 128
CAP_PAIR = 10
N_BATCH = 4
N_GRAN = 4
N_FFN = 2
DEVICES = 32


def draw_tokens(key, part):
    key_base = jax.random.fold_in(key, 11)
    key_row = jax.random.fold_in(key, 12)
    key_col = jax.random.fold_in(key, 13)
    base = jnp.clip(jax.random.normal(key_base, (TOKENS, D), jnp.float32), -6.0, 6.0)
    rising = 0.5 + jnp.arange(TOKENS, dtype=jnp.float32)[:, None] / TOKENS
    row_scale = jnp.exp(jax.random.uniform(key_row, (TOKENS, 1), jnp.float32, -0.7, 0.7))
    col_scale = jnp.exp(jax.random.uniform(key_col, (1, D), jnp.float32, -0.35, 0.35))
    return (base * rising * row_scale * col_scale).astype(jnp.bfloat16)


def draw_seq_ids(key, part):
    key_cut = jax.random.fold_in(key, 21)
    key_pick = jax.random.fold_in(key, 22)
    raw_cuts = jax.random.randint(key_cut, (DEVICES, SEQ_DEV - 1), 0, TOK_DEV + 1)
    cuts = jnp.sort(raw_cuts * raw_cuts // TOK_DEV, axis=1)
    chosen = jax.random.randint(key_pick, (), 0, DEVICES)
    other = (chosen + 1) % DEVICES
    device_index = jnp.arange(DEVICES, dtype=jnp.int32)[:, None]
    even_cuts = jnp.arange(1, SEQ_DEV, dtype=jnp.int32) * TOK_DEV // SEQ_DEV
    cuts = jnp.where(device_index == chosen, TOK_DEV, jnp.where(device_index == other, even_cuts[None, :], cuts))
    row_index = jnp.arange(TOK_DEV, dtype=jnp.int32)
    labels = jnp.sum((row_index[None, :, None] >= cuts[:, None, :]).astype(jnp.int32), axis=2)
    return labels.reshape(DEVICES * TOK_DEV)


def with_ends(values, rng, low, top_value):
    longest = values.shape.index(max(values.shape))
    spots = []
    for shift in (0, 1):
        where = [jax.random.randint(jax.random.fold_in(rng, axis), (), 0, length) for axis, length in enumerate(values.shape)]
        where[longest] = (where[longest] + shift) % values.shape[longest]
        spots.append(tuple(where))
    return values.at[spots[0]].set(low).at[spots[1]].set(top_value)


def steps_of(key, dims, cuts, smallest, high):
    gain = 1.0
    for dim, blocks in cuts:
        steps = jax.random.uniform(jax.random.fold_in(jax.random.fold_in(key, 6), dim), (blocks,), jnp.float32, smallest / len(cuts), high / len(cuts))
        gain = gain * jnp.repeat(jnp.exp(steps), dims[dim] // blocks).reshape((-1,) + (1,) * (len(dims) - 1 - dim))
    return gain


def scatter_about(stream_key, dims, scale, most, pieces=(), kind=jnp.bfloat16):
    values = jax.random.normal(stream_key, dims, jnp.float32) * scale
    if len(pieces) > 0:
        values = steps_of(stream_key, dims, pieces, -0.22, 0.18) * values
    return jnp.clip(values, min=-most, max=most).astype(kind)


def setup_inputs(seed: int = 0) -> dict:
    keys = jax.random.split(jax.random.key(seed), 12)
    return {
        "tokens": draw_tokens(jax.random.fold_in(keys[11], 71), 0),
        "seq_ids": draw_seq_ids(jax.random.fold_in(keys[11], 71), 0),
        "granularity": with_ends(jax.random.randint(keys[2], (SEQS,), 0, N_GRAN), jax.random.fold_in(keys[2], 1), 0, N_GRAN - 1).astype(jnp.int32),
        "w_qkv": scatter_about(keys[3], (D, 3 * D), D ** -0.5, 0.15625, ((0, 4),)),
        "w_out": scatter_about(keys[4], (D, D), (max(4, D // 128)) ** -0.5, 1.75, ((0, 4),)),
        "gain_attn": jnp.clip(1.0 + 0.1 * jax.random.normal(keys[5], (D,), jnp.float32), 0.5, 1.5).astype(jnp.bfloat16),
        "gain_ffn": jnp.clip(1.0 + 0.1 * jax.random.normal(keys[6], (D,), jnp.float32), 0.5, 1.5).astype(jnp.bfloat16),
        "w_gate": scatter_about(keys[7], (D, N_FFN, FF // N_FFN), D ** -0.5, 0.15625, ((0, 4), (1, 2))),
        "w_up": scatter_about(keys[8], (D, N_FFN, FF // N_FFN), D ** -0.5, 0.15625, ((0, 4), (1, 2))),
        "w_down": scatter_about(keys[9], (FF // N_FFN, N_FFN, D), (FF // 8) ** -0.5, 0.21875, ((0, 4), (1, 2))),
        "out_cotangent": scatter_about(keys[10], (TOKENS, D), 1.0, 6.0, ((0, 32),)),
    }


@jax.custom_vjp
def low(v):
    return lax.optimization_barrier(v.astype(jnp.bfloat16)).astype(jnp.float32)

@jax.custom_vjp
def low_back(v):
    return v

def low_keep(v):
    return (low(v), None)

def low_pass(kept, grad):
    return (grad,)

def back_keep(v):
    return (v, None)

def back_low(kept, grad):
    return (low(grad),)
low.defvjp(low_keep, low_pass)
low_back.defvjp(back_keep, back_low)
EPSILON = 1e-06
NEG_FILL = -1e+30
ROPE_BASE = 10000.0
PRECISE = lax.Precision.HIGHEST

def seq_positions(seq_rows, seq_count):
    labels = jnp.arange(seq_count, dtype=jnp.int32)
    member = (seq_rows[:, None] == labels[None, :]).astype(jnp.int32)
    lengths = lax.optimization_barrier(jnp.sum(member, axis=0))
    starts = jnp.cumsum(lengths) - lengths
    first_row = lax.optimization_barrier(jnp.sum(member * starts[None, :], axis=1))
    return jnp.arange(seq_rows.shape[0], dtype=jnp.int32) - first_row

def route_rows(seq_rows, seq_groups, batch_index, batch_count, group_count, capacity):
    labels = jnp.arange(seq_groups.shape[0], dtype=jnp.int32)
    member = (seq_rows[:, None] == labels[None, :]).astype(jnp.int32)
    group_id = lax.optimization_barrier(jnp.sum(member * seq_groups[None, :], axis=1))
    onehot = (group_id[:, None] == jnp.arange(group_count, dtype=jnp.int32)[None, :]).astype(jnp.int32)
    before = jnp.cumsum(onehot, axis=0) - onehot
    order_rank = lax.optimization_barrier(jnp.sum(before * onehot, axis=1))
    keep_row = order_rank < capacity * batch_count
    target = (batch_index + order_rank) % batch_count
    slot_index = order_rank // batch_count
    return (group_id, keep_row, target, slot_index)

def rotate_half(vectors, cosines, sines):
    half_size = vectors.shape[-1] // 2
    front_half = vectors[..., :half_size]
    back_part = vectors[..., half_size:]
    return jnp.concatenate([front_half * cosines - back_part * sines, back_part * cosines + front_half * sines], axis=-1)

def rms_scale(values):
    return lax.rsqrt(lax.optimization_barrier(jnp.mean(values * values, axis=-1, keepdims=True)) + EPSILON)

def layer(parameters, residual, seq_rows, keep_row, group_id):
    w_qkv, w_out, gain_attn, gain_ffn, w_gate, w_up, w_down = parameters
    blocks, row_count, feature_count = residual.shape
    head_size = feature_count // H
    normed = low(residual * rms_scale(residual) * gain_attn)
    packed = low_back(jnp.einsum('btd,de->bte', normed, w_qkv, precision=PRECISE))
    packed = packed.reshape(blocks, row_count, 3, H, head_size)
    positions = jax.vmap(functools.partial(seq_positions, seq_count=SEQ_DEV))(seq_rows)
    frequencies = ROPE_BASE ** (-(2.0 * jnp.arange(head_size // 2, dtype=jnp.float32)) / head_size)
    angles = positions.astype(jnp.float32)[..., None] * frequencies
    cosines = jnp.cos(angles)[:, :, None, :]
    sines = jnp.sin(angles)[:, :, None, :]
    score_scale = 1.0 / math.sqrt(head_size)
    queries = low_back(low(rotate_half(packed[:, :, 0], cosines, sines) * score_scale))
    keys_rot = low_back(low(rotate_half(packed[:, :, 1], cosines, sines)))
    values = low_back(low(packed[:, :, 2]))
    scores = low_back(jnp.einsum('bqhe,bkhe->bhqk', queries, keys_rot, precision=PRECISE))
    row_index = jnp.arange(row_count, dtype=jnp.int32)
    allowed = (seq_rows[:, :, None] == seq_rows[:, None, :]) & (row_index[:, None] >= row_index[None, :])[None]
    scores = jnp.where(allowed[:, None], scores, NEG_FILL)
    probs = jax.nn.softmax(scores, axis=-1)
    attended = jnp.einsum('bhqk,bkhe->bqhe', low(probs), values, precision=PRECISE)
    attended = low_back(low(attended.reshape(blocks, row_count, feature_count)))
    branch_attn = low_back(jnp.einsum('btd,de->bte', attended, w_out, precision=PRECISE))
    middle = residual + branch_attn
    normed_ffn = low_back(low(middle * rms_scale(middle) * gain_ffn))
    gate_pre = low_back(jnp.einsum('btd,dcf->btcf', normed_ffn, w_gate, precision=PRECISE))
    lifted = low_back(jnp.einsum('btd,dcf->btcf', normed_ffn, w_up, precision=PRECISE))
    half_units = w_gate.shape[2]
    prefix = jnp.right_shift(jnp.int32(half_units), 3 - group_id)
    live_cols = (jnp.arange(half_units, dtype=jnp.int32)[None, None, None, :] < prefix[:, :, None, None]) & keep_row[:, :, None, None]
    hidden = low(jax.nn.silu(gate_pre) * lifted) * live_cols.astype(residual.dtype)
    branch_ffn = low(jnp.einsum('btcf,fcd->btd', hidden, w_down, precision=PRECISE))
    return middle + branch_ffn

def reference(tokens, seq_ids, granularity, w_qkv, w_out, gain_attn, gain_ffn, w_gate, w_up, w_down, out_cotangent):
    devices = N_BATCH * N_GRAN * N_FFN
    row_count = TOK_DEV
    seq_rows = seq_ids.reshape(devices, row_count)
    seq_groups = granularity.reshape(devices, SEQ_DEV)
    batch_of = jnp.arange(devices, dtype=jnp.int32) // (N_GRAN * N_FFN)
    routing = functools.partial(route_rows, batch_count=N_BATCH, group_count=N_GRAN, capacity=CAP_PAIR)
    group_id, keep_row, target, slot_index = jax.vmap(routing)(seq_rows, seq_groups, batch_of)
    per_step = 1
    while per_step * 2 * row_count <= 4096 and devices % (per_step * 2) == 0:
        per_step = per_step * 2
    step_count = devices // per_step
    parameters = tuple((p.astype(jnp.float32) for p in (w_qkv, w_out, gain_attn, gain_ffn, w_gate, w_up, w_down)))
    residual = tokens.astype(jnp.float32).reshape(step_count, per_step, row_count, D)
    cotangent = out_cotangent.astype(jnp.float32).reshape(step_count, per_step, row_count, D)
    seq_blocks = seq_rows.reshape(step_count, per_step, row_count)
    keep_blocks = keep_row.reshape(step_count, per_step, row_count)
    group_blocks = group_id.reshape(step_count, per_step, row_count)

    def advance(carried, inputs):
        residual_blk, cotangent_blk, seq_blk, keep_blk, group_blk = inputs

        def forward(weights, values_in):
            return layer(weights, values_in, seq_blk, keep_blk, group_blk)
        result, pull_back = jax.vjp(forward, parameters, residual_blk)
        weight_grads, residual_grad = pull_back(cotangent_blk)
        summed = jax.tree.map(jnp.add, carried, weight_grads)
        return (summed, (result.astype(jnp.bfloat16), residual_grad.astype(jnp.bfloat16)))
    initial = tuple((jnp.zeros_like(p) for p in parameters))
    gradients, (outputs, input_grad) = lax.scan(advance, initial, (residual, cotangent, seq_blocks, keep_blocks, group_blocks))
    return (outputs.reshape(TOKENS, D), input_grad.reshape(TOKENS, D), gradients[0], gradients[1], gradients[2], gradients[3], gradients[4], gradients[5], gradients[6])
```

```python
import math

import jax
import jax.numpy as jnp
from jax import lax
from jax.sharding import PartitionSpec as P

H = 12


EPSILON = 1e-06
NEG_FILL = -1e30
ROPE_BASE = 10000.0
BF = jnp.bfloat16
F32 = jnp.float32


def seq_positions(seq_rows):
    first_row = jnp.sum((seq_rows[None, :] < seq_rows[:, None]).astype(jnp.int32), axis=1)
    return jnp.arange(seq_rows.shape[0], dtype=jnp.int32) - first_row


def row_limits(seq_rows, seq_groups, kept_rows, half_units):
    labels = jnp.arange(seq_groups.shape[0], dtype=jnp.int32)
    member = (seq_rows[:, None] == labels[None, :]).astype(jnp.int32)
    group_id = jnp.sum(member * seq_groups[None, :], axis=1)
    index = jnp.arange(seq_rows.shape[0], dtype=jnp.int32)
    earlier = (group_id[None, :] == group_id[:, None]) & (index[None, :] < index[:, None])
    rank = jnp.sum(earlier.astype(jnp.int32), axis=1)
    return jnp.where(rank < kept_rows, jnp.right_shift(jnp.int32(half_units), 3 - group_id), 0)


def rotate_half(vectors, cosines, sines):
    half_size = vectors.shape[-1] // 2
    front_half = vectors[..., :half_size]
    back_part = vectors[..., half_size:]
    return jnp.concatenate(
        [front_half * cosines - back_part * sines, back_part * cosines + front_half * sines],
        axis=-1,
    )


def rotate_back(vectors, cosines, sines):
    return rotate_half(vectors, cosines, -sines)


def dot(left, right):
    return jnp.dot(left, right, preferred_element_type=F32)


def contract_rows(left, right):
    return lax.dot_general(left, right, (((0,), (0,)), ((), ())), preferred_element_type=F32)


def contract_cols(left, right):
    return lax.dot_general(left, right, (((1,), (1,)), ((), ())), preferred_element_type=F32)


def norm_back(grad_normed, unit_rows, inverse_rms, gain):
    scaled = grad_normed * gain
    return inverse_rms * (scaled - unit_rows * jnp.mean(scaled * unit_rows, axis=-1, keepdims=True))


def after(value, *others):
    return lax.optimization_barrier((value, *others))[0]


def local(
    tokens,
    seq_ids,
    granularity,
    w_qkv,
    w_out,
    gain_attn,
    gain_ffn,
    w_gate,
    w_up,
    w_down,
    out_cotangent,
):
    n = lax.axis_size("batch")
    g = lax.axis_size("gran")
    z = lax.axis_index("batch")
    p = lax.axis_index("gran")
    c = lax.axis_index("ffn")
    rows, width = tokens.shape
    head = width // H
    heads = H // g
    mine = heads * head
    depth = w_qkv.shape[0]
    units = w_gate.shape[2]
    capacity = max(2, (5 * rows + 4 * n * g - 1) // (4 * n * g))

    def hop(x, r):
        return lax.ppermute(x, "gran", [(i, i ^ r) for i in range(g)])

    def pair(x):
        return lax.ppermute(x, "batch", [(i, i ^ 1) for i in range(n)])

    def core(x):
        return lax.ppermute(x, "ffn", [(0, 1), (1, 0)])

    def ring(x, s):
        return lax.ppermute(x, "batch", [(i, (i + s) % n) for i in range(n)])

    def plane_gather(x):
        half = x.shape[0] // 2
        one, two = hop(x, 1), hop(x, 2)
        three = jnp.concatenate([hop(one[:half], 2), hop(two[half:], 1)], axis=0)
        return jnp.stack([x, one, two, three])

    def plane_reduce(parts):
        got = [parts[0]] + [hop(parts[r], r) for r in range(1, g)]
        return sum(v.astype(F32) for v in got)

    def ring_gather(part_for):
        own = part_for(0)
        out = jnp.zeros((n, *own.shape), own.dtype)
        out = lax.dynamic_update_index_in_dim(out, own, z, 0)
        got = []
        for s in range(1, n):
            got.append(ring(part_for(s % 2), s))
        for s in range(1, n):
            out = lax.dynamic_update_index_in_dim(out, got[s - 1], (z - s) % n, 0)
        return out

    positions = seq_positions(seq_ids)
    limits = row_limits(seq_ids, granularity, capacity * n, units)
    about = jnp.stack([seq_ids, positions, limits], axis=0).astype(F32)
    about = jnp.concatenate([about, jnp.zeros((5, rows), F32)], axis=0)
    about = jnp.concatenate([about, pair(about)], axis=0)
    about = jnp.stack([about] + [hop(about, r) for r in range(1, g)])
    block_ids = about[:, 0].astype(jnp.int32)
    block_positions = about[:, 1]
    block_limits = jnp.stack([about[:, 2], about[:, 10]], axis=1).reshape(2 * g * rows, 1)
    block_limits = block_limits.astype(jnp.int32)

    gains = ring_gather(lambda odd: jnp.stack([gain_attn, gain_ffn]))
    gain_first = gains[:, 0].reshape(width).astype(F32)
    gain_second = gains[:, 1].reshape(width).astype(F32)

    half_depth = depth // 2
    qkv_part = lax.dynamic_slice(
        w_qkv.reshape(depth, 3, g, mine), (c * half_depth, 0, p, 0), (half_depth, 3, 1, mine)
    ).reshape(half_depth, 3 * mine)
    qkv_half = ring_gather(lambda odd: qkv_part)
    qkv_other = core(qkv_half)
    qkv_first = jnp.where(c == 0, qkv_half, qkv_other)
    qkv_second = jnp.where(c == 0, qkv_other, qkv_half)
    my_qkv = jnp.concatenate([qkv_first, qkv_second], axis=1).reshape(width, 3 * mine)

    sub = depth // g
    half_sub = sub // 2
    out_part = lax.dynamic_slice(w_out, (p * sub + c * half_sub, 0), (half_sub, width))
    out_part = after(out_part, qkv_half)
    out_half = ring_gather(lambda odd: out_part).reshape(g, n // g, half_sub, width)

    def for_member(stacked, r):
        return lax.dynamic_index_in_dim(stacked, p ^ r, 0, keepdims=False)

    def by_member(pieces):
        out = jnp.zeros((g, *pieces[0].shape), pieces[0].dtype)
        for r in range(g):
            out = lax.dynamic_update_index_in_dim(out, pieces[r], p ^ r, 0)
        return out

    out_pieces = by_member(
        [for_member(out_half, 0)] + [hop(for_member(out_half, r), r) for r in range(1, g)]
    )
    out_other = core(out_pieces)
    out_first = jnp.where(c == 0, out_pieces, out_other)
    out_second = jnp.where(c == 0, out_other, out_pieces)
    my_out = (
        jnp.stack([out_first, out_second], axis=2)
        .transpose(1, 0, 2, 3, 4)
        .reshape(mine, width)
    )

    shares = 2 * g
    strip = units // n // shares
    share = p * 2 + z % 2

    def columns(w, odd):
        picked = lax.dynamic_index_in_dim(
            w.reshape(depth, n, shares, strip), share ^ odd, 2, keepdims=False
        )
        return picked.reshape(depth, n * strip)

    gate_parts = [columns(w_gate, odd) for odd in (0, 1)]
    up_parts = [columns(w_up, odd) for odd in (0, 1)]
    down_rows = w_down.reshape(shares, strip, width)
    down_parts = [
        lax.dynamic_index_in_dim(down_rows, share ^ odd, 0, keepdims=False) for odd in (0, 1)
    ]
    gate_parts = [after(v, out_half) for v in gate_parts]
    my_gate = ring_gather(lambda odd: gate_parts[odd]).reshape(width, n * strip)
    up_parts = [after(v, my_gate) for v in up_parts]
    my_up = ring_gather(lambda odd: up_parts[odd]).reshape(width, n * strip)
    down_parts = [after(v, my_up) for v in down_parts]
    my_down = ring_gather(lambda odd: down_parts[odd]).reshape(n * strip, width)
    gate_matrix = jnp.concatenate([my_gate, core(my_gate)], axis=1)
    up_matrix = jnp.concatenate([my_up, core(my_up)], axis=1)
    down_matrix = jnp.concatenate([my_down, core(my_down)], axis=0)
    span = n * strip
    index = jnp.arange(2 * span, dtype=jnp.int32) % span
    unit_index = (index // strip) * (strip * shares) + share * strip + index % strip

    residual = tokens.astype(F32)
    inverse_first = lax.rsqrt(jnp.mean(residual * residual, axis=-1, keepdims=True) + EPSILON)
    unit_first = residual * inverse_first
    normed = (unit_first * gain_first).astype(BF)
    all_normed = plane_gather(normed).reshape(g * rows, width)
    packed = dot(all_normed, my_qkv).reshape(g, rows, 3, heads, head)
    frequencies = ROPE_BASE ** (-(2.0 * jnp.arange(head // 2, dtype=F32)) / head)
    angles = block_positions[:, :, None] * frequencies
    cosines = jnp.cos(angles)[:, :, None, :]
    sines = jnp.sin(angles)[:, :, None, :]
    score_scale = 1.0 / math.sqrt(head)
    queries = (rotate_half(packed[:, :, 0], cosines, sines) * score_scale).astype(BF)
    keys_rot = rotate_half(packed[:, :, 1], cosines, sines).astype(BF)
    values = packed[:, :, 2].astype(BF)
    row_index = jnp.arange(rows, dtype=jnp.int32)
    allowed = (block_ids[:, :, None] == block_ids[:, None, :]) & (
        row_index[:, None] >= row_index[None, :]
    )
    scores = jnp.einsum("bqhe,bkhe->bhqk", queries, keys_rot, preferred_element_type=F32)
    scores = jnp.where(allowed[:, None], scores, NEG_FILL)
    top_score = jnp.max(scores, axis=-1, keepdims=True)
    exponent = jnp.exp(scores - top_score)
    probs = exponent / jnp.sum(exponent, axis=-1, keepdims=True)
    prob_weights = probs.astype(BF)
    attended = jnp.einsum("bhqk,bkhe->bqhe", prob_weights, values, preferred_element_type=F32)
    attended = attended.reshape(g * rows, mine).astype(BF)
    partial_attn = dot(attended, my_out).astype(BF).reshape(g, rows, width)
    middle = residual + plane_reduce(partial_attn)
    inverse_second = lax.rsqrt(jnp.mean(middle * middle, axis=-1, keepdims=True) + EPSILON)
    unit_second = middle * inverse_second
    normed_ffn = (unit_second * gain_second).astype(BF)

    def gather_rows(x):
        both = jnp.concatenate([x, pair(x)], axis=0)
        return plane_gather(both).reshape(2 * g * rows, width)

    def reduce_rows(x):
        both = plane_reduce(x.reshape(g, 2 * rows, width))
        return both[:rows] + pair(both[rows:].astype(BF)).astype(F32)

    group_grads = gather_rows(after(out_cotangent, all_normed))
    group_rows = gather_rows(normed_ffn)
    live = unit_index[None, :] < block_limits
    gate_pre = dot(group_rows, gate_matrix)
    lifted = dot(group_rows, up_matrix)
    sigmoid_gate = jax.nn.sigmoid(gate_pre)
    activated = gate_pre * sigmoid_gate
    hidden = jnp.where(live, (activated * lifted).astype(BF), jnp.zeros((), BF))
    grad_hidden = jnp.where(live, contract_cols(group_grads, down_matrix), 0.0)
    grad_gate = (
        grad_hidden * lifted * sigmoid_gate * (1.0 + gate_pre * (1.0 - sigmoid_gate))
    ).astype(BF)
    grad_lifted = (grad_hidden * activated).astype(BF)
    partial_input = (
        contract_cols(grad_gate, gate_matrix) + contract_cols(grad_lifted, up_matrix)
    ).astype(BF)
    grad_normed_ffn = reduce_rows(partial_input).astype(BF).astype(F32)

    def core_sum(left, right, split_left):
        if split_left:
            theirs = contract_rows(left[:, span:], right).astype(BF)
            return (contract_rows(left[:, :span], right) + core(theirs).astype(F32)).astype(BF)
        theirs = contract_rows(left, right[:, span:]).astype(BF)
        return (contract_rows(left, right[:, :span]) + core(theirs).astype(F32)).astype(BF)

    def ring_reduce(parts):
        even = lax.dynamic_index_in_dim(parts, z, 0, keepdims=False).astype(F32)
        odd = 0.0
        for s in range(1, n):
            got = ring(lax.dynamic_index_in_dim(parts, (z + s) % n, 0, keepdims=False), s)
            if s % 2:
                odd = odd + got.astype(F32)
            else:
                even = even + got.astype(F32)
        return even, odd

    def all_shares(parts):
        even, odd = ring_reduce(parts)
        flip = z % 2
        first = jnp.where(flip == 0, even, odd).astype(BF)
        second = jnp.where(flip == 0, odd, even).astype(BF)
        gathered = plane_gather(jnp.stack([first, second]))
        return by_member([gathered[r] for r in range(g)]).reshape(shares, *first.shape)

    def columns_back(pieces):
        return (
            pieces.reshape(shares, depth, n, strip)
            .transpose(1, 2, 0, 3)
            .reshape(depth, units)
            .astype(F32)
        )

    gate_sum = core_sum(group_rows, grad_gate, False).reshape(n, depth, span)
    up_sum = core_sum(group_rows, grad_lifted, False).reshape(n, depth, span)
    down_sum = core_sum(hidden, group_grads, True).reshape(n, strip, width)
    share_gate = columns_back(all_shares(gate_sum))
    share_up = columns_back(all_shares(up_sum))
    share_down = all_shares(down_sum).reshape(units // n, width).astype(F32)

    partial_ffn = dot(hidden, down_matrix).astype(BF)
    branch_ffn = reduce_rows(partial_ffn).astype(BF).astype(F32)
    outputs = (middle + branch_ffn).astype(BF)

    grad_middle = out_cotangent.astype(F32) + norm_back(
        grad_normed_ffn, unit_second, inverse_second, gain_second
    )
    grad_branch = plane_gather(grad_middle.astype(BF)).reshape(g * rows, width)
    out_grad = contract_rows(attended, grad_branch)
    grad_attended = contract_cols(grad_branch, my_out).astype(BF).reshape(g, rows, heads, head)
    grad_probs = jnp.einsum("bqhe,bkhe->bhqk", grad_attended, values, preferred_element_type=F32)
    grad_scores = (
        probs * (grad_probs - jnp.sum(probs * grad_probs, axis=-1, keepdims=True))
    ).astype(BF)
    grad_queries = jnp.einsum(
        "bhqk,bkhe->bqhe", grad_scores, keys_rot, preferred_element_type=F32
    ).astype(BF)
    grad_keys = jnp.einsum(
        "bhqk,bqhe->bkhe", grad_scores, queries, preferred_element_type=F32
    ).astype(BF)
    grad_values = jnp.einsum(
        "bhqk,bqhe->bkhe", prob_weights, grad_attended, preferred_element_type=F32
    ).astype(BF)
    grad_packed = (
        jnp.stack(
            [
                rotate_back(grad_queries.astype(F32) * score_scale, cosines, sines),
                rotate_back(grad_keys.astype(F32), cosines, sines),
                grad_values.astype(F32),
            ],
            axis=2,
        )
        .reshape(g * rows, 3 * mine)
        .astype(BF)
    )
    partial_normed = contract_cols(grad_packed, my_qkv).astype(BF).reshape(g, rows, width)
    grad_normed = plane_reduce(partial_normed)
    input_grad = (
        grad_middle + norm_back(grad_normed, unit_first, inverse_first, gain_first)
    ).astype(BF)

    def my_half(x, which):
        return lax.dynamic_index_in_dim(x, which, 1, keepdims=False)

    qkv_grad = contract_rows(all_normed, grad_packed).astype(BF).reshape(n, 2, half_depth, -1)
    qkv_sum = my_half(qkv_grad, c).astype(F32) + core(my_half(qkv_grad, 1 - c)).astype(F32)
    even, odd = ring_reduce(qkv_sum.astype(BF))
    qkv_all = plane_gather((even + odd).astype(BF))
    qkv_all = by_member([qkv_all[r] for r in range(g)])
    qkv_far = core(qkv_all)
    qkv_both = jnp.stack(
        [jnp.where(c == 0, qkv_all, qkv_far), jnp.where(c == 0, qkv_far, qkv_all)]
    )
    share_qkv = (
        qkv_both.reshape(2, g, half_depth, 3, mine)
        .transpose(0, 2, 3, 1, 4)
        .reshape(depth, 3 * width)
        .astype(F32)
    )

    out_grad = out_grad.astype(BF).reshape(n // g, g, 2, half_sub, width)
    out_mine = lax.dynamic_index_in_dim(out_grad, c, 2, keepdims=False)
    out_theirs = lax.dynamic_index_in_dim(out_grad, 1 - c, 2, keepdims=False)
    out_sum = (out_mine.astype(F32) + core(out_theirs).astype(F32)).astype(BF)

    def member_part(r):
        return lax.dynamic_index_in_dim(out_sum, p ^ r, 1, keepdims=False)

    out_sum = by_member([member_part(0)] + [hop(member_part(r), r) for r in range(1, g)])
    even, odd = ring_reduce(out_sum.reshape(n, half_sub, width))
    out_all = plane_gather((even + odd).astype(BF))
    out_all = by_member([out_all[r] for r in range(g)])
    out_far = core(out_all)
    share_out = (
        jnp.stack(
            [jnp.where(c == 0, out_all, out_far), jnp.where(c == 0, out_far, out_all)], axis=1
        )
        .reshape(depth, width)
        .astype(F32)
    )

    share_gain_attn = jnp.sum(share_qkv * w_qkv.astype(F32), axis=1) / gain_attn.astype(F32)
    ffn_part = jnp.sum(
        share_gate * w_gate[:, 0].astype(F32) + share_up * w_up[:, 0].astype(F32), axis=1
    )
    share_gain_ffn = (ffn_part + core(ffn_part)) / gain_ffn.astype(F32)
    return (
        outputs,
        input_grad,
        share_qkv,
        share_out,
        share_gain_attn,
        share_gain_ffn,
        share_gate[:, None, :],
        share_up[:, None, :],
        share_down[:, None, :],
    )


def solution(mesh):
    in_specs = (
        P(("batch", "gran", "ffn"), None),
        P(("batch", "gran", "ffn")),
        P(("batch", "gran", "ffn")),
        P("batch", None),
        P("batch", None),
        P("batch"),
        P("batch"),
        P("batch", "ffn", None),
        P("batch", "ffn", None),
        P("batch", "ffn", None),
        P(("batch", "gran", "ffn"), None),
    )
    out_specs = (
        P(("batch", "gran", "ffn"), None),
        P(("batch", "gran", "ffn"), None),
        P("batch", None),
        P("batch", None),
        P("batch"),
        P("batch"),
        P("batch", "ffn", None),
        P("batch", "ffn", None),
        P("batch", "ffn", None),
    )
    return jax.shard_map(local, mesh=mesh, in_specs=in_specs, out_specs=out_specs, check_vma=False)
```

```python
import functools
import math

import jax
import jax.numpy as jnp
from jax import lax
from jax.experimental import pallas as pl
from jax.experimental.pallas import tpu as pltpu
from jax.sharding import PartitionSpec as P

H = 12


EPSILON = 1e-06
NEG_FILL = -1e30
ROPE_BASE = 10000.0
BF = jnp.bfloat16
F32 = jnp.float32


def row_groups(seq_rows, seq_groups, kept_rows):
    labels = jnp.arange(seq_groups.shape[0], dtype=jnp.int32)
    member = (seq_rows[:, None] == labels[None, :]).astype(jnp.int32)
    group_id = jnp.sum(member * seq_groups[None, :], axis=1)
    index = jnp.arange(seq_rows.shape[0], dtype=jnp.int32)
    earlier = (group_id[None, :] == group_id[:, None]) & (index[None, :] < index[:, None])
    rank = jnp.sum(earlier.astype(jnp.int32), axis=1)
    return jnp.where(rank < kept_rows, group_id, -1)


def dot(left, right):
    return jnp.dot(left, right, preferred_element_type=F32)


def contract_rows(left, right):
    return lax.dot_general(left, right, (((0,), (0,)), ((), ())), preferred_element_type=F32)


def contract_cols(left, right):
    return lax.dot_general(left, right, (((1,), (1,)), ((), ())), preferred_element_type=F32)


def norm_back(grad_normed, unit_rows, inverse_rms, gain):
    scaled = grad_normed * gain
    return inverse_rms * (scaled - unit_rows * jnp.mean(scaled * unit_rows, axis=-1, keepdims=True))


def first_rows(values, count, width):
    return jnp.pad(values.astype(BF)[None, :], ((0, count - 1), (0, width - values.shape[0])))


def after(value, *others):
    return lax.optimization_barrier((value, *others))[0]


def small_cost():
    return pl.CostEstimate(flops=1, bytes_accessed=1, transcendentals=0)


VMEM_LIMIT = 56 * 1024 * 1024


def call(kernel, outs, scratch=(), ins=(), operands=()):
    kinds = {
        "v": pl.BlockSpec(memory_space=pltpu.VMEM),
        "h": pl.BlockSpec(memory_space=pl.ANY),
        "s": pl.BlockSpec(memory_space=pltpu.SMEM),
    }
    return pl.pallas_call(
        kernel,
        out_shape=[jax.ShapeDtypeStruct(shape, dtype) for shape, dtype in outs],
        in_specs=[kinds[k] for k in ins],
        out_specs=[kinds["v"]] * len(outs),
        scratch_shapes=list(scratch),
        compiler_params=pltpu.CompilerParams(vmem_limit_bytes=VMEM_LIMIT),
        cost_estimate=small_cost(),
    )(*operands)


def split_parts(value, rows, to_one, to_two, own, two_low, one_high):
    half = rows // 2
    to_one[:half] = value[rows : rows + half].astype(BF)
    to_one[half:] = value[3 * rows : 3 * rows + half].astype(BF)
    to_two[:half] = value[2 * rows + half : 3 * rows].astype(BF)
    to_two[half:] = value[3 * rows + half :].astype(BF)
    own[...] = value[:rows]
    two_low[...] = value[2 * rows : 2 * rows + half].astype(BF)
    one_high[...] = value[rows + half : 2 * rows].astype(BF)


def split_shapes(rows, width):
    half = rows // 2
    return [
        ((rows, width), BF),
        ((rows, width), BF),
        ((rows, width), F32),
        ((half, width), BF),
        ((half, width), BF),
    ]


def attend_kernel(n, rows, depth, mine, head, place, freq, *refs):
    tokens, refs = refs[:5], refs[5:]
    here, there, refs = refs[:n], refs[n : 2 * n], refs[2 * n :]
    normed, weight, queries, keys, values, attended, cosines, sines, bias, gains = refs[:10]
    gain_rows, unit_rows, sems = refs[10:]
    z, c = place[0], place[2]
    hd = depth // 2
    width = n * depth
    copies = []
    for s in range(n):
        plane = lax.rem(z - s + n, n)
        for which, pieces in ((c, here), (1 - c, there)):
            start = pl.multiple_of(plane * depth + which * hd, 8)
            for k in range(3):
                copies.append(
                    pltpu.make_async_copy(
                        pieces[s].at[pl.ds(k * hd, hd), :],
                        weight.at[pl.ds(start, hd), pl.ds(k * mine, mine)],
                        sems.at[len(copies)],
                    )
                )
        copies.append(
            pltpu.make_async_copy(
                here[s].at[pl.ds(here[s].shape[0] - 16, 16), :], gain_rows.at[plane], sems.at[len(copies)]
            )
        )
    for copy in copies:
        copy.start()

    half = rows // 2
    third = tokens[3].shape[0]
    spans = [(tokens[0], 0, 0, rows), (tokens[1], 0, rows, rows), (tokens[2], 0, 2 * rows, rows)]
    spans += [(tokens[3], 0, 3 * rows, third), (tokens[4], 0, 3 * rows + third, rows - third)]
    for ref, low, at, count in spans:
        x = ref[low : low + count, :].astype(F32)
        inverse = lax.rsqrt(jnp.mean(x * x, axis=-1, keepdims=True) + EPSILON)
        unit_rows[at : at + count] = x * inverse

    row = lax.broadcasted_iota(jnp.int32, (rows, rows), 0)
    col = lax.broadcasted_iota(jnp.int32, (rows, rows), 1)
    lane = lax.broadcasted_iota(jnp.int32, (rows, head), 1)
    sign = jnp.where(lane < head // 2, -1.0, 1.0)
    for b in range(4):
        ref, low = (tokens[b], rows) if b < 3 else (tokens[4], rows - third)
        ids = ref[low : low + 8, :rows].astype(F32)[:1]
        ids_row = jnp.broadcast_to(ids, (rows, rows))
        ids_col = jnp.sum(jnp.where(row == col, ids_row, 0.0), axis=1, keepdims=True)
        before = jnp.sum(jnp.where(ids_row < ids_col, 1.0, 0.0), axis=1, keepdims=True)
        positions = row[:, :1].astype(F32) - before
        angles = positions * freq[:1, :]
        cosines[b * rows : (b + 1) * rows] = jnp.cos(angles)
        sines[b * rows : (b + 1) * rows] = jnp.sin(angles) * sign
        bias[b * rows : (b + 1) * rows] = jnp.where(
            (ids_row == ids_col) & (row >= col), 0.0, NEG_FILL
        )

    for copy in copies:
        copy.wait()
    for k in range(n):
        block = slice(k * depth, (k + 1) * depth)
        both = gain_rows[k].astype(F32)
        gains[0:8, block] = jnp.broadcast_to(both[0:1, :depth], (8, depth))
        gains[8:16, block] = jnp.broadcast_to(both[8:9, :depth], (8, depth))
    normed[...] = (unit_rows[...] * gains[0:1, :]).astype(BF)
    x = normed[...]
    cos, sin = cosines[...], sines[...]
    scale = 1.0 / math.sqrt(head)
    for k, out in enumerate((queries, keys, values)):
        packed = dot(x, weight[:, k * mine : (k + 1) * mine])
        for h in range(mine // head):
            part = packed[:, h * head : (h + 1) * head]
            if k < 2:
                part = part * cos + pltpu.roll(part, head // 2, 1) * sin
            if k == 0:
                part = part * scale
            out[:, h * head : (h + 1) * head] = part.astype(BF)
    for b in range(4):
        for h in range(mine // head):
            here_rows, here_cols = slice(b * rows, (b + 1) * rows), slice(h * head, (h + 1) * head)
            scores = contract_cols(queries[here_rows, here_cols], keys[here_rows, here_cols])
            probs = softmax(scores + bias[here_rows])
            attended[here_rows, here_cols] = dot(
                probs.astype(BF), values[here_rows, here_cols]
            ).astype(BF)


def softmax(scores):
    exponent = jnp.exp(scores - jnp.max(scores, axis=-1, keepdims=True))
    return exponent / jnp.sum(exponent, axis=-1, keepdims=True)


def project_kernel(rows, attended, out, *parts):
    split_parts(dot(attended[...], out[...]), rows, *parts)


def attend_back_kernel(rows, mine, head, *refs):
    grads, refs = refs[:5], refs[5:]
    out, weight, queries, keys, values, cosines, sines, bias = refs[:8]
    branch, packed, *parts = refs[8:-1]
    attended_grad = refs[-1]
    third = grads[3].shape[0]
    at = 0
    for ref in grads:
        branch[at : at + ref.shape[0]] = ref[...]
        at += ref.shape[0]
    del third
    attended_grad[...] = contract_cols(branch[...], out[...]).astype(BF)
    scale = 1.0 / math.sqrt(head)
    for b in range(4):
        r = slice(b * rows, (b + 1) * rows)
        cos, sin = cosines[r], sines[r]
        for h in range(mine // head):
            cols = slice(h * head, (h + 1) * head)
            q, k, v, grad = queries[r, cols], keys[r, cols], values[r, cols], attended_grad[r, cols]
            probs = softmax(contract_cols(q, k) + bias[r])
            grad_probs = contract_cols(grad, v)
            grad_scores = probs * (
                grad_probs - jnp.sum(probs * grad_probs, axis=-1, keepdims=True)
            )
            grad_scores = grad_scores.astype(BF)
            grad_q = dot(grad_scores, k).astype(BF).astype(F32) * scale
            grad_k = contract_rows(grad_scores, q).astype(BF).astype(F32)
            grad_v = contract_rows(probs.astype(BF), grad)
            for j, part in enumerate((grad_q, grad_k, grad_v)):
                if j < 2:
                    part = part * cos - pltpu.roll(part, head // 2, 1) * sin
                packed[r, j * mine + h * head : j * mine + (h + 1) * head] = part.astype(BF)
    split_parts(contract_cols(packed[...], weight[...]), rows, *parts)


def first_part_kernel(depth, mine, members, place, w_qkv, w_out, gains, out, sems):
    p, c = place[1], place[2]
    hd, hs = depth // 2, depth // members // 2
    width = w_out.shape[1]
    moves = []
    for k in range(3):
        column = pl.multiple_of(k * width + p * mine, 128)
        moves.append((w_qkv.at[pl.ds(c * hd, hd), pl.ds(column, mine)], k * hd, hd))
    top = pl.multiple_of((p * 2 + c) * hs, 8)
    for k in range(width // mine):
        block = w_out.at[pl.ds(top, hs), pl.ds(k * mine, mine)]
        moves.append((block, 3 * hd + k * hs, hs))
    moves.append((gains, out.shape[0] - 16, 16))
    copies = [
        pltpu.make_async_copy(source, out.at[pl.ds(at, count), :], sems.at[i])
        for i, (source, at, count) in enumerate(moves)
    ]
    for copy in copies:
        copy.start()
    for copy in copies:
        copy.wait()


def out_weight_kernel(n, members, hs, mine, place, *refs):
    pieces, out, sems = refs[:members], refs[members], refs[members + 1]
    p = place[1]
    copies = []
    for r in range(members):
        for j in range(n // members):
            for half in range(2):
                top = pl.multiple_of(((j * members + (p ^ r)) * 2 + half) * hs, 8)
                for k in range(out.shape[1] // mine):
                    copies.append(
                        pltpu.make_async_copy(
                            pieces[r].at[j, half, pl.ds(k * hs, hs), :],
                            out.at[pl.ds(top, hs), pl.ds(k * mine, mine)],
                            sems.at[len(copies)],
                        )
                    )
    for copy in copies:
        copy.start()
    for copy in copies:
        copy.wait()


def unit_weights_kernel(n, depth, strip, place, *refs):
    here, there = refs[:n], refs[n : 2 * n]
    gate, up, down, sems = refs[2 * n :]
    z = place[0]
    span = n * strip
    copies = []

    def add(source, target):
        copies.append(pltpu.make_async_copy(source, target, sems.at[len(copies)]))

    for s in range(n):
        plane = lax.rem(z - s + n, n)
        top = pl.multiple_of(plane * depth, 8)
        for half, pieces in enumerate((here, there)):
            columns = pl.ds(half * span, span)
            add(pieces[s].at[pl.ds(0, depth), :], gate.at[pl.ds(top, depth), columns])
            add(pieces[s].at[pl.ds(depth, depth), :], up.at[pl.ds(top, depth), columns])
            start = pl.multiple_of(half * span + plane * strip, 8)
            for k in range(down.shape[1] // span):
                add(
                    pieces[s].at[pl.ds(2 * depth + k * strip, strip), :],
                    down.at[pl.ds(start, strip), pl.ds(k * span, span)],
                )
    for copy in copies:
        copy.start()
    for copy in copies:
        copy.wait()


def strips_of(tile, strip):
    at, out = 0, []
    while at < 128:
        share, first = divmod(tile * 128 + at, strip)
        count = min(strip - first, 128 - at)
        out.append((share, first, at, count))
        at += count
    return out


def unit_results_kernel(n, members, depth, strip, place, *refs):
    pieces, w_gate, w_up = refs[:5], refs[5], refs[6]
    gate, up, down, gain, held, sems = refs[7:]
    shares, span = 2 * members, n * strip
    cuts = (held.shape[1] - 2 * depth) // strip
    z, p = place[0], place[1]
    parts = [(0, depth), (depth, depth), (2 * depth, cuts * strip)]
    copies = []
    for low, count in parts:
        group = []
        for r in range(members):
            for odd in range(2):
                share = (p ^ r) * 2 + (lax.rem(z, 2) ^ odd)
                if r < 3:
                    ref, top = pieces[r], odd * held.shape[1] + low
                else:
                    ref, top = pieces[3 + odd], low
                group.append(
                    pltpu.make_async_copy(
                        ref.at[pl.ds(top, count), :],
                        held.at[share, pl.ds(low, count), :],
                        sems.at[len(copies), r * 2 + odd],
                    )
                )
        for copy in group:
            copy.start()
        copies.append(group)
    lanes = lax.broadcasted_iota(jnp.int32, (depth, 128), 1)
    row_tiles = n * shares * strip // 128
    total = jnp.zeros((depth, 128), F32)
    for which, (out, weight) in enumerate(((gate, w_gate), (up, w_up))):
        for copy in copies[which]:
            copy.wait()
        rows = slice(which * depth, (which + 1) * depth)
        for k in range(n):
            for tile in range(shares * strip // 128):
                made = jnp.zeros((depth, 128), F32)
                for share, first, lane, count in strips_of(tile, strip):
                    column = k * strip + first
                    while count > 0:
                        source, offset = divmod(column, 128)
                        some = min(count, 128 - offset)
                        value = held[share, rows, source * 128 : (source + 1) * 128].astype(F32)
                        if lane != offset:
                            value = pltpu.roll(value, (lane - offset) % 128, 1)
                        made = jnp.where((lanes >= lane) & (lanes < lane + some), value, made)
                        column, lane, count = column + some, lane + some, count - some
                at = k * (shares * strip // 128) + tile
                out[pl.ds(at, depth, stride=row_tiles), :] = made
                total += made * weight[:, at * 128 : (at + 1) * 128].astype(F32)
    gain[...] = jnp.sum(total, axis=1, keepdims=True)
    for copy in copies[2]:
        copy.wait()
    wide = cuts * span // 128
    for share in range(shares):
        for k in range(cuts):
            low = 2 * depth + k * strip
            for tile in range(span // 128):
                value = held[share, low : low + strip, tile * 128 : (tile + 1) * 128].astype(F32)
                start = share * strip * wide + k * (span // 128) + tile
                down[pl.ds(start, strip, stride=wide), :] = value


def attention_results_kernel(members, depth, mine, place, *refs):
    here, there, w_qkv = refs[:5], refs[5:10], refs[10]
    qkv, out, gain, held, held_out, sems = refs[11:]
    p, c = place[1], place[2]
    hd, hs = depth // 2, depth // members // 2
    width = held_out.shape[1]
    blocks = width // mine
    copies = []

    def add(source, target):
        copies.append(pltpu.make_async_copy(source, target, sems.at[len(copies)]))

    def place_rows(ref, first, low, count, r, half):
        for k in range(3):
            top, end = max(low, k * hd), min(low + count, (k + 1) * hd)
            if top < end:
                add(
                    ref.at[pl.ds(first + top - low, end - top), :],
                    held.at[
                        pl.ds(pl.multiple_of(half * hd + top - k * hd, 8), end - top),
                        pl.ds(pl.multiple_of(k * width + (p ^ r) * mine, 128), mine),
                    ],
                )
        for k in range(blocks):
            base = 3 * hd + k * hs
            top, end = max(low, base), min(low + count, base + hs)
            if top < end:
                add(
                    ref.at[pl.ds(first + top - low, end - top), :],
                    held_out.at[
                        pl.ds(pl.multiple_of(((p ^ r) * 2 + half) * hs + top - base, 8), end - top),
                        pl.ds(k * mine, mine),
                    ],
                )

    rows = 3 * hd + blocks * hs
    for half, pieces in ((c, here), (1 - c, there)):
        for r in range(3):
            place_rows(pieces[r], 0, 0, rows, r, half)
        third = pieces[3].shape[0]
        place_rows(pieces[3], 0, 0, third, 3, half)
        place_rows(pieces[4], 0, third, rows - third, 3, half)
    for copy in copies:
        copy.start()
    for copy in copies:
        copy.wait()
    total = jnp.zeros((depth, 128), F32)
    for tile in range(3 * width // 128):
        cols = slice(tile * 128, (tile + 1) * 128)
        value = held[:, cols].astype(F32)
        qkv[:, cols] = value
        total += value * w_qkv[:, cols].astype(F32)
    gain[...] = jnp.sum(total, axis=1, keepdims=True)
    out[...] = held_out[...].astype(F32)


def move(kernel, outs, copies, operands, ins):
    kinds = {"h": pl.BlockSpec(memory_space=pl.ANY), "s": pl.BlockSpec(memory_space=pltpu.SMEM)}
    return pl.pallas_call(
        kernel,
        out_shape=[jax.ShapeDtypeStruct(shape, BF) for shape in outs],
        in_specs=[kinds[k] for k in ins],
        out_specs=[pl.BlockSpec(memory_space=pltpu.VMEM)] * len(outs),
        scratch_shapes=[pltpu.SemaphoreType.DMA((copies,))],
        compiler_params=pltpu.CompilerParams(vmem_limit_bytes=VMEM_LIMIT),
        cost_estimate=small_cost(),
    )(*operands)


def local(
    tokens,
    seq_ids,
    granularity,
    w_qkv,
    w_out,
    gain_attn,
    gain_ffn,
    w_gate,
    w_up,
    w_down,
    out_cotangent,
):
    n = lax.axis_size("batch")
    g = lax.axis_size("gran")
    z = lax.axis_index("batch")
    p = lax.axis_index("gran")
    c = lax.axis_index("ffn")
    rows, width = tokens.shape
    head = width // H
    heads = H // g
    mine = heads * head
    depth = w_qkv.shape[0]
    units = w_gate.shape[2]
    capacity = max(2, (5 * rows + 4 * n * g - 1) // (4 * n * g))

    def hop(x, r):
        return lax.ppermute(x, "gran", [(i, i ^ r) for i in range(g)])

    def pair(x):
        return lax.ppermute(x, "batch", [(i, i ^ 1) for i in range(n)])

    def core(x):
        return lax.ppermute(x, "ffn", [(0, 1), (1, 0)])

    def ring(x, s):
        return lax.ppermute(x, "batch", [(i, (i + s) % n) for i in range(n)])

    def gather_first(x):
        return [x, hop(x, 1), hop(x, 2)]

    def gather_rest(pieces):
        half = pieces[0].shape[0] // 32 * 16 or pieces[0].shape[0] // 2
        return [*pieces, hop(pieces[1][:half], 2), hop(pieces[2][half:], 1)]

    def plane_gather(x):
        return gather_rest(gather_first(x))

    def as_members(pieces):
        return jnp.concatenate(pieces, axis=0).reshape(g, *pieces[0].shape)

    def split_rows(x):
        half = x.shape[1] // 2
        return (
            jnp.concatenate([x[1, :half], x[3, :half]], axis=0),
            jnp.concatenate([x[2, half:], x[3, half:]], axis=0),
            x[0],
            x[2, :half],
            x[1, half:],
        )

    def plane_reduce(to_one, to_two, own, two_low, one_high):
        return plane_reduce_rest(hop(to_one, 1), hop(to_two, 2), own, two_low, one_high)

    def plane_reduce_rest(got_one, got_two, own, two_low, one_high):
        half = two_low.shape[0]
        two_low = (two_low.astype(F32) + got_one[half:].astype(F32)).astype(BF)
        one_high = (one_high.astype(F32) + got_two[half:].astype(F32)).astype(BF)
        low, high = hop(two_low, 2), hop(one_high, 1)
        got = [
            jnp.concatenate([v, w], axis=0).astype(F32)
            for v, w in ((got_one[:half], got_two[:half]), (low, high))
        ]
        return own.astype(F32) + got[0] + got[1]

    def by_member(pieces):
        out = jnp.zeros((g, *pieces[0].shape), pieces[0].dtype)
        for r in range(g):
            out = lax.dynamic_update_index_in_dim(out, pieces[r], p ^ r, 0)
        return out

    def ordered(here, there, axis):
        return jnp.stack(
            [jnp.where(c == 0, here, there), jnp.where(c == 0, there, here)], axis=axis
        )

    def cut(*values):
        return lax.optimization_barrier(values)

    def together(body, *operands):
        made = jax.eval_shape(body, *operands)
        return lax.cond(
            seq_ids[0] >= 0,
            body,
            lambda *given: jax.tree.map(lambda v: jnp.zeros(v.shape, v.dtype), made),
            *operands,
        )

    place = jnp.stack([z, p, c]).astype(jnp.int32)
    hd, sub = depth // 2, depth // g
    hs, blocks = sub // 2, width // mine
    gain_part = jnp.concatenate(
        [first_rows(gain_attn, 8, mine), first_rows(gain_ffn, 8, mine)], axis=0
    )
    token_part = jnp.concatenate([tokens, first_rows(seq_ids, 16, width)], axis=0)
    codes = row_groups(seq_ids, granularity, capacity * n)
    grad_part = jnp.concatenate([out_cotangent, first_rows(codes, 16, width)], axis=0)
    if hs % 8 == 0:
        [first_part] = move(
            functools.partial(first_part_kernel, depth, mine, g),
            [(3 * hd + blocks * hs + 16, mine)],
            blocks + 4,
            (place, w_qkv, w_out, gain_part),
            "shhh",
        )
    else:
        out_part = lax.dynamic_slice(w_out, ((p * 2 + c) * hs, 0), (hs, width))
        first_part = jnp.concatenate(
            [
                lax.dynamic_slice(w_qkv, (c * hd, k * width + p * mine), (hd, mine))
                for k in range(3)
            ]
            + [out_part[:, k * mine : (k + 1) * mine] for k in range(blocks)]
            + [gain_part],
            axis=0,
        )
    first_pieces = [first_part] + [ring(first_part, s) for s in range(1, n)]
    token_pieces = plane_gather(token_part)
    grad_all = lax.all_gather(
        jnp.concatenate([grad_part, pair(grad_part)], axis=0), "gran", axis=0
    )

    shares = 2 * g
    strip = units // n // shares
    share = p * 2 + z % 2
    span = n * strip
    cuts = width // span

    def columns(w, odd):
        return lax.dynamic_index_in_dim(
            w.reshape(depth, n, shares, strip), share ^ odd, 2, keepdims=False
        ).reshape(depth, span)

    def second_part(odd):
        rows_down = lax.dynamic_index_in_dim(
            w_down.reshape(shares, strip, width), share ^ odd, 0, keepdims=False
        )
        return jnp.concatenate(
            [columns(w_gate, odd), columns(w_up, odd)]
            + [rows_down[:, k * span : (k + 1) * span] for k in range(cuts)],
            axis=0,
        )

    even_part, odd_part, *first_pieces = cut(second_part(0), second_part(1), *first_pieces)
    second_here = [even_part] + [
        ring(odd_part if k % 2 else even_part, k) for k in range(1, n)
    ]

    all_rows = g * rows

    def unit(values):
        inverse = lax.rsqrt(jnp.mean(values * values, axis=-1, keepdims=True) + EPSILON)
        return values * inverse, inverse

    def attention(token_pieces, first_pieces):
        first_far = [core(v) for v in first_pieces[:2]]
        first_far += [core(v) for v in cut(*first_pieces[2:], *first_far)[: n - 2]]
        frequencies = ROPE_BASE ** (-(2.0 * jnp.arange(head // 2, dtype=F32)) / head)
        frequencies = jnp.broadcast_to(jnp.concatenate([frequencies, frequencies]), (8, head))
        all_normed, my_qkv, queries, keys, values, attended, cosines, sines, bias, gains = call(
            functools.partial(attend_kernel, n, rows, depth, mine, head),
            [
                ((all_rows, width), BF),
                ((width, 3 * mine), BF),
                ((all_rows, mine), BF),
                ((all_rows, mine), BF),
                ((all_rows, mine), BF),
                ((all_rows, mine), BF),
                ((all_rows, head), F32),
                ((all_rows, head), F32),
                ((all_rows, rows), F32),
                ((16, width), F32),
            ],
            [
                pltpu.VMEM((n, 16, mine), BF),
                pltpu.VMEM((all_rows, width), F32),
                pltpu.SemaphoreType.DMA((7 * n,)),
            ],
            "sv" + "v" * 5 + "h" * (2 * n),
            (place, frequencies, *token_pieces, *first_pieces, *first_far),
        )

        low, high = 3 * hd, 3 * hd + blocks * hs
        out_here = jnp.stack([v[low:high] for v in first_pieces])
        out_there = jnp.stack([v[low:high] for v in first_far])

        def out_part_for(r):
            picked = [
                ordered(*(lax.dynamic_index_in_dim(v, s, 0, keepdims=False) for v in (out_here, out_there)), 0)
                for s in [(z - (p ^ r) * (n // g) - j) % n for j in range(n // g)]
            ]
            return jnp.stack(picked)

        out_pieces = [out_part_for(0)] + [hop(out_part_for(r), r) for r in (1, 2)]
        out_pieces.append(hop(after(out_part_for(3), *out_pieces), 3))
        if hs % 8 == 0:
            [my_out] = move(
                functools.partial(out_weight_kernel, n, g, hs, mine),
                [(mine, width)],
                n * 2 * blocks,
                (place, *out_pieces),
                "s" + "h" * g,
            )
        else:
            my_out = by_member(out_pieces).reshape(g, n // g, 2, blocks, hs, mine)
            my_out = my_out.transpose(1, 0, 2, 4, 3, 5).reshape(mine, width)
        attn_parts = call(
            functools.partial(project_kernel, rows),
            split_shapes(rows, width),
            (),
            "vv",
            (attended, my_out),
        )

        middle = tokens.astype(F32) + plane_reduce(*attn_parts)
        unit_second, inverse_second = unit(middle)
        normed_ffn = (unit_second * gains[8:9]).astype(BF)
        both_rows = plane_gather(jnp.concatenate([normed_ffn, pair(normed_ffn)], axis=0))
        group_rows = jnp.concatenate(both_rows, axis=0)
        kept = (all_normed, my_qkv, my_out, queries, keys, values, attended, cosines, sines, bias)
        return kept, gains, middle, unit_second, inverse_second, group_rows

    kept, gains, middle, unit_second, inverse_second, group_rows = together(
        attention, token_pieces, first_pieces
    )
    all_normed, my_qkv, my_out, queries, keys, values, attended, cosines, sines, bias = kept
    gain_first, gain_second = gains[0:1], gains[8:9]
    residual = tokens.astype(F32)
    group_rows, grad_all, *second_here = cut(group_rows, grad_all, *second_here)
    second_far = [core(v) for v in second_here]

    if strip % 8 == 0:
        gate_matrix, up_matrix, down_matrix = move(
            functools.partial(unit_weights_kernel, n, depth, strip),
            [(width, 2 * span), (width, 2 * span), (2 * span, width)],
            2 * n * (2 + cuts),
            (place, *second_here, *second_far),
            "s" + "h" * (2 * n),
        )
    else:
        stacks = []
        for pieces in (second_here, second_far):
            out = jnp.zeros((n, *pieces[0].shape), BF)
            for s in range(n):
                out = lax.dynamic_update_index_in_dim(out, pieces[s], (z - s) % n, 0)
            stacks.append(out)
        gate_matrix, up_matrix = (
            jnp.concatenate(
                [v[:, k * depth : (k + 1) * depth].reshape(width, span) for v in stacks], axis=1
            )
            for k in (0, 1)
        )
        down_matrix = jnp.concatenate(
            [v[:, 2 * depth :].reshape(n, cuts, strip, span).transpose(0, 2, 1, 3) for v in stacks],
            axis=0,
        ).reshape(2 * span, width)
    grad_got = jnp.stack(
        [lax.dynamic_index_in_dim(grad_all, p ^ r, 0, keepdims=False) for r in range(g)]
    ).reshape(g, 2, rows + 16, width)
    group_grads = grad_got[:, :, :rows].reshape(2 * g * rows, width)
    group_codes = grad_got[:, :, rows, :rows].reshape(2 * g * rows, 1).astype(jnp.int32)
    group_limits = jnp.where(
        group_codes < 0, 0, jnp.right_shift(jnp.int32(units), jnp.minimum(3 - group_codes, 3))
    )
    index = jnp.arange(2 * span, dtype=jnp.int32) % span
    unit_index = (index // strip) * (strip * shares) + share * strip + index % strip
    live = unit_index[None, :] < group_limits
    gate_pre = dot(group_rows, gate_matrix)
    lifted = dot(group_rows, up_matrix)
    sigmoid_gate = jax.nn.sigmoid(gate_pre)
    activated = gate_pre * sigmoid_gate
    hidden = jnp.where(live, (activated * lifted).astype(BF), jnp.zeros((), BF))
    grad_hidden = jnp.where(live, contract_cols(group_grads, down_matrix), 0.0)
    grad_gate = (
        grad_hidden * lifted * sigmoid_gate * (1.0 + gate_pre * (1.0 - sigmoid_gate))
    ).astype(BF)
    grad_lifted = (grad_hidden * activated).astype(BF)
    partial_input = (
        contract_cols(grad_gate, gate_matrix) + contract_cols(grad_lifted, up_matrix)
    ).astype(BF)
    input_parts = split_rows(partial_input.reshape(g, 2 * rows, width))

    def core_sum(left, right, split_left):
        if split_left:
            theirs = contract_rows(left[:, span:], right).astype(BF)
            return (contract_rows(left[:, :span], right) + core(theirs).astype(F32)).astype(BF)
        theirs = contract_rows(left, right[:, span:]).astype(BF)
        return (contract_rows(left, right[:, :span]) + core(theirs).astype(F32)).astype(BF)

    gate_sum = core_sum(group_rows, grad_gate, False).reshape(n, depth, span)
    up_sum = core_sum(group_rows, grad_lifted, False).reshape(n, depth, span)
    down_sum = core_sum(hidden, group_grads, True).reshape(n, strip, cuts, span)

    def unit_sums(k):
        own = lax.dynamic_index_in_dim(down_sum, k, 0, keepdims=False).transpose(1, 0, 2)
        return jnp.concatenate(
            [lax.dynamic_index_in_dim(v, k, 0, keepdims=False) for v in (gate_sum, up_sum)]
            + [own.reshape(cuts * strip, span)],
            axis=0,
        )

    to_one, to_two, *waiting = input_parts
    got_one, got_two = hop(to_one, 1), hop(to_two, 2)
    messages = [unit_sums((z + k) % n) for k in range(n)]
    got_one, got_two, *messages = cut(got_one, got_two, *messages)
    sums = [messages[0].astype(F32), 0.0]
    moved = [ring(messages[k], k) for k in range(1, n)]

    def attention_back(got_one, got_two, waiting):
        halves = plane_reduce_rest(got_one, got_two, *waiting)
        grad_normed_ffn = halves[:rows] + pair(halves[rows:].astype(BF)).astype(F32)
        grad_normed_ffn = grad_normed_ffn.astype(BF).astype(F32)
        grad_middle = out_cotangent.astype(F32) + norm_back(
            grad_normed_ffn, unit_second, inverse_second, gain_second
        )
        branch_pieces = plane_gather(grad_middle.astype(BF))
        return grad_middle, call(
            functools.partial(attend_back_kernel, rows, mine, head),
            [((all_rows, width), BF), ((all_rows, 3 * mine), BF), *split_shapes(rows, width)],
            [pltpu.VMEM((all_rows, mine), BF)],
            "v" * 13,
            (*branch_pieces, my_out, my_qkv, queries, keys, values, cosines, sines, bias),
        )

    grad_middle, (grad_branch, grad_packed, *normed_parts) = together(
        attention_back, got_one, got_two, waiting
    )
    grad_branch, grad_packed, *moved = cut(grad_branch, grad_packed, *moved)
    for k in range(1, n):
        sums[k % 2] += moved[k - 1].astype(F32)
    even_sum, odd_sum = (v.astype(BF) for v in sums)

    partial_ffn = dot(hidden, down_matrix).astype(BF).reshape(g, 2 * rows, width)
    partial_ffn = by_member([partial_ffn[r] for r in range(g)]).reshape(-1, width)
    branch_sum = lax.psum_scatter(
        after(partial_ffn, got_one), "gran", scatter_dimension=0, tiled=True
    )

    def my_half(x, which, axis):
        return lax.dynamic_index_in_dim(x, which, axis, keepdims=False)

    def for_member(stacked, r, axis):
        return lax.dynamic_index_in_dim(stacked, p ^ r, axis, keepdims=False)

    out_grad = contract_rows(attended, grad_branch).astype(BF).reshape(n // g, g, 2, hs, width)
    out_sum = my_half(out_grad, c, 2).astype(F32) + core(my_half(out_grad, 1 - c, 2)).astype(F32)
    out_sum = out_sum.astype(BF)
    out_sum = by_member(
        [for_member(out_sum, 0, 1)]
        + [hop(for_member(out_sum, r, 1), r) for r in range(1, g)]
    ).reshape(n, hs, blocks, mine)
    qkv_grad = contract_rows(all_normed, grad_packed).astype(BF).reshape(n, 2, hd, 3, mine)
    qkv_sum = my_half(qkv_grad, c, 1).astype(F32) + core(my_half(qkv_grad, 1 - c, 1)).astype(F32)
    last_part = jnp.concatenate(
        [
            qkv_sum.astype(BF).transpose(0, 2, 1, 3).reshape(n, 3 * hd, mine),
            out_sum.transpose(0, 2, 1, 3).reshape(n, blocks * hs, mine),
        ],
        axis=1,
    )
    last_parts = [
        lax.dynamic_index_in_dim(last_part, (z + k) % n, 0, keepdims=False) for k in range(n)
    ]
    normed_parts, branch_sum, even_sum, odd_sum, *last_parts = cut(
        normed_parts, branch_sum, even_sum, odd_sum, *last_parts
    )
    last_moved = [ring(last_parts[k], k) for k in range(1, n)]

    def results(normed_parts, branch_sum, even_sum, odd_sum):
        grad_normed = plane_reduce(*normed_parts)
        unit_first, inverse_first = unit(residual)
        input_grad = (
            grad_middle + norm_back(grad_normed, unit_first, inverse_first, gain_first)
        ).astype(BF)
        branch_far = pair(after(branch_sum[rows:], grad_normed))
        branch_ffn = branch_sum[:rows].astype(F32) + branch_far.astype(F32)
        outputs = (middle + branch_ffn).astype(BF)
        unit_pieces = plane_gather(
            after(jnp.concatenate([even_sum, odd_sum], axis=0), branch_far)
        )
        if strip % 32 == 0:
            share_gate, share_up, share_down, ffn_part = call(
                functools.partial(unit_results_kernel, n, g, depth, strip),
                [
                    ((depth * units // 128, 128), F32),
                    ((depth * units // 128, 128), F32),
                    ((units // n * width // 128, 128), F32),
                    ((depth, 1), F32),
                ],
                [
                    pltpu.VMEM((shares, 2 * depth + cuts * strip, span), BF),
                    pltpu.SemaphoreType.DMA((3, shares)),
                ],
                "s" + "h" * 5 + "vv",
                (place, *unit_pieces, w_gate[:, 0], w_up[:, 0]),
            )
            ffn_part = ffn_part[:, 0]
        else:
            got = as_members(unit_pieces).reshape(g, 2, -1, span)
            all_units = jnp.zeros((shares, *got.shape[2:]), BF)
            for r in range(g):
                for odd in (0, 1):
                    all_units = lax.dynamic_update_index_in_dim(
                        all_units, got[r, odd], (p ^ r) * 2 + (z % 2) ^ odd, 0
                    )

            def columns_back(pieces):
                return (
                    pieces.reshape(shares, depth, n, strip)
                    .transpose(1, 2, 0, 3)
                    .reshape(depth, units)
                    .astype(F32)
                )

            share_gate = columns_back(all_units[:, :depth])
            share_up = columns_back(all_units[:, depth : 2 * depth])
            share_down = (
                all_units[:, 2 * depth :]
                .reshape(shares, cuts, strip, span)
                .transpose(0, 2, 1, 3)
                .reshape(units // n, width)
                .astype(F32)
            )
            ffn_part = jnp.sum(
                share_gate * w_gate[:, 0].astype(F32) + share_up * w_up[:, 0].astype(F32), axis=1
            )
        share_gain_ffn = (ffn_part + core(ffn_part)) / gain_ffn.astype(F32)
        return (
            outputs,
            input_grad,
            share_gain_ffn,
            share_gate.reshape(depth, 1, units),
            share_up.reshape(depth, 1, units),
            share_down.reshape(units // n, 1, width),
        )

    outputs, input_grad, share_gain_ffn, share_gate, share_up, share_down = together(
        results, normed_parts, branch_sum, even_sum, odd_sum
    )
    outputs, *last_moved = cut(outputs, *last_moved)
    last_sum = last_parts[0].astype(F32) + sum(v.astype(F32) for v in last_moved)
    last_pieces = plane_gather(last_sum.astype(BF))
    if hs % 16 == 0:
        share_qkv, share_out, attn_part = call(
            functools.partial(attention_results_kernel, g, depth, mine),
            [((depth, 3 * width), F32), ((depth, width), F32), ((depth, 1), F32)],
            [
                pltpu.VMEM((depth, 3 * width), BF),
                pltpu.VMEM((depth, width), BF),
                pltpu.SemaphoreType.DMA((2 * (g + 1) * (3 + blocks),)),
            ],
            "s" + "h" * 10 + "v",
            (place, *last_pieces, *(core(v) for v in last_pieces), w_qkv),
        )
        attn_part = attn_part[:, 0]
    else:
        last_got = as_members(last_pieces)
        last_got = by_member([last_got[r] for r in range(g)])
        last_both = ordered(last_got, core(last_got), 0)
        share_qkv = (
            last_both[:, :, : 3 * hd]
            .reshape(2, g, 3, hd, mine)
            .transpose(0, 3, 2, 1, 4)
            .reshape(depth, 3 * width)
            .astype(F32)
        )
        share_out = (
            last_both[:, :, 3 * hd :]
            .reshape(2, g, blocks, hs, mine)
            .transpose(1, 0, 3, 2, 4)
            .reshape(depth, width)
            .astype(F32)
        )
        attn_part = jnp.sum(share_qkv * w_qkv.astype(F32), axis=1)
    share_gain_attn = attn_part / gain_attn.astype(F32)
    return (
        outputs,
        input_grad,
        share_qkv,
        share_out,
        share_gain_attn,
        share_gain_ffn,
        share_gate,
        share_up,
        share_down,
    )


def solution(mesh):
    in_specs = (
        P(("batch", "gran", "ffn"), None),
        P(("batch", "gran", "ffn")),
        P(("batch", "gran", "ffn")),
        P("batch", None),
        P("batch", None),
        P("batch"),
        P("batch"),
        P("batch", "ffn", None),
        P("batch", "ffn", None),
        P("batch", "ffn", None),
        P(("batch", "gran", "ffn"), None),
    )
    out_specs = (
        P(("batch", "gran", "ffn"), None),
        P(("batch", "gran", "ffn"), None),
        P("batch", None),
        P("batch", None),
        P("batch"),
        P("batch"),
        P("batch", "ffn", None),
        P("batch", "ffn", None),
        P("batch", "ffn", None),
    )
    return jax.shard_map(local, mesh=mesh, in_specs=in_specs, out_specs=out_specs, check_vma=False)
```

```python
import functools
import math

import jax
import jax.numpy as jnp
from jax import lax
from jax.experimental import pallas as pl
from jax.experimental.pallas import tpu as pltpu
from jax.sharding import PartitionSpec as P

H = 12


EPSILON = 1e-06
NEG_FILL = -1e30
ROPE_BASE = 10000.0
BF = jnp.bfloat16
F32 = jnp.float32


def row_groups(seq_rows, seq_groups, kept_rows):
    labels = jnp.arange(seq_groups.shape[0], dtype=jnp.int32)
    member = (seq_rows[:, None] == labels[None, :]).astype(jnp.int32)
    group_id = jnp.sum(member * seq_groups[None, :], axis=1)
    index = jnp.arange(seq_rows.shape[0], dtype=jnp.int32)
    earlier = (group_id[None, :] == group_id[:, None]) & (index[None, :] < index[:, None])
    rank = jnp.sum(earlier.astype(jnp.int32), axis=1)
    return jnp.where(rank < kept_rows, group_id, -1)


def dot(left, right):
    return jnp.dot(left, right, preferred_element_type=F32)


def contract_rows(left, right):
    return lax.dot_general(left, right, (((0,), (0,)), ((), ())), preferred_element_type=F32)


def contract_cols(left, right):
    return lax.dot_general(left, right, (((1,), (1,)), ((), ())), preferred_element_type=F32)


def norm_back(grad_normed, unit_rows, inverse_rms, gain):
    scaled = grad_normed * gain
    return inverse_rms * (scaled - unit_rows * jnp.mean(scaled * unit_rows, axis=-1, keepdims=True))


def first_rows(values, count, width):
    return jnp.pad(values.astype(BF)[None, :], ((0, count - 1), (0, width - values.shape[0])))


def after(value, *others):
    return lax.optimization_barrier((value, *others))[0]


def small_cost():
    return pl.CostEstimate(flops=1, bytes_accessed=1, transcendentals=0)


def call(kernel, outs, scratch=(), ins=(), operands=(), out="v", spare=8):
    held = [v for k, v in zip(ins, operands) if k == "v"]
    held += [jax.ShapeDtypeStruct(*v) for v in outs if out == "v"]
    held += [v for v in scratch if v.dtype in (BF, F32)]
    limit = sum(math.prod(v.shape) * v.dtype.itemsize for v in held) + spare * 2**20
    kinds = {
        "v": pl.BlockSpec(memory_space=pltpu.VMEM),
        "h": pl.BlockSpec(memory_space=pl.ANY),
        "s": pl.BlockSpec(memory_space=pltpu.SMEM),
    }
    return pl.pallas_call(
        kernel,
        out_shape=[jax.ShapeDtypeStruct(shape, dtype) for shape, dtype in outs],
        in_specs=[kinds[k] for k in ins],
        out_specs=[kinds[out]] * len(outs),
        scratch_shapes=list(scratch),
        compiler_params=pltpu.CompilerParams(vmem_limit_bytes=limit),
        cost_estimate=small_cost(),
    )(*operands)


def split_parts(value, rows, to_one, to_two, own, two_low, one_high):
    half = rows // 2
    to_one[:half] = value[rows : rows + half].astype(BF)
    to_one[half:] = value[3 * rows : 3 * rows + half].astype(BF)
    to_two[:half] = value[2 * rows + half : 3 * rows].astype(BF)
    to_two[half:] = value[3 * rows + half :].astype(BF)
    own[...] = value[:rows]
    two_low[...] = value[2 * rows : 2 * rows + half].astype(BF)
    one_high[...] = value[rows + half : 2 * rows].astype(BF)


def split_shapes(rows, width):
    half = rows // 2
    return [
        ((rows, width), BF),
        ((rows, width), BF),
        ((rows, width), F32),
        ((half, width), BF),
        ((half, width), BF),
    ]


def attend_kernel(n, rows, depth, mine, head, place, freq, *refs):
    tokens, refs = refs[:5], refs[5:]
    here, there, refs = refs[:n], refs[n : 2 * n], refs[2 * n :]
    normed, weight, queries, keys, values, attended, cosines, sines, bias, gains = refs[:10]
    gain_rows, unit_rows, sems = refs[10:]
    z, c = place[0], place[2]
    hd = depth // 2
    width = n * depth
    copies = []
    for s in range(n):
        plane = lax.rem(z - s + n, n)
        for which, pieces in ((c, here), (1 - c, there)):
            start = pl.multiple_of(plane * depth + which * hd, 8)
            for k in range(3):
                copies.append(
                    pltpu.make_async_copy(
                        pieces[s].at[pl.ds(k * hd, hd), :],
                        weight.at[pl.ds(start, hd), pl.ds(k * mine, mine)],
                        sems.at[len(copies)],
                    )
                )
        copies.append(
            pltpu.make_async_copy(
                here[s].at[pl.ds(here[s].shape[0] - 16, 16), :], gain_rows.at[plane], sems.at[len(copies)]
            )
        )
    for copy in copies:
        copy.start()

    half = rows // 2
    third = tokens[3].shape[0]
    spans = [(tokens[0], 0, 0, rows), (tokens[1], 0, rows, rows), (tokens[2], 0, 2 * rows, rows)]
    spans += [(tokens[3], 0, 3 * rows, third), (tokens[4], 0, 3 * rows + third, rows - third)]
    for ref, low, at, count in spans:
        x = ref[low : low + count, :].astype(F32)
        inverse = lax.rsqrt(jnp.mean(x * x, axis=-1, keepdims=True) + EPSILON)
        unit_rows[at : at + count] = x * inverse

    row = lax.broadcasted_iota(jnp.int32, (rows, rows), 0)
    col = lax.broadcasted_iota(jnp.int32, (rows, rows), 1)
    lane = lax.broadcasted_iota(jnp.int32, (rows, head), 1)
    sign = jnp.where(lane < head // 2, -1.0, 1.0)
    for b in range(4):
        ref, low = (tokens[b], rows) if b < 3 else (tokens[4], rows - third)
        ids = ref[low : low + 8, :rows].astype(F32)[:1]
        ids_row = jnp.broadcast_to(ids, (rows, rows))
        ids_col = jnp.sum(jnp.where(row == col, ids_row, 0.0), axis=1, keepdims=True)
        before = jnp.sum(jnp.where(ids_row < ids_col, 1.0, 0.0), axis=1, keepdims=True)
        positions = row[:, :1].astype(F32) - before
        angles = positions * freq[:1, :]
        cosines[b * rows : (b + 1) * rows] = jnp.cos(angles)
        sines[b * rows : (b + 1) * rows] = jnp.sin(angles) * sign
        bias[b * rows : (b + 1) * rows] = jnp.where(
            (ids_row == ids_col) & (row >= col), 0.0, NEG_FILL
        )

    for copy in copies:
        copy.wait()
    for k in range(n):
        block = slice(k * depth, (k + 1) * depth)
        both = gain_rows[k].astype(F32)
        gains[0:8, block] = jnp.broadcast_to(both[0:1, :depth], (8, depth))
        gains[8:16, block] = jnp.broadcast_to(both[8:9, :depth], (8, depth))
    normed[...] = (unit_rows[...] * gains[0:1, :]).astype(BF)
    x = normed[...]
    cos, sin = cosines[...], sines[...]
    scale = 1.0 / math.sqrt(head)
    for k, out in enumerate((queries, keys, values)):
        packed = dot(x, weight[:, k * mine : (k + 1) * mine])
        for h in range(mine // head):
            part = packed[:, h * head : (h + 1) * head]
            if k < 2:
                part = part * cos + pltpu.roll(part, head // 2, 1) * sin
            if k == 0:
                part = part * scale
            out[:, h * head : (h + 1) * head] = part.astype(BF)
    for b in range(4):
        for h in range(mine // head):
            here_rows, here_cols = slice(b * rows, (b + 1) * rows), slice(h * head, (h + 1) * head)
            scores = contract_cols(queries[here_rows, here_cols], keys[here_rows, here_cols])
            probs = softmax(scores + bias[here_rows])
            attended[here_rows, here_cols] = dot(
                probs.astype(BF), values[here_rows, here_cols]
            ).astype(BF)


def softmax(scores):
    exponent = jnp.exp(scores - jnp.max(scores, axis=-1, keepdims=True))
    return exponent / jnp.sum(exponent, axis=-1, keepdims=True)


def project_kernel(rows, attended, out, *parts):
    split_parts(dot(attended[...], out[...]), rows, *parts)


def attend_back_kernel(rows, mine, head, *refs):
    grads, refs = refs[:5], refs[5:]
    out, weight, queries, keys, values, cosines, sines, bias = refs[:8]
    branch, packed, *parts = refs[8:-1]
    attended_grad = refs[-1]
    third = grads[3].shape[0]
    at = 0
    for ref in grads:
        branch[at : at + ref.shape[0]] = ref[...]
        at += ref.shape[0]
    del third
    attended_grad[...] = contract_cols(branch[...], out[...]).astype(BF)
    scale = 1.0 / math.sqrt(head)
    for b in range(4):
        r = slice(b * rows, (b + 1) * rows)
        cos, sin = cosines[r], sines[r]
        for h in range(mine // head):
            cols = slice(h * head, (h + 1) * head)
            q, k, v, grad = queries[r, cols], keys[r, cols], values[r, cols], attended_grad[r, cols]
            probs = softmax(contract_cols(q, k) + bias[r])
            grad_probs = contract_cols(grad, v)
            grad_scores = probs * (
                grad_probs - jnp.sum(probs * grad_probs, axis=-1, keepdims=True)
            )
            grad_scores = grad_scores.astype(BF)
            grad_q = dot(grad_scores, k).astype(BF).astype(F32) * scale
            grad_k = contract_rows(grad_scores, q).astype(BF).astype(F32)
            grad_v = contract_rows(probs.astype(BF), grad)
            for j, part in enumerate((grad_q, grad_k, grad_v)):
                if j < 2:
                    part = part * cos - pltpu.roll(part, head // 2, 1) * sin
                packed[r, j * mine + h * head : j * mine + (h + 1) * head] = part.astype(BF)
    split_parts(contract_cols(packed[...], weight[...]), rows, *parts)


def first_part_kernel(depth, mine, members, place, w_qkv, w_out, gains, out, sems):
    p, c = place[1], place[2]
    hd, hs = depth // 2, depth // members // 2
    width = w_out.shape[1]
    moves = []
    for k in range(3):
        column = pl.multiple_of(k * width + p * mine, 128)
        moves.append((w_qkv.at[pl.ds(c * hd, hd), pl.ds(column, mine)], k * hd, hd))
    top = pl.multiple_of((p * 2 + c) * hs, 8)
    for k in range(width // mine):
        block = w_out.at[pl.ds(top, hs), pl.ds(k * mine, mine)]
        moves.append((block, 3 * hd + k * hs, hs))
    moves.append((gains, out.shape[0] - 16, 16))
    copies = [
        pltpu.make_async_copy(source, out.at[pl.ds(at, count), :], sems.at[i])
        for i, (source, at, count) in enumerate(moves)
    ]
    for copy in copies:
        copy.start()
    for copy in copies:
        copy.wait()


def out_weight_kernel(n, members, hs, mine, place, *refs):
    pieces, out, sems = refs[:members], refs[members], refs[members + 1]
    p = place[1]
    copies = []
    for r in range(members):
        for j in range(n // members):
            for half in range(2):
                top = pl.multiple_of(((j * members + (p ^ r)) * 2 + half) * hs, 8)
                for k in range(out.shape[1] // mine):
                    copies.append(
                        pltpu.make_async_copy(
                            pieces[r].at[j, half, pl.ds(k * hs, hs), :],
                            out.at[pl.ds(top, hs), pl.ds(k * mine, mine)],
                            sems.at[len(copies)],
                        )
                    )
    for copy in copies:
        copy.start()
    for copy in copies:
        copy.wait()


def strips_of(tile, strip):
    at, out = 0, []
    while at < 128:
        share, first = divmod(tile * 128 + at, strip)
        count = min(strip - first, 128 - at)
        out.append((share, first, at, count))
        at += count
    return out


def unit_results_kernel(n, members, depth, strip, place, *refs):
    pieces, w_gate, w_up = refs[:5], refs[5], refs[6]
    gate, up, down, gain, held, sems = refs[7:]
    shares, span = 2 * members, n * strip
    cuts = (held.shape[1] - 2 * depth) // strip
    z, p = place[0], place[1]
    parts = [(0, depth), (depth, depth), (2 * depth, cuts * strip)]
    copies = []
    for low, count in parts:
        group = []
        for r in range(members):
            for odd in range(2):
                share = (p ^ r) * 2 + (lax.rem(z, 2) ^ odd)
                if r < 3:
                    ref, top = pieces[r], odd * held.shape[1] + low
                else:
                    ref, top = pieces[3 + odd], low
                group.append(
                    pltpu.make_async_copy(
                        ref.at[pl.ds(top, count), :],
                        held.at[share, pl.ds(low, count), :],
                        sems.at[len(copies), r * 2 + odd],
                    )
                )
        for copy in group:
            copy.start()
        copies.append(group)
    lanes = lax.broadcasted_iota(jnp.int32, (depth, 128), 1)
    row_tiles = n * shares * strip // 128
    total = jnp.zeros((depth, 128), F32)
    for which, (out, weight) in enumerate(((gate, w_gate), (up, w_up))):
        for copy in copies[which]:
            copy.wait()
        rows = slice(which * depth, (which + 1) * depth)
        for k in range(n):
            for tile in range(shares * strip // 128):
                made = jnp.zeros((depth, 128), F32)
                for share, first, lane, count in strips_of(tile, strip):
                    column = k * strip + first
                    while count > 0:
                        source, offset = divmod(column, 128)
                        some = min(count, 128 - offset)
                        value = held[share, rows, source * 128 : (source + 1) * 128].astype(F32)
                        if lane != offset:
                            value = pltpu.roll(value, (lane - offset) % 128, 1)
                        made = jnp.where((lanes >= lane) & (lanes < lane + some), value, made)
                        column, lane, count = column + some, lane + some, count - some
                at = k * (shares * strip // 128) + tile
                out[pl.ds(at, depth, stride=row_tiles), :] = made
                total += made * weight[:, at * 128 : (at + 1) * 128].astype(F32)
    gain[...] = jnp.sum(total, axis=1, keepdims=True)
    for copy in copies[2]:
        copy.wait()
    wide = cuts * span // 128
    for share in range(shares):
        for k in range(cuts):
            low = 2 * depth + k * strip
            for tile in range(span // 128):
                value = held[share, low : low + strip, tile * 128 : (tile + 1) * 128].astype(F32)
                start = share * strip * wide + k * (span // 128) + tile
                down[pl.ds(start, strip, stride=wide), :] = value


def attention_results_kernel(members, depth, mine, place, *refs):
    here, there, w_qkv = refs[:5], refs[5:10], refs[10]
    qkv, out, gain, held, held_out, sems = refs[11:]
    p, c = place[1], place[2]
    hd, hs = depth // 2, depth // members // 2
    width = held_out.shape[1]
    blocks = width // mine
    copies = []

    def add(source, target):
        copies.append(pltpu.make_async_copy(source, target, sems.at[len(copies)]))

    def place_rows(ref, first, low, count, r, half):
        for k in range(3):
            top, end = max(low, k * hd), min(low + count, (k + 1) * hd)
            if top < end:
                add(
                    ref.at[pl.ds(first + top - low, end - top), :],
                    held.at[
                        pl.ds(pl.multiple_of(half * hd + top - k * hd, 8), end - top),
                        pl.ds(pl.multiple_of(k * width + (p ^ r) * mine, 128), mine),
                    ],
                )
        for k in range(blocks):
            base = 3 * hd + k * hs
            top, end = max(low, base), min(low + count, base + hs)
            if top < end:
                add(
                    ref.at[pl.ds(first + top - low, end - top), :],
                    held_out.at[
                        pl.ds(pl.multiple_of(((p ^ r) * 2 + half) * hs + top - base, 8), end - top),
                        pl.ds(k * mine, mine),
                    ],
                )

    rows = 3 * hd + blocks * hs
    for half, pieces in ((c, here), (1 - c, there)):
        for r in range(3):
            place_rows(pieces[r], 0, 0, rows, r, half)
        third = pieces[3].shape[0]
        place_rows(pieces[3], 0, 0, third, 3, half)
        place_rows(pieces[4], 0, third, rows - third, 3, half)
    for copy in copies:
        copy.start()
    for copy in copies:
        copy.wait()
    total = jnp.zeros((depth, 128), F32)
    for tile in range(3 * width // 128):
        cols = slice(tile * 128, (tile + 1) * 128)
        value = held[:, cols].astype(F32)
        qkv[:, cols] = value
        total += value * w_qkv[:, cols].astype(F32)
    gain[...] = jnp.sum(total, axis=1, keepdims=True)
    out[...] = held_out[...].astype(F32)


def out_sums_kernel(members, hs, mine, place, attended, branch, mine_out, theirs_out, held):
    c = place[2]
    for k in range(branch.shape[1] // mine):
        cols = slice(k * mine, (k + 1) * mine)
        held[...] = contract_rows(attended[...], branch[:, cols])
        for out, half in ((mine_out, c), (theirs_out, 1 - c)):
            for quarter in range(members):
                start = pl.multiple_of((quarter * 2 + half) * hs, 8)
                value = held[pl.ds(start, hs), :]
                out[quarter, k * hs : (k + 1) * hs, :] = value.astype(BF)


def weight_sums_kernel(members, depth, mine, place, normed, packed, mine_out, theirs_out, held):
    c = place[2]
    hd = depth // 2
    for plane in range(members):
        block = slice(plane * depth, (plane + 1) * depth)
        held[...] = contract_rows(normed[:, block], packed[...])
        for out, half in ((mine_out, c), (theirs_out, 1 - c)):
            start = pl.multiple_of(half * hd, 8)
            for k in range(3):
                value = held[pl.ds(start, hd), k * mine : (k + 1) * mine]
                out[plane, k * hd : (k + 1) * hd, :] = value.astype(BF)


def last_parts_kernel(members, low, place, *refs):
    sums, quarters, outs, held = refs[0], refs[1 : members + 1], refs[members + 1 : -1], refs[-1]
    z, p = place[0], place[1]
    for r in range(members):
        held[r] = quarters[r][...]
    for k in range(members):
        plane = lax.rem(z + k, members)
        outs[k][:low] = sums[plane]
        outs[k][low:] = held[p ^ plane]


def feed_forward_kernel(n, members, depth, strip, rows, place, unit_index, *refs):
    pieces, grad_all, refs = refs[:5], refs[5], refs[6:]
    here, there, refs = refs[:n], refs[n : 2 * n], refs[2 * n :]
    outs, scratch = refs[:15], refs[15:]
    x, cot, hidden, grad_gate, grad_lifted, *splits = scratch[:15]
    gate, up, down, codes, in_sems, out_sems = scratch[15:]
    z, p = place[0], place[1]
    span = n * strip
    units = span * 2 * members
    size = 2 * rows
    started, finishing = [], []

    def fetch(source, target):
        copy = pltpu.make_async_copy(source, target, in_sems.at[len(started)])
        copy.start()
        started.append(copy)

    def flush(index, low, count):
        copy = pltpu.make_async_copy(
            scratch[index].at[pl.ds(low, count), :],
            outs[index].at[pl.ds(low, count), :],
            out_sems.at[len(finishing)],
        )
        copy.start()
        finishing.append(copy)

    at = 0
    for ref in pieces:
        fetch(ref, x.at[pl.ds(at, ref.shape[0]), :])
        at += ref.shape[0]
    for s in range(n):
        plane = lax.rem(z - s + n, n)
        top = pl.multiple_of(plane * depth, 8)
        for half, parts in enumerate((here, there)):
            columns = pl.ds(half * span, span)
            fetch(parts[s].at[pl.ds(0, depth), :], gate.at[pl.ds(top, depth), columns])
            fetch(parts[s].at[pl.ds(depth, depth), :], up.at[pl.ds(top, depth), columns])
    first = len(started)
    for r in range(members):
        for e in range(2):
            block = 2 * r + e
            low = e * (rows + 16)
            fetch(grad_all.at[p ^ r, pl.ds(low, rows), :], cot.at[pl.ds(block * rows, rows), :])
            fetch(grad_all.at[p ^ r, pl.ds(low + rows, 16), pl.ds(0, rows)], codes.at[block])
    for s in range(n):
        plane = lax.rem(z - s + n, n)
        for half, parts in enumerate((here, there)):
            start = pl.multiple_of(half * span + plane * strip, 8)
            for j in range(down.shape[1] // span):
                fetch(
                    parts[s].at[pl.ds(2 * depth + j * strip, strip), :],
                    down.at[pl.ds(start, strip), pl.ds(j * span, span)],
                )
    for copy in started[:first]:
        copy.wait()
    flush(0, 0, x.shape[0])
    row = lax.broadcasted_iota(jnp.int32, (rows, rows), 0)
    col = lax.broadcasted_iota(jnp.int32, (rows, rows), 1)

    def store(value, r, parts):
        to_one, to_two, own, two_low, one_high = parts
        low, high = value[:rows].astype(BF), value[rows:].astype(BF)
        if r == 0:
            own[...] = value
        elif r == 1:
            to_one[:rows], one_high[...] = low, high
        elif r == 2:
            two_low[...], to_two[:rows] = low, high
        else:
            to_one[rows:], to_two[rows:] = low, high

    for chunk in range(2):
        block = slice(chunk * 2 * size, (chunk + 1) * 2 * size)
        gate_pre = dot(x[block], gate[...])
        lifted = dot(x[block], up[...])
        sigmoid = jax.nn.sigmoid(gate_pre)
        activated = gate_pre * sigmoid
        if chunk == 0:
            for copy in started[first:]:
                copy.wait()
            flush(1, 0, cot.shape[0])
        limits = []
        for b in range(4 * chunk, 4 * chunk + 4):
            line = jnp.broadcast_to(codes[b].astype(F32)[:1], (rows, rows))
            code = jnp.sum(jnp.where(row == col, line, 0.0), axis=1, keepdims=True)
            limits.append(
                sum(jnp.where(code == k, float(units >> (members - 1 - k)), 0.0) for k in range(members))
            )
        live = unit_index[:1, :] < jnp.concatenate(limits, axis=0)
        hidden[block] = jnp.where(live, activated * lifted, 0.0).astype(BF)
        grad_hidden = jnp.where(live, contract_cols(cot[block], down[...]), 0.0)
        grad_gate[block] = (
            grad_hidden * lifted * sigmoid * (1.0 + gate_pre * (1.0 - sigmoid))
        ).astype(BF)
        grad_lifted[block] = (grad_hidden * activated).astype(BF)
        for index in (2, 3, 4):
            flush(index, chunk * 2 * size, 2 * size)
        grads = contract_cols(grad_gate[block], gate[...])
        grads += contract_cols(grad_lifted[block], up[...])
        for i in range(2):
            store(grads[i * size : (i + 1) * size], 2 * chunk + i, splits[:5])
        value = dot(hidden[block], down[...])
        for i in range(2):
            store(value[i * size : (i + 1) * size], 2 * chunk + i, splits[5:])
    for index in range(5, 15):
        flush(index, 0, scratch[index].shape[0])
    for copy in finishing:
        copy.wait()


def move(kernel, outs, copies, operands, ins):
    kinds = {"h": pl.BlockSpec(memory_space=pl.ANY), "s": pl.BlockSpec(memory_space=pltpu.SMEM)}
    return pl.pallas_call(
        kernel,
        out_shape=[jax.ShapeDtypeStruct(shape, BF) for shape in outs],
        in_specs=[kinds[k] for k in ins],
        out_specs=[pl.BlockSpec(memory_space=pltpu.VMEM)] * len(outs),
        scratch_shapes=[pltpu.SemaphoreType.DMA((copies,))],
        compiler_params=pltpu.CompilerParams(vmem_limit_bytes=16 * 2**20),
        cost_estimate=small_cost(),
    )(*operands)


def local(
    tokens,
    seq_ids,
    granularity,
    w_qkv,
    w_out,
    gain_attn,
    gain_ffn,
    w_gate,
    w_up,
    w_down,
    out_cotangent,
):
    n = lax.axis_size("batch")
    g = lax.axis_size("gran")
    z = lax.axis_index("batch")
    p = lax.axis_index("gran")
    c = lax.axis_index("ffn")
    rows, width = tokens.shape
    head = width // H
    heads = H // g
    mine = heads * head
    depth = w_qkv.shape[0]
    units = w_gate.shape[2]
    capacity = max(2, (5 * rows + 4 * n * g - 1) // (4 * n * g))

    def hop(x, r):
        return lax.ppermute(x, "gran", [(i, i ^ r) for i in range(g)])

    def pair(x):
        return lax.ppermute(x, "batch", [(i, i ^ 1) for i in range(n)])

    def core(x):
        return lax.ppermute(x, "ffn", [(0, 1), (1, 0)])

    def ring(x, s):
        return lax.ppermute(x, "batch", [(i, (i + s) % n) for i in range(n)])

    def gather_first(x):
        return [x, hop(x, 1), hop(x, 2)]

    def gather_rest(pieces):
        half = pieces[0].shape[0] // 32 * 16 or pieces[0].shape[0] // 2
        return [*pieces, hop(pieces[1][:half], 2), hop(pieces[2][half:], 1)]

    def plane_gather(x):
        return gather_rest(gather_first(x))

    def as_members(pieces):
        return jnp.concatenate(pieces, axis=0).reshape(g, *pieces[0].shape)

    def split_rows(x):
        half = x.shape[1] // 2
        return (
            jnp.concatenate([x[1, :half], x[3, :half]], axis=0),
            jnp.concatenate([x[2, half:], x[3, half:]], axis=0),
            x[0],
            x[2, :half],
            x[1, half:],
        )

    def plane_reduce(to_one, to_two, own, two_low, one_high):
        return plane_reduce_rest(hop(to_one, 1), hop(to_two, 2), own, two_low, one_high)

    def plane_reduce_rest(got_one, got_two, own, two_low, one_high):
        half = two_low.shape[0]
        two_low = (two_low.astype(F32) + got_one[half:].astype(F32)).astype(BF)
        one_high = (one_high.astype(F32) + got_two[half:].astype(F32)).astype(BF)
        low, high = hop(two_low, 2), hop(one_high, 1)
        got = [
            jnp.concatenate([v, w], axis=0).astype(F32)
            for v, w in ((got_one[:half], got_two[:half]), (low, high))
        ]
        return own.astype(F32) + got[0] + got[1]

    def by_member(pieces):
        out = jnp.zeros((g, *pieces[0].shape), pieces[0].dtype)
        for r in range(g):
            out = lax.dynamic_update_index_in_dim(out, pieces[r], p ^ r, 0)
        return out

    def ordered(here, there, axis):
        return jnp.stack(
            [jnp.where(c == 0, here, there), jnp.where(c == 0, there, here)], axis=axis
        )

    def cut(*values):
        return lax.optimization_barrier(values)

    def together(body, *operands):
        made = jax.eval_shape(body, *operands)
        return lax.cond(
            seq_ids[0] >= 0,
            body,
            lambda *given: jax.tree.map(lambda v: jnp.zeros(v.shape, v.dtype), made),
            *operands,
        )

    place = jnp.stack([z, p, c]).astype(jnp.int32)
    hd, sub = depth // 2, depth // g
    hs, blocks = sub // 2, width // mine
    gain_part = jnp.concatenate(
        [first_rows(gain_attn, 8, mine), first_rows(gain_ffn, 8, mine)], axis=0
    )
    token_part = jnp.concatenate([tokens, first_rows(seq_ids, 16, width)], axis=0)
    codes = row_groups(seq_ids, granularity, capacity * n)
    grad_part = jnp.concatenate([out_cotangent, first_rows(codes, 16, width)], axis=0)
    if hs % 8 == 0:
        [first_part] = move(
            functools.partial(first_part_kernel, depth, mine, g),
            [(3 * hd + blocks * hs + 16, mine)],
            blocks + 4,
            (place, w_qkv, w_out, gain_part),
            "shhh",
        )
    else:
        out_part = lax.dynamic_slice(w_out, ((p * 2 + c) * hs, 0), (hs, width))
        first_part = jnp.concatenate(
            [
                lax.dynamic_slice(w_qkv, (c * hd, k * width + p * mine), (hd, mine))
                for k in range(3)
            ]
            + [out_part[:, k * mine : (k + 1) * mine] for k in range(blocks)]
            + [gain_part],
            axis=0,
        )
    shares = 2 * g
    strip = units // n // shares
    share = p * 2 + z % 2
    span = n * strip
    cuts = width // span

    def columns(w, odd):
        return lax.dynamic_index_in_dim(
            w.reshape(depth, n, shares, strip), share ^ odd, 2, keepdims=False
        ).reshape(depth, span)

    def second_part(odd):
        rows_down = lax.dynamic_index_in_dim(
            w_down.reshape(shares, strip, width), share ^ odd, 0, keepdims=False
        )
        return jnp.concatenate(
            [columns(w_gate, odd), columns(w_up, odd)]
            + [rows_down[:, k * span : (k + 1) * span] for k in range(cuts)],
            axis=0,
        )

    first_moved = [ring(first_part, k) for k in range(1, n)]

    def rows_out(first_part, token_part, grad_part):
        token_pieces = plane_gather(token_part)
        first_part, grad_part, *token_pieces = cut(first_part, grad_part, *token_pieces)
        grad_both = jnp.concatenate([grad_part, pair(grad_part)], axis=0)
        return token_pieces, core(first_part), grad_both, second_part(0), second_part(1)

    token_pieces, own_far, grad_both, even_part, odd_part = together(
        rows_out, first_part, token_part, grad_part
    )
    even_part, odd_part, own_far, grad_both, *first_moved = cut(
        even_part, odd_part, own_far, grad_both, *first_moved
    )
    grad_all = lax.all_gather(grad_both, "gran", axis=0)
    first_pieces = [first_part, *first_moved]
    second_here = [even_part] + [
        ring(odd_part if k % 2 else even_part, k) for k in range(1, n)
    ]

    all_rows = g * rows

    def unit(values):
        inverse = lax.rsqrt(jnp.mean(values * values, axis=-1, keepdims=True) + EPSILON)
        return values * inverse, inverse

    def attention(token_pieces, first_pieces, own_far):
        first_far = [own_far, *(core(v) for v in first_pieces[1:3])]
        first_far += [core(v) for v in cut(*first_pieces[3:], *first_far)[: n - 3]]
        frequencies = ROPE_BASE ** (-(2.0 * jnp.arange(head // 2, dtype=F32)) / head)
        frequencies = jnp.broadcast_to(jnp.concatenate([frequencies, frequencies]), (8, head))
        all_normed, my_qkv, queries, keys, values, attended, cosines, sines, bias, gains = call(
            functools.partial(attend_kernel, n, rows, depth, mine, head),
            [
                ((all_rows, width), BF),
                ((width, 3 * mine), BF),
                ((all_rows, mine), BF),
                ((all_rows, mine), BF),
                ((all_rows, mine), BF),
                ((all_rows, mine), BF),
                ((all_rows, head), F32),
                ((all_rows, head), F32),
                ((all_rows, rows), F32),
                ((16, width), F32),
            ],
            [
                pltpu.VMEM((n, 16, mine), BF),
                pltpu.VMEM((all_rows, width), F32),
                pltpu.SemaphoreType.DMA((7 * n,)),
            ],
            "sv" + "v" * 5 + "h" * (2 * n),
            (place, frequencies, *token_pieces, *first_pieces, *first_far),
        )

        low, high = 3 * hd, 3 * hd + blocks * hs
        out_here = jnp.stack([v[low:high] for v in first_pieces])
        out_there = jnp.stack([v[low:high] for v in first_far])

        def out_part_for(r):
            picked = [
                ordered(*(lax.dynamic_index_in_dim(v, s, 0, keepdims=False) for v in (out_here, out_there)), 0)
                for s in [(z - (p ^ r) * (n // g) - j) % n for j in range(n // g)]
            ]
            return jnp.stack(picked)

        out_pieces = [out_part_for(0)] + [hop(out_part_for(r), r) for r in (1, 2)]
        out_pieces.append(hop(after(out_part_for(3), attended, *out_pieces), 3))
        if hs % 8 == 0:
            [my_out] = move(
                functools.partial(out_weight_kernel, n, g, hs, mine),
                [(mine, width)],
                n * 2 * blocks,
                (place, *out_pieces),
                "s" + "h" * g,
            )
        else:
            my_out = by_member(out_pieces).reshape(g, n // g, 2, blocks, hs, mine)
            my_out = my_out.transpose(1, 0, 2, 4, 3, 5).reshape(mine, width)
        attn_parts = call(
            functools.partial(project_kernel, rows),
            split_shapes(rows, width),
            (),
            "vv",
            (attended, my_out),
        )

        middle = tokens.astype(F32) + plane_reduce(*attn_parts)
        unit_second, inverse_second = unit(middle)
        normed_ffn = (unit_second * gains[8:9]).astype(BF)
        both_rows = jnp.concatenate([normed_ffn, pair(normed_ffn)], axis=0)
        kept = (all_normed, my_qkv, my_out, queries, keys, values, attended, cosines, sines, bias)
        return kept, gains, middle, unit_second, inverse_second, both_rows

    kept, gains, middle, unit_second, inverse_second, both_rows = together(
        attention, token_pieces, first_pieces, own_far
    )
    all_normed, my_qkv, my_out, queries, keys, values, attended, cosines, sines, bias = kept
    gain_first, gain_second = gains[0:1], gains[8:9]
    residual = tokens.astype(F32)
    both_rows, grad_all, *second_here = cut(both_rows, grad_all, *second_here)
    row_pieces = plane_gather(both_rows)
    second_far = [core(v) for v in second_here]

    index = jnp.arange(2 * span, dtype=jnp.int32) % span
    unit_index = (index // strip) * (strip * shares) + share * strip + index % strip
    pair_rows = 2 * all_rows
    if strip % 16 == 0:
        shapes = [((pair_rows, width), BF)] * 2 + [((pair_rows, 2 * span), BF)] * 3
        shapes += split_shapes(2 * rows, width) * 2
        group_rows, group_grads, hidden, grad_gate, grad_lifted, *parts = call(
            functools.partial(feed_forward_kernel, n, g, depth, strip, rows),
            shapes,
            [pltpu.VMEM(*v) for v in shapes]
            + [
                pltpu.VMEM((width, 2 * span), BF),
                pltpu.VMEM((width, 2 * span), BF),
                pltpu.VMEM((2 * span, width), BF),
                pltpu.VMEM((2 * g, 16, rows), BF),
                pltpu.SemaphoreType.DMA((5 + 2 * n * (2 + cuts) + 4 * g,)),
                pltpu.SemaphoreType.DMA((18,)),
            ],
            "sv" + "h" * (6 + 2 * n),
            (
                place,
                jnp.broadcast_to(unit_index.astype(F32), (8, 2 * span)),
                *row_pieces,
                grad_all,
                *second_here,
                *second_far,
            ),
            out="h",
        )
        input_parts, partial_ffn = parts[:5], parts[5:]
    else:
        group_rows = jnp.concatenate(row_pieces, axis=0)
        stacks = []
        for pieces in (second_here, second_far):
            out = jnp.zeros((n, *pieces[0].shape), BF)
            for s in range(n):
                out = lax.dynamic_update_index_in_dim(out, pieces[s], (z - s) % n, 0)
            stacks.append(out)
        gate_matrix, up_matrix = (
            jnp.concatenate(
                [v[:, k * depth : (k + 1) * depth].reshape(width, span) for v in stacks], axis=1
            )
            for k in (0, 1)
        )
        down_matrix = jnp.concatenate(
            [v[:, 2 * depth :].reshape(n, cuts, strip, span).transpose(0, 2, 1, 3) for v in stacks],
            axis=0,
        ).reshape(2 * span, width)
        grad_got = jnp.stack(
            [lax.dynamic_index_in_dim(grad_all, p ^ r, 0, keepdims=False) for r in range(g)]
        ).reshape(g, 2, rows + 16, width)
        group_grads = grad_got[:, :, :rows].reshape(2 * g * rows, width)
        group_codes = grad_got[:, :, rows, :rows].reshape(2 * g * rows, 1).astype(jnp.int32)
        group_limits = jnp.where(
            group_codes < 0, 0, jnp.right_shift(jnp.int32(units), jnp.minimum(3 - group_codes, 3))
        )
        live = unit_index[None, :] < group_limits
        gate_pre = dot(group_rows, gate_matrix)
        lifted = dot(group_rows, up_matrix)
        sigmoid_gate = jax.nn.sigmoid(gate_pre)
        activated = gate_pre * sigmoid_gate
        hidden = jnp.where(live, (activated * lifted).astype(BF), jnp.zeros((), BF))
        grad_hidden = jnp.where(live, contract_cols(group_grads, down_matrix), 0.0)
        grad_gate = (
            grad_hidden * lifted * sigmoid_gate * (1.0 + gate_pre * (1.0 - sigmoid_gate))
        ).astype(BF)
        grad_lifted = (grad_hidden * activated).astype(BF)
        partial_input = (
            contract_cols(grad_gate, gate_matrix) + contract_cols(grad_lifted, up_matrix)
        ).astype(BF)
        input_parts = split_rows(partial_input.reshape(g, 2 * rows, width))
        partial_ffn = split_rows(dot(hidden, down_matrix).astype(BF).reshape(g, 2 * rows, width))

    def unit_grads(half):
        low = slice(half * span, (half + 1) * span)
        return (
            contract_rows(group_rows, grad_gate[:, low]),
            contract_rows(group_rows, grad_lifted[:, low]),
            contract_rows(hidden[:, low], group_grads),
        )

    to_one, to_two, *waiting = input_parts
    got = cut(hop(to_one, 1), hop(to_two, 2), *(v.astype(BF) for v in unit_grads(1)))
    reduced = plane_reduce_rest(*got[:2], *waiting)
    gate_sum, up_sum, down_sum = (
        (v + core(w).astype(F32)).astype(BF) for v, w in zip(unit_grads(0), got[2:])
    )
    halves, gate_sum, up_sum, down_sum = cut(reduced, gate_sum, up_sum, down_sum)
    gate_sum = gate_sum.reshape(n, depth, span)
    up_sum = up_sum.reshape(n, depth, span)
    down_sum = down_sum.reshape(n, strip, cuts, span)

    def unit_sums(k):
        own = lax.dynamic_index_in_dim(down_sum, k, 0, keepdims=False).transpose(1, 0, 2)
        return jnp.concatenate(
            [lax.dynamic_index_in_dim(v, k, 0, keepdims=False) for v in (gate_sum, up_sum)]
            + [own.reshape(cuts * strip, span)],
            axis=0,
        )

    own_half, far_half = halves[:rows], pair(halves[rows:].astype(BF))
    to_one, to_two, *branch_waiting = partial_ffn
    to_one, to_two = cut(to_one, to_two, halves)[:2]
    branch_got = hop(to_one, 1), hop(to_two, 2)
    messages = [unit_sums((z + k) % n) for k in range(n)]
    far_half, branch_got, *messages = cut(far_half, branch_got, *messages)
    sums = [messages[0].astype(F32), 0.0]
    moved = [ring(messages[k], k) for k in range(1, n)]

    def my_half(x, which, axis):
        return lax.dynamic_index_in_dim(x, which, axis, keepdims=False)

    def for_member(stacked, r, axis):
        return lax.dynamic_index_in_dim(stacked, p ^ r, axis, keepdims=False)

    def attention_back(own_half, far_half, branch_got):
        grad_normed_ffn = (own_half + far_half.astype(F32)).astype(BF).astype(F32)
        grad_middle = out_cotangent.astype(F32) + norm_back(
            grad_normed_ffn, unit_second, inverse_second, gain_second
        )
        branch_pieces = plane_gather(grad_middle.astype(BF))
        fast = n == g and hs % 16 == 0
        if fast:
            branch_rows = jnp.concatenate(branch_pieces, axis=0)
            out_here, out_there = call(
                functools.partial(out_sums_kernel, g, hs, mine),
                [((g, blocks * hs, mine), BF)] * 2,
                [pltpu.VMEM((mine, mine), F32)],
                "svv",
                (place, attended, branch_rows),
            )
            out_there, *branch_pieces = cut(core(out_there), *branch_pieces)
            out_sum = (out_here.astype(F32) + out_there.astype(F32)).astype(BF)
        got_one, got_two, *branch_pieces = cut(*branch_got, *branch_pieces)
        branch_sum = plane_reduce_rest(got_one, got_two, *branch_waiting)
        grad_branch, grad_packed, *normed_parts = call(
            functools.partial(attend_back_kernel, rows, mine, head),
            [((all_rows, width), BF), ((all_rows, 3 * mine), BF), *split_shapes(rows, width)],
            [pltpu.VMEM((all_rows, mine), BF)],
            "v" * 13,
            (*branch_pieces, my_out, my_qkv, queries, keys, values, cosines, sines, bias),
        )
        branch_sum, grad_packed = cut(branch_sum, grad_packed)
        if fast:
            quarters = [hop(for_member(after(out_sum, grad_packed), r, 0), r) for r in (1, 2)]
            sum_here, sum_there = call(
                functools.partial(weight_sums_kernel, g, depth, mine),
                [((g, 3 * hd, mine), BF)] * 2,
                [pltpu.VMEM((depth, 3 * mine), F32)],
                "svv",
                (place, all_normed, grad_packed),
            )
            sum_there, out_sum, *quarters = cut(sum_there, out_sum, *quarters)
            quarters.append(hop(for_member(out_sum, 3, 0), 3))
            weight_sum = (sum_here.astype(F32) + core(sum_there).astype(F32)).astype(BF)
            last_parts = call(
                functools.partial(last_parts_kernel, g, 3 * hd),
                [((3 * hd + blocks * hs, mine), BF)] * g,
                [pltpu.VMEM((g, blocks * hs, mine), BF)],
                "s" + "v" * (g + 1),
                (place, weight_sum, for_member(out_sum, 0, 0), *quarters),
            )
        else:
            out_grad = contract_rows(attended, grad_branch).astype(BF)
            out_grad = out_grad.reshape(n // g, g, 2, hs, width)
            out_sum = my_half(out_grad, c, 2).astype(F32)
            out_sum = (out_sum + core(my_half(out_grad, 1 - c, 2)).astype(F32)).astype(BF)
            out_sum = by_member(
                [for_member(out_sum, 0, 1)]
                + [hop(for_member(out_sum, r, 1), r) for r in range(1, g)]
            ).reshape(n, hs, blocks, mine)
            qkv_grad = contract_rows(all_normed, grad_packed).astype(BF).reshape(n, 2, hd, 3, mine)
            qkv_sum = my_half(qkv_grad, c, 1).astype(F32)
            qkv_sum += core(my_half(qkv_grad, 1 - c, 1)).astype(F32)
            last_part = jnp.concatenate(
                [
                    qkv_sum.astype(BF).transpose(0, 2, 1, 3).reshape(n, 3 * hd, mine),
                    out_sum.transpose(0, 2, 1, 3).reshape(n, blocks * hs, mine),
                ],
                axis=1,
            )
            last_parts = [
                lax.dynamic_index_in_dim(last_part, (z + k) % n, 0, keepdims=False) for k in range(n)
            ]
        return grad_middle, normed_parts, last_parts, branch_sum

    grad_middle, normed_parts, last_parts, branch_sum = together(
        attention_back, own_half, far_half, branch_got
    )
    cut_values = cut(*moved, *last_parts)
    moved, last_parts = cut_values[: n - 1], cut_values[n - 1 :]
    for k in range(1, n):
        sums[k % 2] += moved[k - 1].astype(F32)
    even_sum, odd_sum = (v.astype(BF) for v in sums)
    last_moved = [ring(last_parts[k], k) for k in range(1, n)]

    def units_out(even_sum, odd_sum, normed_parts):
        unit_pieces = plane_gather(jnp.concatenate([even_sum, odd_sum], axis=0))
        normed_parts = cut(*normed_parts, *unit_pieces)[:5]
        grad_normed = plane_reduce(*normed_parts)
        unit_first, inverse_first = unit(residual)
        input_grad = (
            grad_middle + norm_back(grad_normed, unit_first, inverse_first, gain_first)
        ).astype(BF)
        return list(unit_pieces), input_grad

    unit_pieces, input_grad = together(units_out, even_sum, odd_sum, normed_parts)
    got = cut(*unit_pieces, *last_moved)
    unit_pieces, last_moved = got[:5], got[5:]
    last_sum = last_parts[0].astype(F32) + sum(v.astype(F32) for v in last_moved)
    last_one = gather_first(last_sum.astype(BF))
    if strip % 32 == 0:
        share_gate, share_up, share_down, ffn_part = call(
            functools.partial(unit_results_kernel, n, g, depth, strip),
            [
                ((depth * units // 128, 128), F32),
                ((depth * units // 128, 128), F32),
                ((units // n * width // 128, 128), F32),
                ((depth, 1), F32),
            ],
            [
                pltpu.VMEM((shares, 2 * depth + cuts * strip, span), BF),
                pltpu.SemaphoreType.DMA((3, shares)),
            ],
            "s" + "h" * 5 + "vv",
            (place, *unit_pieces, w_gate[:, 0], w_up[:, 0]),
        )
        ffn_part = ffn_part[:, 0]
    else:
        got = as_members(unit_pieces).reshape(g, 2, -1, span)
        all_units = jnp.zeros((shares, *got.shape[2:]), BF)
        for r in range(g):
            for odd in (0, 1):
                all_units = lax.dynamic_update_index_in_dim(
                    all_units, got[r, odd], (p ^ r) * 2 + (z % 2) ^ odd, 0
                )

        def columns_back(pieces):
            return (
                pieces.reshape(shares, depth, n, strip)
                .transpose(1, 2, 0, 3)
                .reshape(depth, units)
                .astype(F32)
            )

        share_gate = columns_back(all_units[:, :depth])
        share_up = columns_back(all_units[:, depth : 2 * depth])
        share_down = (
            all_units[:, 2 * depth :]
            .reshape(shares, cuts, strip, span)
            .transpose(0, 2, 1, 3)
            .reshape(units // n, width)
            .astype(F32)
        )
        ffn_part = jnp.sum(
            share_gate * w_gate[:, 0].astype(F32) + share_up * w_up[:, 0].astype(F32), axis=1
        )
    *last_one, ffn_part = cut(*last_one, ffn_part)
    last_pieces = gather_rest(last_one)
    share_gain_ffn = (ffn_part + core(ffn_part)) / gain_ffn.astype(F32)
    branch_ffn = branch_sum[:rows] + pair(branch_sum[rows:].astype(BF)).astype(F32)
    outputs = (middle + branch_ffn.astype(BF).astype(F32)).astype(BF)
    if hs % 16 == 0:
        share_qkv, share_out, attn_part = call(
            functools.partial(attention_results_kernel, g, depth, mine),
            [((depth, 3 * width), F32), ((depth, width), F32), ((depth, 1), F32)],
            [
                pltpu.VMEM((depth, 3 * width), BF),
                pltpu.VMEM((depth, width), BF),
                pltpu.SemaphoreType.DMA((2 * (g + 1) * (3 + blocks),)),
            ],
            "s" + "h" * 10 + "v",
            (place, *last_pieces, *(core(v) for v in last_pieces), w_qkv),
        )
        attn_part = attn_part[:, 0]
    else:
        last_got = as_members(last_pieces)
        last_got = by_member([last_got[r] for r in range(g)])
        last_both = ordered(last_got, core(last_got), 0)
        share_qkv = (
            last_both[:, :, : 3 * hd]
            .reshape(2, g, 3, hd, mine)
            .transpose(0, 3, 2, 1, 4)
            .reshape(depth, 3 * width)
            .astype(F32)
        )
        share_out = (
            last_both[:, :, 3 * hd :]
            .reshape(2, g, blocks, hs, mine)
            .transpose(1, 0, 3, 2, 4)
            .reshape(depth, width)
            .astype(F32)
        )
        attn_part = jnp.sum(share_qkv * w_qkv.astype(F32), axis=1)
    share_gain_attn = attn_part / gain_attn.astype(F32)
    return (
        outputs,
        input_grad,
        share_qkv,
        share_out,
        share_gain_attn,
        share_gain_ffn,
        share_gate.reshape(depth, 1, units),
        share_up.reshape(depth, 1, units),
        share_down.reshape(units // n, 1, width),
    )


def solution(mesh):
    in_specs = (
        P(("batch", "gran", "ffn"), None),
        P(("batch", "gran", "ffn")),
        P(("batch", "gran", "ffn")),
        P("batch", None),
        P("batch", None),
        P("batch"),
        P("batch"),
        P("batch", "ffn", None),
        P("batch", "ffn", None),
        P("batch", "ffn", None),
        P(("batch", "gran", "ffn"), None),
    )
    out_specs = (
        P(("batch", "gran", "ffn"), None),
        P(("batch", "gran", "ffn"), None),
        P("batch", None),
        P("batch", None),
        P("batch"),
        P("batch"),
        P("batch", "ffn", None),
        P("batch", "ffn", None),
        P("batch", "ffn", None),
    )
    return jax.shard_map(local, mesh=mesh, in_specs=in_specs, out_specs=out_specs, check_vma=False)
```

```python
import functools
import math

import jax
import jax.numpy as jnp
from jax import lax
from jax.experimental import pallas as pl
from jax.experimental.pallas import tpu as pltpu
from jax.sharding import PartitionSpec as P

H = 12


EPSILON = 1e-06
NEG_FILL = -1e30
ROPE_BASE = 10000.0
BF = jnp.bfloat16
F32 = jnp.float32


def row_groups(seq_rows, seq_groups, kept_rows):
    labels = jnp.arange(seq_groups.shape[0], dtype=jnp.int32)
    member = (seq_rows[:, None] == labels[None, :]).astype(jnp.int32)
    group_id = jnp.sum(member * seq_groups[None, :], axis=1)
    index = jnp.arange(seq_rows.shape[0], dtype=jnp.int32)
    earlier = (group_id[None, :] == group_id[:, None]) & (index[None, :] < index[:, None])
    rank = jnp.sum(earlier.astype(jnp.int32), axis=1)
    return jnp.where(rank < kept_rows, group_id, -1)


def dot(left, right):
    return jnp.dot(left, right, preferred_element_type=F32)


def contract_rows(left, right):
    return lax.dot_general(left, right, (((0,), (0,)), ((), ())), preferred_element_type=F32)


def contract_cols(left, right):
    return lax.dot_general(left, right, (((1,), (1,)), ((), ())), preferred_element_type=F32)


def norm_back(grad_normed, unit_rows, inverse_rms, gain):
    scaled = grad_normed * gain
    return inverse_rms * (scaled - unit_rows * jnp.mean(scaled * unit_rows, axis=-1, keepdims=True))


def first_rows(values, count, width):
    return jnp.pad(values.astype(BF)[None, :], ((0, count - 1), (0, width - values.shape[0])))


def after(value, *others):
    return lax.optimization_barrier((value, *others))[0]


def small_cost():
    return pl.CostEstimate(flops=1, bytes_accessed=1, transcendentals=0)


def call(kernel, outs, scratch=(), ins=(), operands=(), out="v", spare=8):
    held = [v for k, v in zip(ins, operands) if k == "v"]
    held += [jax.ShapeDtypeStruct(*v) for v in outs if out == "v"]
    held += [v for v in scratch if v.dtype in (BF, F32)]
    limit = sum(math.prod(v.shape) * v.dtype.itemsize for v in held) + spare * 2**20
    kinds = {
        "v": pl.BlockSpec(memory_space=pltpu.VMEM),
        "h": pl.BlockSpec(memory_space=pl.ANY),
        "s": pl.BlockSpec(memory_space=pltpu.SMEM),
    }
    return pl.pallas_call(
        kernel,
        out_shape=[jax.ShapeDtypeStruct(shape, dtype) for shape, dtype in outs],
        in_specs=[kinds[k] for k in ins],
        out_specs=[kinds[out]] * len(outs),
        scratch_shapes=list(scratch),
        compiler_params=pltpu.CompilerParams(vmem_limit_bytes=limit),
        cost_estimate=small_cost(),
    )(*operands)


def split_parts(value, rows, to_one, to_two, own, two_low, one_high):
    half = rows // 2
    to_one[:half] = value[rows : rows + half].astype(BF)
    to_one[half:] = value[3 * rows : 3 * rows + half].astype(BF)
    to_two[:half] = value[2 * rows + half : 3 * rows].astype(BF)
    to_two[half:] = value[3 * rows + half :].astype(BF)
    own[...] = value[:rows]
    two_low[...] = value[2 * rows : 2 * rows + half].astype(BF)
    one_high[...] = value[rows + half : 2 * rows].astype(BF)


def split_shapes(rows, width):
    half = rows // 2
    return [
        ((rows, width), BF),
        ((rows, width), BF),
        ((rows, width), F32),
        ((half, width), BF),
        ((half, width), BF),
    ]


def reduce_first_kernel(got_one, got_two, own, two_low, one_high, to_two, to_one, total):
    half = two_low.shape[0]
    to_two[...] = (two_low[...].astype(F32) + got_one[half:].astype(F32)).astype(BF)
    to_one[...] = (one_high[...].astype(F32) + got_two[half:].astype(F32)).astype(BF)
    total[:half] = own[:half].astype(F32) + got_one[:half].astype(F32)
    total[half:] = own[half:].astype(F32) + got_two[:half].astype(F32)


def attend_kernel(n, rows, depth, mine, head, place, freq, *refs):
    tokens, refs = refs[:5], refs[5:]
    here, there, refs = refs[:n], refs[n : 2 * n], refs[2 * n :]
    normed, weight, queries, keys, values, attended, cosines, sines, bias, gains = refs[:10]
    gain_rows, unit_rows, sems = refs[10:]
    z, c = place[0], place[2]
    hd = depth // 2
    width = n * depth
    copies = []
    for s in range(n):
        plane = lax.rem(z - s + n, n)
        for which, pieces in ((c, here), (1 - c, there)):
            start = pl.multiple_of(plane * depth + which * hd, 8)
            for k in range(3):
                copies.append(
                    pltpu.make_async_copy(
                        pieces[s].at[pl.ds(k * hd, hd), :],
                        weight.at[pl.ds(start, hd), pl.ds(k * mine, mine)],
                        sems.at[len(copies)],
                    )
                )
        copies.append(
            pltpu.make_async_copy(
                here[s].at[pl.ds(here[s].shape[0] - 16, 16), :], gain_rows.at[plane], sems.at[len(copies)]
            )
        )
    for copy in copies:
        copy.start()

    half = rows // 2
    third = tokens[3].shape[0]
    spans = [(tokens[0], 0, 0, rows), (tokens[1], 0, rows, rows), (tokens[2], 0, 2 * rows, rows)]
    spans += [(tokens[3], 0, 3 * rows, third), (tokens[4], 0, 3 * rows + third, rows - third)]
    for ref, low, at, count in spans:
        x = ref[low : low + count, :].astype(F32)
        inverse = lax.rsqrt(jnp.mean(x * x, axis=-1, keepdims=True) + EPSILON)
        unit_rows[at : at + count] = x * inverse

    row = lax.broadcasted_iota(jnp.int32, (rows, rows), 0)
    col = lax.broadcasted_iota(jnp.int32, (rows, rows), 1)
    lane = lax.broadcasted_iota(jnp.int32, (rows, head), 1)
    sign = jnp.where(lane < head // 2, -1.0, 1.0)
    for b in range(4):
        ref, low = (tokens[b], rows) if b < 3 else (tokens[4], rows - third)
        ids = ref[low : low + 8, :rows].astype(F32)[:1]
        ids_row = jnp.broadcast_to(ids, (rows, rows))
        ids_col = jnp.sum(jnp.where(row == col, ids_row, 0.0), axis=1, keepdims=True)
        before = jnp.sum(jnp.where(ids_row < ids_col, 1.0, 0.0), axis=1, keepdims=True)
        positions = row[:, :1].astype(F32) - before
        angles = positions * freq[:1, :]
        cosines[b * rows : (b + 1) * rows] = jnp.cos(angles)
        sines[b * rows : (b + 1) * rows] = jnp.sin(angles) * sign
        bias[b * rows : (b + 1) * rows] = jnp.where(
            (ids_row == ids_col) & (row >= col), 0.0, NEG_FILL
        )

    for copy in copies:
        copy.wait()
    for k in range(n):
        block = slice(k * depth, (k + 1) * depth)
        both = gain_rows[k].astype(F32)
        gains[0:8, block] = jnp.broadcast_to(both[0:1, :depth], (8, depth))
        gains[8:16, block] = jnp.broadcast_to(both[8:9, :depth], (8, depth))
    normed[...] = (unit_rows[...] * gains[0:1, :]).astype(BF)
    x = normed[...]
    cos, sin = cosines[...], sines[...]
    scale = 1.0 / math.sqrt(head)
    for k, out in enumerate((queries, keys, values)):
        packed = dot(x, weight[:, k * mine : (k + 1) * mine])
        for h in range(mine // head):
            part = packed[:, h * head : (h + 1) * head]
            if k < 2:
                part = part * cos + pltpu.roll(part, head // 2, 1) * sin
            if k == 0:
                part = part * scale
            out[:, h * head : (h + 1) * head] = part.astype(BF)
    for b in range(4):
        for h in range(mine // head):
            here_rows, here_cols = slice(b * rows, (b + 1) * rows), slice(h * head, (h + 1) * head)
            scores = contract_cols(queries[here_rows, here_cols], keys[here_rows, here_cols])
            probs = softmax(scores + bias[here_rows])
            attended[here_rows, here_cols] = dot(
                probs.astype(BF), values[here_rows, here_cols]
            ).astype(BF)


def softmax(scores):
    exponent = jnp.exp(scores - jnp.max(scores, axis=-1, keepdims=True))
    return exponent / jnp.sum(exponent, axis=-1, keepdims=True)


def project_kernel(rows, attended, out, *parts):
    split_parts(dot(attended[...], out[...]), rows, *parts)


def attend_back_kernel(rows, mine, head, *refs):
    grads, refs = refs[:5], refs[5:]
    out, weight, queries, keys, values, cosines, sines, bias = refs[:8]
    branch, packed, *parts = refs[8:-1]
    attended_grad = refs[-1]
    third = grads[3].shape[0]
    at = 0
    for ref in grads:
        branch[at : at + ref.shape[0]] = ref[...]
        at += ref.shape[0]
    del third
    attended_grad[...] = contract_cols(branch[...], out[...]).astype(BF)
    scale = 1.0 / math.sqrt(head)
    for b in range(4):
        r = slice(b * rows, (b + 1) * rows)
        cos, sin = cosines[r], sines[r]
        for h in range(mine // head):
            cols = slice(h * head, (h + 1) * head)
            q, k, v, grad = queries[r, cols], keys[r, cols], values[r, cols], attended_grad[r, cols]
            probs = softmax(contract_cols(q, k) + bias[r])
            grad_probs = contract_cols(grad, v)
            grad_scores = probs * (
                grad_probs - jnp.sum(probs * grad_probs, axis=-1, keepdims=True)
            )
            grad_scores = grad_scores.astype(BF)
            grad_q = dot(grad_scores, k).astype(BF).astype(F32) * scale
            grad_k = contract_rows(grad_scores, q).astype(BF).astype(F32)
            grad_v = contract_rows(probs.astype(BF), grad)
            for j, part in enumerate((grad_q, grad_k, grad_v)):
                if j < 2:
                    part = part * cos - pltpu.roll(part, head // 2, 1) * sin
                packed[r, j * mine + h * head : j * mine + (h + 1) * head] = part.astype(BF)
    split_parts(contract_cols(packed[...], weight[...]), rows, *parts)


def first_part_kernel(depth, mine, members, place, w_qkv, w_out, gains, out, sems):
    p, c = place[1], place[2]
    hd, hs = depth // 2, depth // members // 2
    width = w_out.shape[1]
    moves = []
    for k in range(3):
        column = pl.multiple_of(k * width + p * mine, 128)
        moves.append((w_qkv.at[pl.ds(c * hd, hd), pl.ds(column, mine)], k * hd, hd))
    top = pl.multiple_of((p * 2 + c) * hs, 8)
    for k in range(width // mine):
        block = w_out.at[pl.ds(top, hs), pl.ds(k * mine, mine)]
        moves.append((block, 3 * hd + k * hs, hs))
    moves.append((gains, out.shape[0] - 16, 16))
    copies = [
        pltpu.make_async_copy(source, out.at[pl.ds(at, count), :], sems.at[i])
        for i, (source, at, count) in enumerate(moves)
    ]
    for copy in copies:
        copy.start()
    for copy in copies:
        copy.wait()


def out_weight_kernel(n, members, hs, mine, place, *refs):
    pieces, out, sems = refs[:members], refs[members], refs[members + 1]
    p = place[1]
    copies = []
    for r in range(members):
        for j in range(n // members):
            for half in range(2):
                top = pl.multiple_of(((j * members + (p ^ r)) * 2 + half) * hs, 8)
                for k in range(out.shape[1] // mine):
                    copies.append(
                        pltpu.make_async_copy(
                            pieces[r].at[j, half, pl.ds(k * hs, hs), :],
                            out.at[pl.ds(top, hs), pl.ds(k * mine, mine)],
                            sems.at[len(copies)],
                        )
                    )
    for copy in copies:
        copy.start()
    for copy in copies:
        copy.wait()


def strips_of(tile, strip):
    at, out = 0, []
    while at < 128:
        share, first = divmod(tile * 128 + at, strip)
        count = min(strip - first, 128 - at)
        out.append((share, first, at, count))
        at += count
    return out


def unit_results_kernel(n, members, depth, strip, place, *refs):
    pieces, w_gate, w_up = refs[:5], refs[5], refs[6]
    gate, up, down, gain, held, sems = refs[7:]
    shares, span = 2 * members, n * strip
    cuts = (held.shape[1] - 2 * depth) // strip
    z, p = place[0], place[1]
    parts = [(0, depth), (depth, depth), (2 * depth, cuts * strip)]
    copies = []
    for low, count in parts:
        group = []
        for r in range(members):
            for odd in range(2):
                share = (p ^ r) * 2 + (lax.rem(z, 2) ^ odd)
                if r < 3:
                    ref, top = pieces[r], odd * held.shape[1] + low
                else:
                    ref, top = pieces[3 + odd], low
                group.append(
                    pltpu.make_async_copy(
                        ref.at[pl.ds(top, count), :],
                        held.at[share, pl.ds(low, count), :],
                        sems.at[len(copies), r * 2 + odd],
                    )
                )
        for copy in group:
            copy.start()
        copies.append(group)
    lanes = lax.broadcasted_iota(jnp.int32, (depth, 128), 1)
    row_tiles = n * shares * strip // 128
    total = jnp.zeros((depth, 128), F32)
    for which, (out, weight) in enumerate(((gate, w_gate), (up, w_up))):
        for copy in copies[which]:
            copy.wait()
        rows = slice(which * depth, (which + 1) * depth)
        for k in range(n):
            for tile in range(shares * strip // 128):
                made = jnp.zeros((depth, 128), F32)
                for share, first, lane, count in strips_of(tile, strip):
                    column = k * strip + first
                    while count > 0:
                        source, offset = divmod(column, 128)
                        some = min(count, 128 - offset)
                        value = held[share, rows, source * 128 : (source + 1) * 128].astype(F32)
                        if lane != offset:
                            value = pltpu.roll(value, (lane - offset) % 128, 1)
                        made = jnp.where((lanes >= lane) & (lanes < lane + some), value, made)
                        column, lane, count = column + some, lane + some, count - some
                at = k * (shares * strip // 128) + tile
                out[pl.ds(at, depth, stride=row_tiles), :] = made
                total += made * weight[:, at * 128 : (at + 1) * 128].astype(F32)
    gain[...] = jnp.sum(total, axis=1, keepdims=True)
    for copy in copies[2]:
        copy.wait()
    wide = cuts * span // 128
    for share in range(shares):
        for k in range(cuts):
            low = 2 * depth + k * strip
            for tile in range(span // 128):
                value = held[share, low : low + strip, tile * 128 : (tile + 1) * 128].astype(F32)
                start = share * strip * wide + k * (span // 128) + tile
                down[pl.ds(start, strip, stride=wide), :] = value


def attention_results_kernel(members, depth, mine, place, *refs):
    here, there, w_qkv = refs[:5], refs[5:10], refs[10]
    qkv, out, gain, held, held_out, sems = refs[11:]
    p, c = place[1], place[2]
    hd, hs = depth // 2, depth // members // 2
    width = held_out.shape[1]
    blocks = width // mine
    copies = []

    def add(source, target):
        copies.append(pltpu.make_async_copy(source, target, sems.at[len(copies)]))

    def place_rows(ref, first, low, count, r, half):
        for k in range(3):
            top, end = max(low, k * hd), min(low + count, (k + 1) * hd)
            if top < end:
                add(
                    ref.at[pl.ds(first + top - low, end - top), :],
                    held.at[
                        pl.ds(pl.multiple_of(half * hd + top - k * hd, 8), end - top),
                        pl.ds(pl.multiple_of(k * width + (p ^ r) * mine, 128), mine),
                    ],
                )
        for k in range(blocks):
            base = 3 * hd + k * hs
            top, end = max(low, base), min(low + count, base + hs)
            if top < end:
                add(
                    ref.at[pl.ds(first + top - low, end - top), :],
                    held_out.at[
                        pl.ds(pl.multiple_of(((p ^ r) * 2 + half) * hs + top - base, 8), end - top),
                        pl.ds(k * mine, mine),
                    ],
                )

    rows = 3 * hd + blocks * hs
    for half, pieces in ((c, here), (1 - c, there)):
        for r in range(3):
            place_rows(pieces[r], 0, 0, rows, r, half)
        third = pieces[3].shape[0]
        place_rows(pieces[3], 0, 0, third, 3, half)
        place_rows(pieces[4], 0, third, rows - third, 3, half)
    for copy in copies:
        copy.start()
    for copy in copies:
        copy.wait()
    total = jnp.zeros((depth, 128), F32)
    for tile in range(3 * width // 128):
        cols = slice(tile * 128, (tile + 1) * 128)
        value = held[:, cols].astype(F32)
        qkv[:, cols] = value
        total += value * w_qkv[:, cols].astype(F32)
    gain[...] = jnp.sum(total, axis=1, keepdims=True)
    out[...] = held_out[...].astype(F32)


def out_sums_kernel(members, hs, mine, place, attended, branch, mine_out, theirs_out, held):
    c = place[2]
    for k in range(branch.shape[1] // mine):
        cols = slice(k * mine, (k + 1) * mine)
        held[...] = contract_rows(attended[...], branch[:, cols])
        for out, half in ((mine_out, c), (theirs_out, 1 - c)):
            for quarter in range(members):
                start = pl.multiple_of((quarter * 2 + half) * hs, 8)
                value = held[pl.ds(start, hs), :]
                out[quarter, k * hs : (k + 1) * hs, :] = value.astype(BF)


def weight_sums_kernel(members, depth, mine, place, normed, packed, mine_out, theirs_out, held):
    c = place[2]
    hd = depth // 2
    for plane in range(members):
        block = slice(plane * depth, (plane + 1) * depth)
        held[...] = contract_rows(normed[:, block], packed[...])
        for out, half in ((mine_out, c), (theirs_out, 1 - c)):
            start = pl.multiple_of(half * hd, 8)
            for k in range(3):
                value = held[pl.ds(start, hd), k * mine : (k + 1) * mine]
                out[plane, k * hd : (k + 1) * hd, :] = value.astype(BF)


def last_parts_kernel(members, low, place, *refs):
    sums, quarters, outs, held = refs[0], refs[1 : members + 1], refs[members + 1 : -1], refs[-1]
    z, p = place[0], place[1]
    for r in range(members):
        held[r] = quarters[r][...]
    for k in range(members):
        plane = lax.rem(z + k, members)
        outs[k][:low] = sums[plane]
        outs[k][low:] = held[p ^ plane]


def feed_forward_kernel(n, members, depth, strip, rows, e, place, unit_index, *refs):
    pieces, all_grads, refs = refs[:5], refs[5], refs[6:]
    here, there, refs = refs[:n], refs[n : 2 * n], refs[2 * n :]
    outs, scratch = refs[:14], refs[14:28]
    splits, (x, cot, hidden, grads_two) = scratch[:10], scratch[10:]
    gate, up, down, codes, in_sems, out_sems = refs[28:]
    z, p = place[0], place[1]
    span = n * strip
    units = span * 2 * members
    started, finishing = [], []

    def fetch(source, target):
        copy = pltpu.make_async_copy(source, target, in_sems.at[len(started)])
        copy.start()
        started.append(copy)

    def flush(index):
        copy = pltpu.make_async_copy(scratch[index], outs[index], out_sems.at[index])
        copy.start()
        finishing.append(copy)

    at = 0
    for ref in pieces:
        fetch(ref, x.at[pl.ds(at, ref.shape[0]), :])
        at += ref.shape[0]
    for s in range(n):
        plane = lax.rem(z - s + n, n)
        top = pl.multiple_of(plane * depth, 8)
        for half, parts in enumerate((here, there)):
            columns = pl.ds(half * span, span)
            fetch(parts[s].at[pl.ds(0, depth), :], gate.at[pl.ds(top, depth), columns])
            fetch(parts[s].at[pl.ds(depth, depth), :], up.at[pl.ds(top, depth), columns])
    first = len(started)
    for r in range(members):
        fetch(all_grads.at[p ^ r, e, pl.ds(0, rows), :], cot.at[pl.ds(r * rows, rows), :])
        fetch(all_grads.at[p ^ r, e, pl.ds(rows, 16), pl.ds(0, rows)], codes.at[r])
    for s in range(n):
        plane = lax.rem(z - s + n, n)
        for half, parts in enumerate((here, there)):
            start = pl.multiple_of(half * span + plane * strip, 8)
            for j in range(down.shape[1] // span):
                fetch(
                    parts[s].at[pl.ds(2 * depth + j * strip, strip), :],
                    down.at[pl.ds(start, strip), pl.ds(j * span, span)],
                )
    for copy in started[:first]:
        copy.wait()
    flush(10)
    row = lax.broadcasted_iota(jnp.int32, (rows, rows), 0)
    col = lax.broadcasted_iota(jnp.int32, (rows, rows), 1)

    gate_pre = dot(x[...], gate[...])
    lifted = dot(x[...], up[...])
    sigmoid = jax.nn.sigmoid(gate_pre)
    activated = gate_pre * sigmoid
    for copy in started[first:]:
        copy.wait()
    flush(11)
    limits = []
    for r in range(members):
        line = jnp.broadcast_to(codes[r].astype(F32)[:1], (rows, rows))
        code = jnp.sum(jnp.where(row == col, line, 0.0), axis=1, keepdims=True)
        limits.append(
            sum(jnp.where(code == k, float(units >> (members - 1 - k)), 0.0) for k in range(members))
        )
    live = unit_index[:1, :] < jnp.concatenate(limits, axis=0)
    hidden[...] = jnp.where(live, activated * lifted, 0.0).astype(BF)
    grad_hidden = jnp.where(live, contract_cols(cot[...], down[...]), 0.0)
    wide = 2 * span
    grads_two[:, :wide] = (
        grad_hidden * lifted * sigmoid * (1.0 + gate_pre * (1.0 - sigmoid))
    ).astype(BF)
    grads_two[:, wide:] = (grad_hidden * activated).astype(BF)
    flush(12)
    flush(13)
    grads = contract_cols(grads_two[:, :wide], gate[...])
    grads += contract_cols(grads_two[:, wide:], up[...])
    split_parts(grads, rows, *splits[:5])
    for index in range(5):
        flush(index)
    split_parts(dot(hidden[...], down[...]), rows, *splits[5:])
    for index in range(5, 10):
        flush(index)
    for copy in finishing:
        copy.wait()


def unit_sums_kernel(n, depth, strip, *refs):
    parts, (here, there) = (refs[:4], refs[4:8]), refs[8:]
    span = n * strip
    for plane in range(n):
        block = slice(plane * depth, (plane + 1) * depth)
        made = sum(contract_rows(x[:, block], grads[...]) for x, _, _, grads in parts)
        for k in range(2):
            for half, out in enumerate((here, there)):
                low = (2 * k + half) * span
                value = made[:, low : low + span].astype(BF)
                out[plane, k * depth : (k + 1) * depth, :] = value
    for j in range(parts[0][1].shape[1] // span):
        cols = slice(j * span, (j + 1) * span)
        made = sum(contract_rows(hidden[...], cot[:, cols]) for _, cot, hidden, _ in parts)
        made = made.astype(BF)
        for half, out in enumerate((here, there)):
            for plane in range(n):
                low, at = half * span + plane * strip, 2 * depth + j * strip
                out[plane, at : at + strip, :] = made[low : low + strip]


def move(kernel, outs, copies, operands, ins):
    kinds = {"h": pl.BlockSpec(memory_space=pl.ANY), "s": pl.BlockSpec(memory_space=pltpu.SMEM)}
    return pl.pallas_call(
        kernel,
        out_shape=[jax.ShapeDtypeStruct(shape, BF) for shape in outs],
        in_specs=[kinds[k] for k in ins],
        out_specs=[pl.BlockSpec(memory_space=pltpu.VMEM)] * len(outs),
        scratch_shapes=[pltpu.SemaphoreType.DMA((copies,))],
        compiler_params=pltpu.CompilerParams(vmem_limit_bytes=56 * 2**20),
        cost_estimate=small_cost(),
    )(*operands)


def local(
    tokens,
    seq_ids,
    granularity,
    w_qkv,
    w_out,
    gain_attn,
    gain_ffn,
    w_gate,
    w_up,
    w_down,
    out_cotangent,
):
    n = lax.axis_size("batch")
    g = lax.axis_size("gran")
    z = lax.axis_index("batch")
    p = lax.axis_index("gran")
    c = lax.axis_index("ffn")
    rows, width = tokens.shape
    head = width // H
    heads = H // g
    mine = heads * head
    depth = w_qkv.shape[0]
    units = w_gate.shape[2]
    capacity = max(2, (5 * rows + 4 * n * g - 1) // (4 * n * g))

    def hop(x, r):
        return lax.ppermute(x, "gran", [(i, i ^ r) for i in range(g)])

    def pair(x):
        return lax.ppermute(x, "batch", [(i, i ^ 1) for i in range(n)])

    def core(x):
        return lax.ppermute(x, "ffn", [(0, 1), (1, 0)])

    def ring(x, s):
        return lax.ppermute(x, "batch", [(i, (i + s) % n) for i in range(n)])

    def gather_first(x):
        return [x, hop(x, 1), hop(x, 2)]

    def gather_rest(pieces):
        half = pieces[0].shape[0] // 32 * 16 or pieces[0].shape[0] // 2
        return [*pieces, hop(pieces[1][:half], 2), hop(pieces[2][half:], 1)]

    def plane_gather(x):
        return gather_rest(gather_first(x))

    def as_members(pieces):
        return jnp.concatenate(pieces, axis=0).reshape(g, *pieces[0].shape)

    def split_rows(x):
        half = x.shape[1] // 2
        return (
            jnp.concatenate([x[1, :half], x[3, :half]], axis=0),
            jnp.concatenate([x[2, half:], x[3, half:]], axis=0),
            x[0],
            x[2, :half],
            x[1, half:],
        )

    def plane_reduce(to_one, to_two, own, two_low, one_high):
        return plane_reduce_rest(hop(to_one, 1), hop(to_two, 2), own, two_low, one_high)

    def plane_reduce_rest(got_one, got_two, own, two_low, one_high):
        half, columns = two_low.shape
        two_low, one_high, total = call(
            reduce_first_kernel,
            [((half, columns), BF), ((half, columns), BF), ((2 * half, columns), F32)],
            (),
            "v" * 5,
            (got_one, got_two, own, two_low, one_high),
        )
        return total + jnp.concatenate([hop(two_low, 2), hop(one_high, 1)], axis=0).astype(F32)

    def by_member(pieces):
        out = jnp.zeros((g, *pieces[0].shape), pieces[0].dtype)
        for r in range(g):
            out = lax.dynamic_update_index_in_dim(out, pieces[r], p ^ r, 0)
        return out

    def ordered(here, there, axis):
        return jnp.stack(
            [jnp.where(c == 0, here, there), jnp.where(c == 0, there, here)], axis=axis
        )

    def cut(*values):
        return lax.optimization_barrier(values)

    def together(body, *operands):
        made = jax.eval_shape(body, *operands)
        return lax.cond(
            seq_ids[0] >= 0,
            body,
            lambda *given: jax.tree.map(lambda v: jnp.zeros(v.shape, v.dtype), made),
            *operands,
        )

    place = jnp.stack([z, p, c]).astype(jnp.int32)
    hd, sub = depth // 2, depth // g
    hs, blocks = sub // 2, width // mine
    gain_part = jnp.concatenate(
        [first_rows(gain_attn, 8, mine), first_rows(gain_ffn, 8, mine)], axis=0
    )
    token_part = jnp.concatenate([tokens, first_rows(seq_ids, 16, width)], axis=0)
    codes = row_groups(seq_ids, granularity, capacity * n)
    grad_part = jnp.concatenate([out_cotangent, first_rows(codes, 16, width)], axis=0)
    if hs % 8 == 0:
        [first_part] = move(
            functools.partial(first_part_kernel, depth, mine, g),
            [(3 * hd + blocks * hs + 16, mine)],
            blocks + 4,
            (place, w_qkv, w_out, gain_part),
            "shhh",
        )
    else:
        out_part = lax.dynamic_slice(w_out, ((p * 2 + c) * hs, 0), (hs, width))
        first_part = jnp.concatenate(
            [
                lax.dynamic_slice(w_qkv, (c * hd, k * width + p * mine), (hd, mine))
                for k in range(3)
            ]
            + [out_part[:, k * mine : (k + 1) * mine] for k in range(blocks)]
            + [gain_part],
            axis=0,
        )
    shares = 2 * g
    strip = units // n // shares
    share = p * 2 + z % 2
    span = n * strip
    cuts = width // span

    def columns(w, odd):
        return lax.dynamic_index_in_dim(
            w.reshape(depth, n, shares, strip), share ^ odd, 2, keepdims=False
        ).reshape(depth, span)

    def second_part(odd):
        rows_down = lax.dynamic_index_in_dim(
            w_down.reshape(shares, strip, width), share ^ odd, 0, keepdims=False
        )
        return jnp.concatenate(
            [columns(w_gate, odd), columns(w_up, odd)]
            + [rows_down[:, k * span : (k + 1) * span] for k in range(cuts)],
            axis=0,
        )

    first_moved = [ring(first_part, k) for k in range(1, n)]

    def rows_out(first_part, token_part, grad_part):
        token_pieces = plane_gather(token_part)
        first_part, grad_part, *token_pieces = cut(first_part, grad_part, *token_pieces)
        grad_both = jnp.stack([grad_part, pair(grad_part)])
        return token_pieces, core(first_part), grad_both, second_part(0), second_part(1)

    token_pieces, own_far, grad_both, even_part, odd_part = together(
        rows_out, first_part, token_part, grad_part
    )
    even_part, odd_part, own_far, grad_both, *first_moved = cut(
        even_part, odd_part, own_far, grad_both, *first_moved
    )
    all_grads = lax.all_gather(grad_both, "gran", axis=0)
    first_pieces = [first_part, *first_moved]
    second_odd = {k: ring(odd_part, k) for k in range(1, n, 2)}

    all_rows = g * rows

    def unit(values):
        inverse = lax.rsqrt(jnp.mean(values * values, axis=-1, keepdims=True) + EPSILON)
        return values * inverse, inverse

    def attention(token_pieces, first_pieces, own_far):
        first_far = [own_far, *(core(v) for v in first_pieces[1:])]
        frequencies = ROPE_BASE ** (-(2.0 * jnp.arange(head // 2, dtype=F32)) / head)
        frequencies = jnp.broadcast_to(jnp.concatenate([frequencies, frequencies]), (8, head))
        all_normed, my_qkv, queries, keys, values, attended, cosines, sines, bias, gains = call(
            functools.partial(attend_kernel, n, rows, depth, mine, head),
            [
                ((all_rows, width), BF),
                ((width, 3 * mine), BF),
                ((all_rows, mine), BF),
                ((all_rows, mine), BF),
                ((all_rows, mine), BF),
                ((all_rows, mine), BF),
                ((all_rows, head), F32),
                ((all_rows, head), F32),
                ((all_rows, rows), F32),
                ((16, width), F32),
            ],
            [
                pltpu.VMEM((n, 16, mine), BF),
                pltpu.VMEM((all_rows, width), F32),
                pltpu.SemaphoreType.DMA((7 * n,)),
            ],
            "sv" + "v" * 5 + "h" * (2 * n),
            (place, frequencies, *token_pieces, *first_pieces, *first_far),
        )

        low, high = 3 * hd, 3 * hd + blocks * hs
        out_here = jnp.stack([v[low:high] for v in first_pieces])
        out_there = jnp.stack([v[low:high] for v in first_far])

        def out_part_for(r):
            picked = [
                ordered(*(lax.dynamic_index_in_dim(v, s, 0, keepdims=False) for v in (out_here, out_there)), 0)
                for s in [(z - (p ^ r) * (n // g) - j) % n for j in range(n // g)]
            ]
            return jnp.stack(picked)

        out_pieces = [out_part_for(0)] + [hop(out_part_for(r), r) for r in range(1, g)]
        if hs % 8 == 0:
            [my_out] = move(
                functools.partial(out_weight_kernel, n, g, hs, mine),
                [(mine, width)],
                n * 2 * blocks,
                (place, *out_pieces),
                "s" + "h" * g,
            )
        else:
            my_out = by_member(out_pieces).reshape(g, n // g, 2, blocks, hs, mine)
            my_out = my_out.transpose(1, 0, 2, 4, 3, 5).reshape(mine, width)
        attn_parts = call(
            functools.partial(project_kernel, rows),
            split_shapes(rows, width),
            (),
            "vv",
            (attended, my_out),
        )

        kept = (all_normed, my_qkv, my_out, queries, keys, values, attended, cosines, sines, bias)
        return kept, gains, attn_parts

    kept, gains, attn_parts = together(attention, token_pieces, first_pieces, own_far)
    even_part, *got = cut(even_part, *attn_parts, *second_odd.values())
    attn_parts, second_odd = got[:5], dict(zip(second_odd, got[5:]))
    second_even = {k: ring(even_part, k) for k in range(2, n, 2)}

    def attention_end(attn_parts, even_part, odd_parts):
        to_one, to_two, *waiting = attn_parts
        got_one, got_two, even_part, *odd_far = cut(
            hop(to_one, 1), hop(to_two, 2), even_part, *(core(v) for v in odd_parts)
        )
        reduced, own_far = cut(plane_reduce_rest(got_one, got_two, *waiting), core(even_part))
        middle = tokens.astype(F32) + reduced
        unit_second, inverse_second = unit(middle)
        normed_ffn = (unit_second * gains[8:9]).astype(BF)
        far_rows = pair(normed_ffn)
        own_pieces = plane_gather(normed_ffn)
        return middle, unit_second, inverse_second, own_pieces, gather_first(far_rows), own_far, odd_far

    middle, unit_second, inverse_second, own_pieces, far_pieces, own_far, odd_far = together(
        attention_end, attn_parts, even_part, list(second_odd.values())
    )
    all_normed, my_qkv, my_out, queries, keys, values, attended, cosines, sines, bias = kept
    gain_first, gain_second = gains[0:1], gains[8:9]
    residual = tokens.astype(F32)
    *got, all_grads = cut(*own_pieces, *far_pieces, *second_even.values(), all_grads)
    own_pieces, far_pieces, second_even = got[:5], got[5:8], dict(zip(second_even, got[8:]))
    odd_far = dict(zip(second_odd, odd_far))
    even_far = {k: core(v) for k, v in second_even.items()}
    second_here = {0: even_part, **second_odd, **second_even}
    second_far = {0: own_far, **odd_far, **even_far}
    second_here = [second_here[k] for k in range(n)]
    second_far = [second_far[k] for k in range(n)]

    index = jnp.arange(2 * span, dtype=jnp.int32) % span
    unit_index = (index // strip) * (strip * shares) + share * strip + index % strip
    fast_units = strip % 16 == 0

    def feed_forward(e, row_pieces):
        if fast_units:
            shapes = split_shapes(rows, width) * 2
            shapes += [((all_rows, width), BF)] * 2
            shapes += [((all_rows, 2 * span), BF), ((all_rows, 4 * span), BF)]
            got = call(
                functools.partial(feed_forward_kernel, n, g, depth, strip, rows, e),
                shapes,
                [pltpu.VMEM(*v) for v in shapes]
                + [
                    pltpu.VMEM((width, 2 * span), BF),
                    pltpu.VMEM((width, 2 * span), BF),
                    pltpu.VMEM((2 * span, width), BF),
                    pltpu.VMEM((g, 16, rows), BF),
                    pltpu.SemaphoreType.DMA((5 + 2 * n * (2 + cuts) + 2 * g,)),
                    pltpu.SemaphoreType.DMA((14,)),
                ],
                "sv" + "h" * (6 + 2 * n),
                (
                    place,
                    jnp.broadcast_to(unit_index.astype(F32), (8, 2 * span)),
                    *row_pieces,
                    all_grads,
                    *second_here,
                    *second_far,
                ),
                out="h",
                spare=16,
            )
            return got[:5], got[5:10], got[10:]
        group_rows = jnp.concatenate(row_pieces, axis=0)
        stacks = []
        for pieces in (second_here, second_far):
            out = jnp.zeros((n, *pieces[0].shape), BF)
            for k in range(n):
                out = lax.dynamic_update_index_in_dim(out, pieces[k], (z - k) % n, 0)
            stacks.append(out)
        gate_matrix, up_matrix = (
            jnp.concatenate(
                [v[:, k * depth : (k + 1) * depth].reshape(width, span) for v in stacks], axis=1
            )
            for k in (0, 1)
        )
        down_matrix = jnp.concatenate(
            [v[:, 2 * depth :].reshape(n, cuts, strip, span).transpose(0, 2, 1, 3) for v in stacks],
            axis=0,
        ).reshape(2 * span, width)
        grad_got = jnp.stack(
            [lax.dynamic_index_in_dim(all_grads, p ^ r, 0, keepdims=False)[e] for r in range(g)]
        )
        group_grads = grad_got[:, :rows].reshape(all_rows, width)
        group_codes = grad_got[:, rows, :rows].reshape(all_rows, 1).astype(jnp.int32)
        group_limits = jnp.where(
            group_codes < 0, 0, jnp.right_shift(jnp.int32(units), jnp.minimum(3 - group_codes, 3))
        )
        live = unit_index[None, :] < group_limits
        gate_pre = dot(group_rows, gate_matrix)
        lifted = dot(group_rows, up_matrix)
        sigmoid_gate = jax.nn.sigmoid(gate_pre)
        activated = gate_pre * sigmoid_gate
        hidden = jnp.where(live, (activated * lifted).astype(BF), jnp.zeros((), BF))
        grad_hidden = jnp.where(live, contract_cols(group_grads, down_matrix), 0.0)
        grad_gate = (
            grad_hidden * lifted * sigmoid_gate * (1.0 + gate_pre * (1.0 - sigmoid_gate))
        ).astype(BF)
        grad_lifted = (grad_hidden * activated).astype(BF)
        partial_input = (
            contract_cols(grad_gate, gate_matrix) + contract_cols(grad_lifted, up_matrix)
        ).astype(BF)
        partial_ffn = dot(hidden, down_matrix).astype(BF)
        return (
            list(split_rows(partial_input.reshape(g, rows, width))),
            list(split_rows(partial_ffn.reshape(g, rows, width))),
            [group_rows, group_grads, hidden, jnp.concatenate([grad_gate, grad_lifted], axis=1)],
        )

    def unit_grads(own, far):
        if fast_units:
            return call(
                functools.partial(unit_sums_kernel, n, depth, strip),
                [((n, 2 * depth + cuts * strip, span), BF)] * 2,
                (),
                "v" * 8,
                (*own, *far),
            )
        group_rows, group_grads, hidden, grads_two = (
            jnp.concatenate([v, w], axis=0) for v, w in zip(own, far)
        )

        def half_grads(half):
            low = slice(half * span, (half + 1) * span)
            made = contract_rows(hidden[:, low], group_grads).astype(BF)
            made = made.reshape(n, strip, cuts, span).transpose(0, 2, 1, 3)
            return jnp.concatenate(
                [
                    contract_rows(group_rows, v[:, low]).astype(BF).reshape(n, depth, span)
                    for v in (grads_two[:, : 2 * span], grads_two[:, 2 * span :])
                ]
                + [made.reshape(n, cuts * strip, span)],
                axis=1,
            )

        return [half_grads(0), half_grads(1)]

    far_pieces = gather_rest(list(far_pieces))
    own_out = together(functools.partial(feed_forward, 0), own_pieces)
    (own_input, own_ffn, own_saved), far_pieces = cut(own_out, far_pieces)
    to_one, to_two, *own_waiting = own_input
    own_got, (far_input, far_ffn, far_saved) = cut(
        (hop(to_one, 1), hop(to_two, 2)), together(functools.partial(feed_forward, 1), far_pieces)
    )
    to_one, to_two, *far_waiting = far_input
    own_half, far_got, (sums_here, sums_there) = cut(
        plane_reduce_rest(*own_got, *own_waiting),
        (hop(to_one, 1), hop(to_two, 2)),
        together(unit_grads, own_saved, far_saved),
    )
    far_sum, far_sums = cut(plane_reduce_rest(*far_got, *far_waiting), core(sums_there))

    def unit_sums(k):
        here, there = (
            lax.dynamic_index_in_dim(v, k, 0, keepdims=False).astype(F32)
            for v in (sums_here, far_sums)
        )
        return (here + there).astype(BF)

    def mixed(own, far):
        half = own.shape[0] // 2
        return jnp.concatenate([own[:half], far[:half], own[half:], far[half:]], axis=0)

    far_half = pair(far_sum.astype(BF))
    to_one, to_two, branch_own = (mixed(v, w) for v, w in zip(own_ffn[:3], far_ffn[:3]))
    branch_waiting = [branch_own] + [
        jnp.concatenate([v, w], axis=0) for v, w in zip(own_ffn[3:], far_ffn[3:])
    ]
    to_one, to_two = cut(to_one, to_two, far_sum)[:2]
    branch_got = hop(to_one, 1), hop(to_two, 2)
    messages = [unit_sums((z + k) % n) for k in range(n)]
    far_half, branch_got, *messages = cut(far_half, branch_got, *messages)
    sums = [messages[0].astype(F32), 0.0]
    moved = [ring(messages[k], k) for k in range(1, n)]

    def my_half(x, which, axis):
        return lax.dynamic_index_in_dim(x, which, axis, keepdims=False)

    def for_member(stacked, r, axis):
        return lax.dynamic_index_in_dim(stacked, p ^ r, axis, keepdims=False)

    def attention_back(own_half, far_half, branch_got):
        grad_normed_ffn = (own_half + far_half.astype(F32)).astype(BF).astype(F32)
        grad_middle = out_cotangent.astype(F32) + norm_back(
            grad_normed_ffn, unit_second, inverse_second, gain_second
        )
        branch_pieces = plane_gather(grad_middle.astype(BF))
        fast = n == g and hs % 16 == 0
        if fast:
            branch_rows = jnp.concatenate(branch_pieces, axis=0)
            out_here, out_there = call(
                functools.partial(out_sums_kernel, g, hs, mine),
                [((g, blocks * hs, mine), BF)] * 2,
                [pltpu.VMEM((mine, mine), F32)],
                "svv",
                (place, attended, branch_rows),
            )
            out_there, *branch_pieces = cut(core(out_there), *branch_pieces)
            out_sum = (out_here.astype(F32) + out_there.astype(F32)).astype(BF)
        got_one, got_two, *branch_pieces = cut(*branch_got, *branch_pieces)
        branch_sum = plane_reduce_rest(got_one, got_two, *branch_waiting)
        branch_sum = branch_sum.reshape(2, 2, rows // 2, width).transpose(1, 0, 2, 3)
        branch_sum = branch_sum.reshape(2 * rows, width)
        grad_branch, grad_packed, *normed_parts = call(
            functools.partial(attend_back_kernel, rows, mine, head),
            [((all_rows, width), BF), ((all_rows, 3 * mine), BF), *split_shapes(rows, width)],
            [pltpu.VMEM((all_rows, mine), BF)],
            "v" * 13,
            (*branch_pieces, my_out, my_qkv, queries, keys, values, cosines, sines, bias),
        )
        branch_sum, grad_packed = cut(branch_sum, grad_packed)
        if fast:
            quarters = [hop(for_member(after(out_sum, grad_packed), r, 0), r) for r in (1, 2)]
            sum_here, sum_there = call(
                functools.partial(weight_sums_kernel, g, depth, mine),
                [((g, 3 * hd, mine), BF)] * 2,
                [pltpu.VMEM((depth, 3 * mine), F32)],
                "svv",
                (place, all_normed, grad_packed),
            )
            sum_there, out_sum, *quarters = cut(sum_there, out_sum, *quarters)
            quarters.append(hop(for_member(out_sum, 3, 0), 3))
            weight_sum = (sum_here.astype(F32) + core(sum_there).astype(F32)).astype(BF)
            last_parts = call(
                functools.partial(last_parts_kernel, g, 3 * hd),
                [((3 * hd + blocks * hs, mine), BF)] * g,
                [pltpu.VMEM((g, blocks * hs, mine), BF)],
                "s" + "v" * (g + 1),
                (place, weight_sum, for_member(out_sum, 0, 0), *quarters),
            )
        else:
            out_grad = contract_rows(attended, grad_branch).astype(BF)
            out_grad = out_grad.reshape(n // g, g, 2, hs, width)
            out_sum = my_half(out_grad, c, 2).astype(F32)
            out_sum = (out_sum + core(my_half(out_grad, 1 - c, 2)).astype(F32)).astype(BF)
            out_sum = by_member(
                [for_member(out_sum, 0, 1)]
                + [hop(for_member(out_sum, r, 1), r) for r in range(1, g)]
            ).reshape(n, hs, blocks, mine)
            qkv_grad = contract_rows(all_normed, grad_packed).astype(BF).reshape(n, 2, hd, 3, mine)
            qkv_sum = my_half(qkv_grad, c, 1).astype(F32)
            qkv_sum += core(my_half(qkv_grad, 1 - c, 1)).astype(F32)
            last_part = jnp.concatenate(
                [
                    qkv_sum.astype(BF).transpose(0, 2, 1, 3).reshape(n, 3 * hd, mine),
                    out_sum.transpose(0, 2, 1, 3).reshape(n, blocks * hs, mine),
                ],
                axis=1,
            )
            last_parts = [
                lax.dynamic_index_in_dim(last_part, (z + k) % n, 0, keepdims=False) for k in range(n)
            ]
        normed_parts = cut(*normed_parts, *last_parts)[:5]
        grad_normed = plane_reduce(*normed_parts)
        unit_first, inverse_first = unit(residual)
        input_grad = (
            grad_middle + norm_back(grad_normed, unit_first, inverse_first, gain_first)
        ).astype(BF)
        return input_grad, last_parts, branch_sum

    input_grad, last_parts, branch_sum = together(
        attention_back, own_half, far_half, branch_got
    )
    cut_values = cut(*moved, *last_parts)
    moved, last_parts = cut_values[: n - 1], cut_values[n - 1 :]
    for k in range(1, n):
        sums[k % 2] += moved[k - 1].astype(F32)
    even_sum, odd_sum = (v.astype(BF) for v in sums)
    last_moved = [ring(last_parts[k], k) for k in range(1, n)]

    def units_out(even_sum, odd_sum):
        return plane_gather(jnp.concatenate([even_sum, odd_sum], axis=0))

    unit_pieces = together(units_out, even_sum, odd_sum)
    got = cut(*unit_pieces, *last_moved)
    unit_pieces, last_moved = got[:5], got[5:]
    last_sum = last_parts[0].astype(F32) + sum(v.astype(F32) for v in last_moved)
    last_one = gather_first(last_sum.astype(BF))
    if strip % 32 == 0:
        share_gate, share_up, share_down, ffn_part = call(
            functools.partial(unit_results_kernel, n, g, depth, strip),
            [
                ((depth * units // 128, 128), F32),
                ((depth * units // 128, 128), F32),
                ((units // n * width // 128, 128), F32),
                ((depth, 1), F32),
            ],
            [
                pltpu.VMEM((shares, 2 * depth + cuts * strip, span), BF),
                pltpu.SemaphoreType.DMA((3, shares)),
            ],
            "s" + "h" * 5 + "vv",
            (place, *unit_pieces, w_gate[:, 0], w_up[:, 0]),
        )
        ffn_part = ffn_part[:, 0]
    else:
        got = as_members(unit_pieces).reshape(g, 2, -1, span)
        all_units = jnp.zeros((shares, *got.shape[2:]), BF)
        for r in range(g):
            for odd in (0, 1):
                all_units = lax.dynamic_update_index_in_dim(
                    all_units, got[r, odd], (p ^ r) * 2 + (z % 2) ^ odd, 0
                )

        def columns_back(pieces):
            return (
                pieces.reshape(shares, depth, n, strip)
                .transpose(1, 2, 0, 3)
                .reshape(depth, units)
                .astype(F32)
            )

        share_gate = columns_back(all_units[:, :depth])
        share_up = columns_back(all_units[:, depth : 2 * depth])
        share_down = (
            all_units[:, 2 * depth :]
            .reshape(shares, cuts, strip, span)
            .transpose(0, 2, 1, 3)
            .reshape(units // n, width)
            .astype(F32)
        )
        ffn_part = jnp.sum(
            share_gate * w_gate[:, 0].astype(F32) + share_up * w_up[:, 0].astype(F32), axis=1
        )
    *last_one, ffn_part = cut(*last_one, ffn_part)
    last_pieces = gather_rest(last_one)
    share_gain_ffn = (ffn_part + core(ffn_part)) / gain_ffn.astype(F32)
    branch_ffn = branch_sum[:rows] + pair(branch_sum[rows:].astype(BF)).astype(F32)
    outputs = (middle + branch_ffn.astype(BF).astype(F32)).astype(BF)
    if hs % 16 == 0:
        share_qkv, share_out, attn_part = call(
            functools.partial(attention_results_kernel, g, depth, mine),
            [((depth, 3 * width), F32), ((depth, width), F32), ((depth, 1), F32)],
            [
                pltpu.VMEM((depth, 3 * width), BF),
                pltpu.VMEM((depth, width), BF),
                pltpu.SemaphoreType.DMA((2 * (g + 1) * (3 + blocks),)),
            ],
            "s" + "h" * 10 + "v",
            (place, *last_pieces, *(core(v) for v in last_pieces), w_qkv),
        )
        attn_part = attn_part[:, 0]
    else:
        last_got = as_members(last_pieces)
        last_got = by_member([last_got[r] for r in range(g)])
        last_both = ordered(last_got, core(last_got), 0)
        share_qkv = (
            last_both[:, :, : 3 * hd]
            .reshape(2, g, 3, hd, mine)
            .transpose(0, 3, 2, 1, 4)
            .reshape(depth, 3 * width)
            .astype(F32)
        )
        share_out = (
            last_both[:, :, 3 * hd :]
            .reshape(2, g, blocks, hs, mine)
            .transpose(1, 0, 3, 2, 4)
            .reshape(depth, width)
            .astype(F32)
        )
        attn_part = jnp.sum(share_qkv * w_qkv.astype(F32), axis=1)
    share_gain_attn = attn_part / gain_attn.astype(F32)
    return (
        outputs,
        input_grad,
        share_qkv,
        share_out,
        share_gain_attn,
        share_gain_ffn,
        share_gate.reshape(depth, 1, units),
        share_up.reshape(depth, 1, units),
        share_down.reshape(units // n, 1, width),
    )


def solution(mesh):
    in_specs = (
        P(("batch", "gran", "ffn"), None),
        P(("batch", "gran", "ffn")),
        P(("batch", "gran", "ffn")),
        P("batch", None),
        P("batch", None),
        P("batch"),
        P("batch"),
        P("batch", "ffn", None),
        P("batch", "ffn", None),
        P("batch", "ffn", None),
        P(("batch", "gran", "ffn"), None),
    )
    out_specs = (
        P(("batch", "gran", "ffn"), None),
        P(("batch", "gran", "ffn"), None),
        P("batch", None),
        P("batch", None),
        P("batch"),
        P("batch"),
        P("batch", "ffn", None),
        P("batch", "ffn", None),
        P("batch", "ffn", None),
    )
    return jax.shard_map(local, mesh=mesh, in_specs=in_specs, out_specs=out_specs, check_vma=False)
```

```python
import functools
import math

import jax
import jax.numpy as jnp
from jax import lax
from jax.experimental import pallas as pl
from jax.experimental.pallas import tpu as pltpu
from jax.sharding import PartitionSpec as P

H = 12


EPSILON = 1e-06
NEG_FILL = -1e30
ROPE_BASE = 10000.0
BF = jnp.bfloat16
F32 = jnp.float32


def row_groups(seq_rows, seq_groups, kept_rows):
    labels = jnp.arange(seq_groups.shape[0], dtype=jnp.int32)
    member = (seq_rows[:, None] == labels[None, :]).astype(jnp.int32)
    group_id = jnp.sum(member * seq_groups[None, :], axis=1)
    index = jnp.arange(seq_rows.shape[0], dtype=jnp.int32)
    earlier = (group_id[None, :] == group_id[:, None]) & (index[None, :] < index[:, None])
    rank = jnp.sum(earlier.astype(jnp.int32), axis=1)
    return jnp.where(rank < kept_rows, group_id, -1)


def dot(left, right):
    return jnp.dot(left, right, preferred_element_type=F32)


def contract_rows(left, right):
    return lax.dot_general(left, right, (((0,), (0,)), ((), ())), preferred_element_type=F32)


def contract_cols(left, right):
    return lax.dot_general(left, right, (((1,), (1,)), ((), ())), preferred_element_type=F32)


def norm_back(grad_normed, unit_rows, inverse_rms, gain):
    scaled = grad_normed * gain
    return inverse_rms * (scaled - unit_rows * jnp.mean(scaled * unit_rows, axis=-1, keepdims=True))


def first_rows(values, count, width):
    return jnp.pad(values.astype(BF)[None, :], ((0, count - 1), (0, width - values.shape[0])))


def after(value, *others):
    return lax.optimization_barrier((value, *others))[0]


def small_cost():
    return pl.CostEstimate(flops=1, bytes_accessed=1, transcendentals=0)


def call(kernel, outs, scratch=(), ins=(), operands=(), out="v", spare=8):
    held = [v for k, v in zip(ins, operands) if k == "v"]
    held += [jax.ShapeDtypeStruct(*v) for v in outs if out == "v"]
    held += [v for v in scratch if v.dtype in (BF, F32)]
    limit = sum(math.prod(v.shape) * v.dtype.itemsize for v in held) + spare * 2**20
    kinds = {
        "v": pl.BlockSpec(memory_space=pltpu.VMEM),
        "h": pl.BlockSpec(memory_space=pl.ANY),
        "s": pl.BlockSpec(memory_space=pltpu.SMEM),
    }
    return pl.pallas_call(
        kernel,
        out_shape=[jax.ShapeDtypeStruct(shape, dtype) for shape, dtype in outs],
        in_specs=[kinds[k] for k in ins],
        out_specs=[kinds[out]] * len(outs),
        scratch_shapes=list(scratch),
        compiler_params=pltpu.CompilerParams(vmem_limit_bytes=limit),
        cost_estimate=small_cost(),
    )(*operands)


def split_parts(value, rows, to_one, to_two, own, two_low, one_high):
    half = rows // 2
    to_one[:half] = value[rows : rows + half].astype(BF)
    to_one[half:] = value[3 * rows : 3 * rows + half].astype(BF)
    to_two[:half] = value[2 * rows + half : 3 * rows].astype(BF)
    to_two[half:] = value[3 * rows + half :].astype(BF)
    own[...] = value[:rows]
    two_low[...] = value[2 * rows : 2 * rows + half].astype(BF)
    one_high[...] = value[rows + half : 2 * rows].astype(BF)


def split_shapes(rows, width):
    half = rows // 2
    return [
        ((rows, width), BF),
        ((rows, width), BF),
        ((rows, width), F32),
        ((half, width), BF),
        ((half, width), BF),
    ]


def reduce_first_kernel(got_one, got_two, own, two_low, one_high, to_two, to_one, total):
    half = two_low.shape[0]
    to_two[...] = (two_low[...].astype(F32) + got_one[half:].astype(F32)).astype(BF)
    to_one[...] = (one_high[...].astype(F32) + got_two[half:].astype(F32)).astype(BF)
    total[:half] = own[:half].astype(F32) + got_one[:half].astype(F32)
    total[half:] = own[half:].astype(F32) + got_two[:half].astype(F32)


def attend_kernel(n, rows, depth, mine, head, place, freq, *refs):
    tokens, refs = refs[:5], refs[5:]
    here, there, refs = refs[:n], refs[n : 2 * n], refs[2 * n :]
    normed, weight, queries, keys, values, attended, cosines, sines, bias, gains = refs[:10]
    gain_rows, unit_rows, sems = refs[10:]
    z, c = place[0], place[2]
    hd = depth // 2
    width = n * depth
    copies = []
    for s in range(n):
        plane = lax.rem(z - s + n, n)
        for which, pieces in ((c, here), (1 - c, there)):
            start = pl.multiple_of(plane * depth + which * hd, 8)
            for k in range(3):
                copies.append(
                    pltpu.make_async_copy(
                        pieces[s].at[pl.ds(k * hd, hd), :],
                        weight.at[pl.ds(start, hd), pl.ds(k * mine, mine)],
                        sems.at[len(copies)],
                    )
                )
        copies.append(
            pltpu.make_async_copy(
                here[s].at[pl.ds(here[s].shape[0] - 16, 16), :], gain_rows.at[plane], sems.at[len(copies)]
            )
        )
    for copy in copies:
        copy.start()

    half = rows // 2
    third = tokens[3].shape[0]
    spans = [(tokens[0], 0, 0, rows), (tokens[1], 0, rows, rows), (tokens[2], 0, 2 * rows, rows)]
    spans += [(tokens[3], 0, 3 * rows, third), (tokens[4], 0, 3 * rows + third, rows - third)]
    for ref, low, at, count in spans:
        x = ref[low : low + count, :].astype(F32)
        inverse = lax.rsqrt(jnp.mean(x * x, axis=-1, keepdims=True) + EPSILON)
        unit_rows[at : at + count] = x * inverse

    row = lax.broadcasted_iota(jnp.int32, (rows, rows), 0)
    col = lax.broadcasted_iota(jnp.int32, (rows, rows), 1)
    lane = lax.broadcasted_iota(jnp.int32, (rows, head), 1)
    sign = jnp.where(lane < head // 2, -1.0, 1.0)
    for b in range(4):
        ref, low = (tokens[b], rows) if b < 3 else (tokens[4], rows - third)
        ids = ref[low : low + 8, :rows].astype(F32)[:1]
        ids_row = jnp.broadcast_to(ids, (rows, rows))
        ids_col = jnp.sum(jnp.where(row == col, ids_row, 0.0), axis=1, keepdims=True)
        before = jnp.sum(jnp.where(ids_row < ids_col, 1.0, 0.0), axis=1, keepdims=True)
        positions = row[:, :1].astype(F32) - before
        angles = positions * freq[:1, :]
        cosines[b * rows : (b + 1) * rows] = jnp.cos(angles)
        sines[b * rows : (b + 1) * rows] = jnp.sin(angles) * sign
        bias[b * rows : (b + 1) * rows] = jnp.where(
            (ids_row == ids_col) & (row >= col), 0.0, NEG_FILL
        )

    for copy in copies:
        copy.wait()
    for k in range(n):
        block = slice(k * depth, (k + 1) * depth)
        both = gain_rows[k].astype(F32)
        gains[0:8, block] = jnp.broadcast_to(both[0:1, :depth], (8, depth))
        gains[8:16, block] = jnp.broadcast_to(both[8:9, :depth], (8, depth))
    normed[...] = (unit_rows[...] * gains[0:1, :]).astype(BF)
    x = normed[...]
    cos, sin = cosines[...], sines[...]
    scale = 1.0 / math.sqrt(head)
    for k, out in enumerate((queries, keys, values)):
        packed = dot(x, weight[:, k * mine : (k + 1) * mine])
        for h in range(mine // head):
            part = packed[:, h * head : (h + 1) * head]
            if k < 2:
                part = part * cos + pltpu.roll(part, head // 2, 1) * sin
            if k == 0:
                part = part * scale
            out[:, h * head : (h + 1) * head] = part.astype(BF)
    for b in range(4):
        for h in range(mine // head):
            here_rows, here_cols = slice(b * rows, (b + 1) * rows), slice(h * head, (h + 1) * head)
            scores = contract_cols(queries[here_rows, here_cols], keys[here_rows, here_cols])
            probs = softmax(scores + bias[here_rows])
            attended[here_rows, here_cols] = dot(
                probs.astype(BF), values[here_rows, here_cols]
            ).astype(BF)


def softmax(scores):
    exponent = jnp.exp(scores - jnp.max(scores, axis=-1, keepdims=True))
    return exponent / jnp.sum(exponent, axis=-1, keepdims=True)


def project_kernel(rows, attended, out, *parts):
    split_parts(dot(attended[...], out[...]), rows, *parts)


def attend_back_kernel(rows, mine, head, *refs):
    grads, refs = refs[:5], refs[5:]
    out, weight, queries, keys, values, cosines, sines, bias = refs[:8]
    branch, packed, *parts = refs[8:-1]
    attended_grad = refs[-1]
    third = grads[3].shape[0]
    at = 0
    for ref in grads:
        branch[at : at + ref.shape[0]] = ref[...]
        at += ref.shape[0]
    del third
    attended_grad[...] = contract_cols(branch[...], out[...]).astype(BF)
    scale = 1.0 / math.sqrt(head)
    for b in range(4):
        r = slice(b * rows, (b + 1) * rows)
        cos, sin = cosines[r], sines[r]
        for h in range(mine // head):
            cols = slice(h * head, (h + 1) * head)
            q, k, v, grad = queries[r, cols], keys[r, cols], values[r, cols], attended_grad[r, cols]
            probs = softmax(contract_cols(q, k) + bias[r])
            grad_probs = contract_cols(grad, v)
            grad_scores = probs * (
                grad_probs - jnp.sum(probs * grad_probs, axis=-1, keepdims=True)
            )
            grad_scores = grad_scores.astype(BF)
            grad_q = dot(grad_scores, k).astype(BF).astype(F32) * scale
            grad_k = contract_rows(grad_scores, q).astype(BF).astype(F32)
            grad_v = contract_rows(probs.astype(BF), grad)
            for j, part in enumerate((grad_q, grad_k, grad_v)):
                if j < 2:
                    part = part * cos - pltpu.roll(part, head // 2, 1) * sin
                packed[r, j * mine + h * head : j * mine + (h + 1) * head] = part.astype(BF)
    split_parts(contract_cols(packed[...], weight[...]), rows, *parts)


def first_part_kernel(depth, mine, members, place, w_qkv, w_out, gains, out, sems):
    p, c = place[1], place[2]
    hd, hs = depth // 2, depth // members // 2
    width = w_out.shape[1]
    moves = []
    for k in range(3):
        column = pl.multiple_of(k * width + p * mine, 128)
        moves.append((w_qkv.at[pl.ds(c * hd, hd), pl.ds(column, mine)], k * hd, hd))
    top = pl.multiple_of((p * 2 + c) * hs, 8)
    for k in range(width // mine):
        block = w_out.at[pl.ds(top, hs), pl.ds(k * mine, mine)]
        moves.append((block, 3 * hd + k * hs, hs))
    moves.append((gains, out.shape[0] - 16, 16))
    copies = [
        pltpu.make_async_copy(source, out.at[pl.ds(at, count), :], sems.at[i])
        for i, (source, at, count) in enumerate(moves)
    ]
    for copy in copies:
        copy.start()
    for copy in copies:
        copy.wait()


def out_weight_kernel(n, members, hs, mine, place, *refs):
    pieces, out, sems = refs[:members], refs[members], refs[members + 1]
    p = place[1]
    copies = []
    for r in range(members):
        for j in range(n // members):
            for half in range(2):
                top = pl.multiple_of(((j * members + (p ^ r)) * 2 + half) * hs, 8)
                for k in range(out.shape[1] // mine):
                    copies.append(
                        pltpu.make_async_copy(
                            pieces[r].at[j, half, pl.ds(k * hs, hs), :],
                            out.at[pl.ds(top, hs), pl.ds(k * mine, mine)],
                            sems.at[len(copies)],
                        )
                    )
    for copy in copies:
        copy.start()
    for copy in copies:
        copy.wait()


def strips_of(tile, strip):
    at, out = 0, []
    while at < 128:
        share, first = divmod(tile * 128 + at, strip)
        count = min(strip - first, 128 - at)
        out.append((share, first, at, count))
        at += count
    return out


def fetch_shares(members, rows, low, count, place, pieces, target, sems):
    z, p = place[0], place[1]
    copies = []
    for r in range(members):
        for odd in range(2):
            share = (p ^ r) * 2 + (lax.rem(z, 2) ^ odd)
            ref, top = (pieces[r], odd * rows + low) if r < 3 else (pieces[3 + odd], low)
            copy = pltpu.make_async_copy(
                ref.at[pl.ds(top, count), :], target.at[share], sems.at[len(copies)]
            )
            copy.start()
            copies.append(copy)
    return copies


def columns_results_kernel(n, members, depth, strip, rows, place, *refs):
    pieces, w_gate, w_up = refs[:5], refs[5], refs[6]
    gate, up, gain, held_gate, held_up, sems = refs[7:]
    shares = 2 * members
    copies = [
        fetch_shares(members, rows, k * depth, depth, place, pieces, held, sems.at[k])
        for k, held in enumerate((held_gate, held_up))
    ]
    lanes = lax.broadcasted_iota(jnp.int32, (depth, 128), 1)
    row_tiles = n * shares * strip // 128
    total = jnp.zeros((depth, 128), F32)
    for which, (out, held, weight) in enumerate(
        ((gate, held_gate, w_gate), (up, held_up, w_up))
    ):
        for copy in copies[which]:
            copy.wait()
        for k in range(n):
            for tile in range(shares * strip // 128):
                made = jnp.zeros((depth, 128), F32)
                for share, first, lane, count in strips_of(tile, strip):
                    column = k * strip + first
                    while count > 0:
                        source, offset = divmod(column, 128)
                        some = min(count, 128 - offset)
                        value = held[share, :, source * 128 : (source + 1) * 128].astype(F32)
                        if lane != offset:
                            value = pltpu.roll(value, (lane - offset) % 128, 1)
                        made = jnp.where((lanes >= lane) & (lanes < lane + some), value, made)
                        column, lane, count = column + some, lane + some, count - some
                at = k * (shares * strip // 128) + tile
                out[pl.ds(at, depth, stride=row_tiles), :] = made
                total += made * weight[:, at * 128 : (at + 1) * 128].astype(F32)
    gain[...] = jnp.sum(total, axis=1, keepdims=True)


def rows_results_kernel(n, members, depth, strip, rows, place, *refs):
    pieces, down, held, sems = refs[:5], refs[5], refs[6], refs[7]
    span, cuts = n * strip, (rows - 2 * depth) // strip
    copies = fetch_shares(members, rows, 2 * depth, cuts * strip, place, pieces, held, sems)
    for copy in copies:
        copy.wait()
    wide = cuts * span // 128
    for share in range(2 * members):
        for k in range(cuts):
            for tile in range(span // 128):
                block = slice(k * strip, (k + 1) * strip), slice(tile * 128, (tile + 1) * 128)
                start = share * strip * wide + k * (span // 128) + tile
                down[pl.ds(start, strip, stride=wide), :] = held[(share, *block)].astype(F32)


def attention_results_kernel(members, depth, mine, place, *refs):
    here, there, w_qkv = refs[:5], refs[5:10], refs[10]
    qkv, out, gain, held, held_out, sems = refs[11:]
    p, c = place[1], place[2]
    hd, hs = depth // 2, depth // members // 2
    width = held_out.shape[1]
    blocks = width // mine
    copies = []

    def add(source, target):
        copies.append(pltpu.make_async_copy(source, target, sems.at[len(copies)]))

    def place_rows(ref, first, low, count, r, half):
        for k in range(3):
            top, end = max(low, k * hd), min(low + count, (k + 1) * hd)
            if top < end:
                add(
                    ref.at[pl.ds(first + top - low, end - top), :],
                    held.at[
                        pl.ds(pl.multiple_of(half * hd + top - k * hd, 8), end - top),
                        pl.ds(pl.multiple_of(k * width + (p ^ r) * mine, 128), mine),
                    ],
                )
        for k in range(blocks):
            base = 3 * hd + k * hs
            top, end = max(low, base), min(low + count, base + hs)
            if top < end:
                add(
                    ref.at[pl.ds(first + top - low, end - top), :],
                    held_out.at[
                        pl.ds(pl.multiple_of(((p ^ r) * 2 + half) * hs + top - base, 8), end - top),
                        pl.ds(k * mine, mine),
                    ],
                )

    rows = 3 * hd + blocks * hs
    for half, pieces in ((c, here), (1 - c, there)):
        for r in range(3):
            place_rows(pieces[r], 0, 0, rows, r, half)
        third = pieces[3].shape[0]
        place_rows(pieces[3], 0, 0, third, 3, half)
        place_rows(pieces[4], 0, third, rows - third, 3, half)
    for copy in copies:
        copy.start()
    for copy in copies:
        copy.wait()
    total = jnp.zeros((depth, 128), F32)
    for tile in range(3 * width // 128):
        cols = slice(tile * 128, (tile + 1) * 128)
        value = held[:, cols].astype(F32)
        qkv[:, cols] = value
        total += value * w_qkv[:, cols].astype(F32)
    gain[...] = jnp.sum(total, axis=1, keepdims=True)
    out[...] = held_out[...].astype(F32)


def out_sums_kernel(members, hs, mine, place, attended, branch, mine_out, theirs_out, held):
    c = place[2]
    for k in range(branch.shape[1] // mine):
        cols = slice(k * mine, (k + 1) * mine)
        held[...] = contract_rows(attended[...], branch[:, cols])
        for out, half in ((mine_out, c), (theirs_out, 1 - c)):
            for quarter in range(members):
                start = pl.multiple_of((quarter * 2 + half) * hs, 8)
                value = held[pl.ds(start, hs), :]
                out[quarter, k * hs : (k + 1) * hs, :] = value.astype(BF)


def weight_sums_kernel(members, depth, mine, place, normed, packed, mine_out, theirs_out, held):
    c = place[2]
    hd = depth // 2
    for plane in range(members):
        block = slice(plane * depth, (plane + 1) * depth)
        held[...] = contract_rows(normed[:, block], packed[...])
        for out, half in ((mine_out, c), (theirs_out, 1 - c)):
            start = pl.multiple_of(half * hd, 8)
            for k in range(3):
                value = held[pl.ds(start, hd), k * mine : (k + 1) * mine]
                out[plane, k * hd : (k + 1) * hd, :] = value.astype(BF)


def last_parts_kernel(members, low, place, *refs):
    sums, quarters, outs, held = refs[0], refs[1 : members + 1], refs[members + 1 : -1], refs[-1]
    z, p = place[0], place[1]
    for r in range(members):
        held[r] = quarters[r][...]
    for k in range(members):
        plane = lax.rem(z + k, members)
        outs[k][:low] = sums[plane]
        outs[k][low:] = held[p ^ plane]


def feed_forward_kernel(n, members, depth, strip, rows, e, place, unit_index, *refs):
    pieces, all_grads, refs = refs[:5], refs[5], refs[6:]
    here, there, refs = refs[:n], refs[n : 2 * n], refs[2 * n :]
    outs, scratch = refs[:14], refs[14:28]
    splits, (x, cot, hidden, grads_two) = scratch[:10], scratch[10:]
    gate, up, down, codes, in_sems, out_sems = refs[28:]
    z, p = place[0], place[1]
    span = n * strip
    units = span * 2 * members
    started, finishing = [], []

    def fetch(source, target):
        copy = pltpu.make_async_copy(source, target, in_sems.at[len(started)])
        copy.start()
        started.append(copy)

    def flush(index):
        copy = pltpu.make_async_copy(scratch[index], outs[index], out_sems.at[index])
        copy.start()
        finishing.append(copy)

    at = 0
    for ref in pieces:
        fetch(ref, x.at[pl.ds(at, ref.shape[0]), :])
        at += ref.shape[0]
    for s in range(n):
        plane = lax.rem(z - s + n, n)
        top = pl.multiple_of(plane * depth, 8)
        for half, parts in enumerate((here, there)):
            columns = pl.ds(half * span, span)
            fetch(parts[s].at[pl.ds(0, depth), :], gate.at[pl.ds(top, depth), columns])
            fetch(parts[s].at[pl.ds(depth, depth), :], up.at[pl.ds(top, depth), columns])
    first = len(started)
    for r in range(members):
        fetch(all_grads.at[p ^ r, e, pl.ds(0, rows), :], cot.at[pl.ds(r * rows, rows), :])
        fetch(all_grads.at[p ^ r, e, pl.ds(rows, 16), pl.ds(0, rows)], codes.at[r])
    for s in range(n):
        plane = lax.rem(z - s + n, n)
        for half, parts in enumerate((here, there)):
            start = pl.multiple_of(half * span + plane * strip, 8)
            for j in range(down.shape[1] // span):
                fetch(
                    parts[s].at[pl.ds(2 * depth + j * strip, strip), :],
                    down.at[pl.ds(start, strip), pl.ds(j * span, span)],
                )
    for copy in started[:first]:
        copy.wait()
    flush(10)
    row = lax.broadcasted_iota(jnp.int32, (rows, rows), 0)
    col = lax.broadcasted_iota(jnp.int32, (rows, rows), 1)

    gate_pre = dot(x[...], gate[...])
    lifted = dot(x[...], up[...])
    sigmoid = jax.nn.sigmoid(gate_pre)
    activated = gate_pre * sigmoid
    for copy in started[first:]:
        copy.wait()
    flush(11)
    limits = []
    for r in range(members):
        line = jnp.broadcast_to(codes[r].astype(F32)[:1], (rows, rows))
        code = jnp.sum(jnp.where(row == col, line, 0.0), axis=1, keepdims=True)
        limits.append(
            sum(jnp.where(code == k, float(units >> (members - 1 - k)), 0.0) for k in range(members))
        )
    live = unit_index[:1, :] < jnp.concatenate(limits, axis=0)
    hidden[...] = jnp.where(live, activated * lifted, 0.0).astype(BF)
    grad_hidden = jnp.where(live, contract_cols(cot[...], down[...]), 0.0)
    wide = 2 * span
    grads_two[:, :wide] = (
        grad_hidden * lifted * sigmoid * (1.0 + gate_pre * (1.0 - sigmoid))
    ).astype(BF)
    grads_two[:, wide:] = (grad_hidden * activated).astype(BF)
    flush(12)
    flush(13)
    grads = contract_cols(grads_two[:, :wide], gate[...])
    grads += contract_cols(grads_two[:, wide:], up[...])
    split_parts(grads, rows, *splits[:5])
    for index in range(5):
        flush(index)
    split_parts(dot(hidden[...], down[...]), rows, *splits[5:])
    for index in range(5, 10):
        flush(index)
    for copy in finishing:
        copy.wait()


def unit_sums_kernel(n, depth, strip, *refs):
    given, outs, held = refs[:8], refs[8:10], refs[10:18]
    sums, in_sems, out_sems = refs[18:20], refs[20], refs[21]
    parts = held[:4], held[4:]
    span = n * strip
    fetched = [
        pltpu.make_async_copy(given[i], held[i], in_sems.at[i]) for i in (0, 3, 4, 7, 1, 2, 5, 6)
    ]
    for copy in fetched:
        copy.start()
    for copy in fetched[:4]:
        copy.wait()
    finishing = []

    def flush(half, plane, low, count):
        place = (plane, pl.ds(low, count), slice(None))
        copy = pltpu.make_async_copy(
            sums[half].at[place], outs[half].at[place], out_sems.at[len(finishing)]
        )
        copy.start()
        finishing.append(copy)

    for plane in range(n):
        block = slice(plane * depth, (plane + 1) * depth)
        made = sum(contract_rows(x[:, block], grads[...]) for x, _, _, grads in parts)
        for half in range(2):
            for k in range(2):
                low = (2 * k + half) * span
                value = made[:, low : low + span].astype(BF)
                sums[half][plane, k * depth : (k + 1) * depth, :] = value
            flush(half, plane, 0, 2 * depth)
    for copy in fetched[4:]:
        copy.wait()
    cuts = held[1].shape[1] // span
    for j in range(cuts):
        cols = slice(j * span, (j + 1) * span)
        made = sum(contract_rows(hidden[...], cot[:, cols]) for _, cot, hidden, _ in parts)
        made = made.astype(BF)
        for half in range(2):
            for plane in range(n):
                low, at = half * span + plane * strip, 2 * depth + j * strip
                sums[half][plane, at : at + strip, :] = made[low : low + strip]
    for half in range(2):
        for plane in range(n):
            flush(half, plane, 2 * depth, cuts * strip)
    for copy in finishing:
        copy.wait()


def move(kernel, outs, copies, operands, ins):
    kinds = {"h": pl.BlockSpec(memory_space=pl.ANY), "s": pl.BlockSpec(memory_space=pltpu.SMEM)}
    return pl.pallas_call(
        kernel,
        out_shape=[jax.ShapeDtypeStruct(shape, BF) for shape in outs],
        in_specs=[kinds[k] for k in ins],
        out_specs=[pl.BlockSpec(memory_space=pltpu.VMEM)] * len(outs),
        scratch_shapes=[pltpu.SemaphoreType.DMA((copies,))],
        compiler_params=pltpu.CompilerParams(vmem_limit_bytes=56 * 2**20),
        cost_estimate=small_cost(),
    )(*operands)


def local(
    tokens,
    seq_ids,
    granularity,
    w_qkv,
    w_out,
    gain_attn,
    gain_ffn,
    w_gate,
    w_up,
    w_down,
    out_cotangent,
):
    n = lax.axis_size("batch")
    g = lax.axis_size("gran")
    z = lax.axis_index("batch")
    p = lax.axis_index("gran")
    c = lax.axis_index("ffn")
    rows, width = tokens.shape
    head = width // H
    heads = H // g
    mine = heads * head
    depth = w_qkv.shape[0]
    units = w_gate.shape[2]
    capacity = max(2, (5 * rows + 4 * n * g - 1) // (4 * n * g))

    def hop(x, r):
        return lax.ppermute(x, "gran", [(i, i ^ r) for i in range(g)])

    def pair(x):
        return lax.ppermute(x, "batch", [(i, i ^ 1) for i in range(n)])

    def core(x):
        return lax.ppermute(x, "ffn", [(0, 1), (1, 0)])

    def ring(x, s):
        return lax.ppermute(x, "batch", [(i, (i + s) % n) for i in range(n)])

    def gather_first(x):
        return [x, hop(x, 1), hop(x, 2)]

    def gather_rest(pieces):
        half = pieces[0].shape[0] // 32 * 16 or pieces[0].shape[0] // 2
        return [*pieces, hop(pieces[1][:half], 2), hop(pieces[2][half:], 1)]

    def plane_gather(x):
        return gather_rest(gather_first(x))

    def as_members(pieces):
        return jnp.concatenate(pieces, axis=0).reshape(g, *pieces[0].shape)

    def split_rows(x):
        half = x.shape[1] // 2
        return (
            jnp.concatenate([x[1, :half], x[3, :half]], axis=0),
            jnp.concatenate([x[2, half:], x[3, half:]], axis=0),
            x[0],
            x[2, :half],
            x[1, half:],
        )

    def plane_reduce(to_one, to_two, own, two_low, one_high):
        return summed(*plane_reduce_rest(hop(to_one, 1), hop(to_two, 2), own, two_low, one_high))

    def plane_reduce_rest(got_one, got_two, own, two_low, one_high):
        half, columns = two_low.shape
        two_low, one_high, total = call(
            reduce_first_kernel,
            [((half, columns), BF), ((half, columns), BF), ((2 * half, columns), F32)],
            (),
            "v" * 5,
            (got_one, got_two, own, two_low, one_high),
        )
        return total, hop(two_low, 2), hop(one_high, 1)

    def summed(total, low, high):
        return total + jnp.concatenate([low, high], axis=0).astype(F32)

    def by_member(pieces):
        out = jnp.zeros((g, *pieces[0].shape), pieces[0].dtype)
        for r in range(g):
            out = lax.dynamic_update_index_in_dim(out, pieces[r], p ^ r, 0)
        return out

    def ordered(here, there, axis):
        return jnp.stack(
            [jnp.where(c == 0, here, there), jnp.where(c == 0, there, here)], axis=axis
        )

    def cut(*values):
        return lax.optimization_barrier(values)

    def together(body, *operands):
        made = jax.eval_shape(body, *operands)
        return lax.cond(
            seq_ids[0] >= 0,
            body,
            lambda *given: jax.tree.map(lambda v: jnp.zeros(v.shape, v.dtype), made),
            *operands,
        )

    place = jnp.stack([z, p, c]).astype(jnp.int32)
    hd, sub = depth // 2, depth // g
    hs, blocks = sub // 2, width // mine
    gain_part = jnp.concatenate(
        [first_rows(gain_attn, 8, mine), first_rows(gain_ffn, 8, mine)], axis=0
    )
    token_part = jnp.concatenate([tokens, first_rows(seq_ids, 16, width)], axis=0)
    codes = row_groups(seq_ids, granularity, capacity * n)
    grad_part = jnp.concatenate([out_cotangent, first_rows(codes, 16, width)], axis=0)
    if hs % 8 == 0:
        [first_part] = move(
            functools.partial(first_part_kernel, depth, mine, g),
            [(3 * hd + blocks * hs + 16, mine)],
            blocks + 4,
            (place, w_qkv, w_out, gain_part),
            "shhh",
        )
    else:
        out_part = lax.dynamic_slice(w_out, ((p * 2 + c) * hs, 0), (hs, width))
        first_part = jnp.concatenate(
            [
                lax.dynamic_slice(w_qkv, (c * hd, k * width + p * mine), (hd, mine))
                for k in range(3)
            ]
            + [out_part[:, k * mine : (k + 1) * mine] for k in range(blocks)]
            + [gain_part],
            axis=0,
        )
    shares = 2 * g
    strip = units // n // shares
    share = p * 2 + z % 2
    span = n * strip
    cuts = width // span

    def columns(w, odd):
        return lax.dynamic_index_in_dim(
            w.reshape(depth, n, shares, strip), share ^ odd, 2, keepdims=False
        ).reshape(depth, span)

    def second_part(odd):
        rows_down = lax.dynamic_index_in_dim(
            w_down.reshape(shares, strip, width), share ^ odd, 0, keepdims=False
        )
        return jnp.concatenate(
            [columns(w_gate, odd), columns(w_up, odd)]
            + [rows_down[:, k * span : (k + 1) * span] for k in range(cuts)],
            axis=0,
        )

    first_moved = [ring(first_part, k) for k in range(1, n)]

    def rows_out(first_part, token_part, grad_part):
        token_pieces = plane_gather(token_part)
        first_part, grad_part, *token_pieces = cut(first_part, grad_part, *token_pieces)
        grad_both = jnp.stack([grad_part, pair(grad_part)])
        return token_pieces, core(first_part), grad_both, second_part(0), second_part(1)

    token_pieces, own_far, grad_both, even_part, odd_part = together(
        rows_out, first_part, token_part, grad_part
    )
    even_part, odd_part, own_far, grad_both, *first_moved = cut(
        even_part, odd_part, own_far, grad_both, *first_moved
    )
    all_grads = lax.all_gather(grad_both, "gran", axis=0)
    first_pieces = [first_part, *first_moved]
    second_odd = {k: ring(odd_part, k) for k in range(1, n, 2)}

    all_rows = g * rows

    def unit(values):
        inverse = lax.rsqrt(jnp.mean(values * values, axis=-1, keepdims=True) + EPSILON)
        return values * inverse, inverse

    def attention(token_pieces, first_pieces, own_far):
        first_far = [own_far, *(core(v) for v in first_pieces[1:])]
        frequencies = ROPE_BASE ** (-(2.0 * jnp.arange(head // 2, dtype=F32)) / head)
        frequencies = jnp.broadcast_to(jnp.concatenate([frequencies, frequencies]), (8, head))
        all_normed, my_qkv, queries, keys, values, attended, cosines, sines, bias, gains = call(
            functools.partial(attend_kernel, n, rows, depth, mine, head),
            [
                ((all_rows, width), BF),
                ((width, 3 * mine), BF),
                ((all_rows, mine), BF),
                ((all_rows, mine), BF),
                ((all_rows, mine), BF),
                ((all_rows, mine), BF),
                ((all_rows, head), F32),
                ((all_rows, head), F32),
                ((all_rows, rows), F32),
                ((16, width), F32),
            ],
            [
                pltpu.VMEM((n, 16, mine), BF),
                pltpu.VMEM((all_rows, width), F32),
                pltpu.SemaphoreType.DMA((7 * n,)),
            ],
            "sv" + "v" * 5 + "h" * (2 * n),
            (place, frequencies, *token_pieces, *first_pieces, *first_far),
        )

        low, high = 3 * hd, 3 * hd + blocks * hs
        out_here = jnp.stack([v[low:high] for v in first_pieces])
        out_there = jnp.stack([v[low:high] for v in first_far])

        def out_part_for(r):
            picked = [
                ordered(*(lax.dynamic_index_in_dim(v, s, 0, keepdims=False) for v in (out_here, out_there)), 0)
                for s in [(z - (p ^ r) * (n // g) - j) % n for j in range(n // g)]
            ]
            return jnp.stack(picked)

        out_pieces = [out_part_for(0)] + [hop(out_part_for(r), r) for r in range(1, g)]
        if hs % 8 == 0:
            [my_out] = move(
                functools.partial(out_weight_kernel, n, g, hs, mine),
                [(mine, width)],
                n * 2 * blocks,
                (place, *out_pieces),
                "s" + "h" * g,
            )
        else:
            my_out = by_member(out_pieces).reshape(g, n // g, 2, blocks, hs, mine)
            my_out = my_out.transpose(1, 0, 2, 4, 3, 5).reshape(mine, width)
        attn_parts = call(
            functools.partial(project_kernel, rows),
            split_shapes(rows, width),
            (),
            "vv",
            (attended, my_out),
        )

        kept = (all_normed, my_qkv, my_out, queries, keys, values, attended, cosines, sines, bias)
        return kept, gains, attn_parts

    kept, gains, attn_parts = together(attention, token_pieces, first_pieces, own_far)
    even_part, *got = cut(even_part, *attn_parts, *second_odd.values())
    attn_parts, second_odd = got[:5], dict(zip(second_odd, got[5:]))
    second_even = {k: ring(even_part, k) for k in range(2, n, 2)}

    def attention_end(attn_parts, even_part, odd_parts):
        to_one, to_two, *waiting = attn_parts
        got_one, got_two, even_part, *odd_far = cut(
            hop(to_one, 1), hop(to_two, 2), even_part, *(core(v) for v in odd_parts)
        )
        reduced, own_far = cut(plane_reduce_rest(got_one, got_two, *waiting), core(even_part))
        middle = tokens.astype(F32) + summed(*reduced)
        unit_second, inverse_second = unit(middle)
        normed_ffn = (unit_second * gains[8:9]).astype(BF)
        far_rows = pair(normed_ffn)
        own_pieces = plane_gather(normed_ffn)
        return middle, unit_second, inverse_second, own_pieces, gather_first(far_rows), own_far, odd_far

    middle, unit_second, inverse_second, own_pieces, far_pieces, own_far, odd_far = together(
        attention_end, attn_parts, even_part, list(second_odd.values())
    )
    all_normed, my_qkv, my_out, queries, keys, values, attended, cosines, sines, bias = kept
    gain_first, gain_second = gains[0:1], gains[8:9]
    residual = tokens.astype(F32)
    *got, all_grads = cut(*own_pieces, *far_pieces, *second_even.values(), all_grads)
    own_pieces, far_pieces, second_even = got[:5], got[5:8], dict(zip(second_even, got[8:]))
    odd_far = dict(zip(second_odd, odd_far))
    even_far = {k: core(v) for k, v in second_even.items()}
    second_here = {0: even_part, **second_odd, **second_even}
    second_far = {0: own_far, **odd_far, **even_far}
    second_here = [second_here[k] for k in range(n)]
    second_far = [second_far[k] for k in range(n)]

    index = jnp.arange(2 * span, dtype=jnp.int32) % span
    unit_index = (index // strip) * (strip * shares) + share * strip + index % strip
    fast_units = strip % 16 == 0

    def feed_forward(e, row_pieces):
        if fast_units:
            shapes = split_shapes(rows, width) * 2
            shapes += [((all_rows, width), BF)] * 2
            shapes += [((all_rows, 2 * span), BF), ((all_rows, 4 * span), BF)]
            got = call(
                functools.partial(feed_forward_kernel, n, g, depth, strip, rows, e),
                shapes,
                [pltpu.VMEM(*v) for v in shapes]
                + [
                    pltpu.VMEM((width, 2 * span), BF),
                    pltpu.VMEM((width, 2 * span), BF),
                    pltpu.VMEM((2 * span, width), BF),
                    pltpu.VMEM((g, 16, rows), BF),
                    pltpu.SemaphoreType.DMA((5 + 2 * n * (2 + cuts) + 2 * g,)),
                    pltpu.SemaphoreType.DMA((14,)),
                ],
                "sv" + "h" * (6 + 2 * n),
                (
                    place,
                    jnp.broadcast_to(unit_index.astype(F32), (8, 2 * span)),
                    *row_pieces,
                    all_grads,
                    *second_here,
                    *second_far,
                ),
                out="h",
                spare=16,
            )
            return got[:5], got[5:10], got[10:]
        group_rows = jnp.concatenate(row_pieces, axis=0)
        stacks = []
        for pieces in (second_here, second_far):
            out = jnp.zeros((n, *pieces[0].shape), BF)
            for k in range(n):
                out = lax.dynamic_update_index_in_dim(out, pieces[k], (z - k) % n, 0)
            stacks.append(out)
        gate_matrix, up_matrix = (
            jnp.concatenate(
                [v[:, k * depth : (k + 1) * depth].reshape(width, span) for v in stacks], axis=1
            )
            for k in (0, 1)
        )
        down_matrix = jnp.concatenate(
            [v[:, 2 * depth :].reshape(n, cuts, strip, span).transpose(0, 2, 1, 3) for v in stacks],
            axis=0,
        ).reshape(2 * span, width)
        grad_got = jnp.stack(
            [lax.dynamic_index_in_dim(all_grads, p ^ r, 0, keepdims=False)[e] for r in range(g)]
        )
        group_grads = grad_got[:, :rows].reshape(all_rows, width)
        group_codes = grad_got[:, rows, :rows].reshape(all_rows, 1).astype(jnp.int32)
        group_limits = jnp.where(
            group_codes < 0, 0, jnp.right_shift(jnp.int32(units), jnp.minimum(3 - group_codes, 3))
        )
        live = unit_index[None, :] < group_limits
        gate_pre = dot(group_rows, gate_matrix)
        lifted = dot(group_rows, up_matrix)
        sigmoid_gate = jax.nn.sigmoid(gate_pre)
        activated = gate_pre * sigmoid_gate
        hidden = jnp.where(live, (activated * lifted).astype(BF), jnp.zeros((), BF))
        grad_hidden = jnp.where(live, contract_cols(group_grads, down_matrix), 0.0)
        grad_gate = (
            grad_hidden * lifted * sigmoid_gate * (1.0 + gate_pre * (1.0 - sigmoid_gate))
        ).astype(BF)
        grad_lifted = (grad_hidden * activated).astype(BF)
        partial_input = (
            contract_cols(grad_gate, gate_matrix) + contract_cols(grad_lifted, up_matrix)
        ).astype(BF)
        partial_ffn = dot(hidden, down_matrix).astype(BF)
        return (
            list(split_rows(partial_input.reshape(g, rows, width))),
            list(split_rows(partial_ffn.reshape(g, rows, width))),
            [group_rows, group_grads, hidden, jnp.concatenate([grad_gate, grad_lifted], axis=1)],
        )

    def unit_grads(own, far):
        if fast_units:
            return call(
                functools.partial(unit_sums_kernel, n, depth, strip),
                [((n, 2 * depth + cuts * strip, span), BF)] * 2,
                [pltpu.VMEM(v.shape, BF) for v in (*own, *far)]
                + [pltpu.VMEM((n, 2 * depth + cuts * strip, span), BF)] * 2
                + [pltpu.SemaphoreType.DMA((8,)), pltpu.SemaphoreType.DMA((4 * n,))],
                "h" * 8,
                (*own, *far),
                out="h",
                spare=16,
            )
        group_rows, group_grads, hidden, grads_two = (
            jnp.concatenate([v, w], axis=0) for v, w in zip(own, far)
        )

        def half_grads(half):
            low = slice(half * span, (half + 1) * span)
            made = contract_rows(hidden[:, low], group_grads).astype(BF)
            made = made.reshape(n, strip, cuts, span).transpose(0, 2, 1, 3)
            return jnp.concatenate(
                [
                    contract_rows(group_rows, v[:, low]).astype(BF).reshape(n, depth, span)
                    for v in (grads_two[:, : 2 * span], grads_two[:, 2 * span :])
                ]
                + [made.reshape(n, cuts * strip, span)],
                axis=1,
            )

        return [half_grads(0), half_grads(1)]

    far_pieces = gather_rest(list(far_pieces))
    own_out = together(functools.partial(feed_forward, 0), own_pieces)
    (own_input, own_ffn, own_saved), far_pieces = cut(own_out, far_pieces)
    to_one, to_two, *own_waiting = own_input
    own_got, (far_input, far_ffn, far_saved) = cut(
        (hop(to_one, 1), hop(to_two, 2)), together(functools.partial(feed_forward, 1), far_pieces)
    )
    to_one, to_two, *far_waiting = far_input
    own_half, far_got, (sums_here, sums_there) = cut(
        plane_reduce_rest(*own_got, *own_waiting),
        (hop(to_one, 1), hop(to_two, 2)),
        together(unit_grads, own_saved, far_saved),
    )
    far_sum, far_sums = cut(plane_reduce_rest(*far_got, *far_waiting), core(sums_there))
    far_sum = summed(*far_sum)

    def unit_sums(k):
        here, there = (
            lax.dynamic_index_in_dim(v, k, 0, keepdims=False).astype(F32)
            for v in (sums_here, far_sums)
        )
        return (here + there).astype(BF)

    def mixed(own, far):
        half = own.shape[0] // 2
        return jnp.concatenate([own[:half], far[:half], own[half:], far[half:]], axis=0)

    far_half = pair(far_sum.astype(BF))
    to_one, to_two, branch_own = (mixed(v, w) for v, w in zip(own_ffn[:3], far_ffn[:3]))
    branch_waiting = [branch_own] + [
        jnp.concatenate([v, w], axis=0) for v, w in zip(own_ffn[3:], far_ffn[3:])
    ]
    to_one, to_two = cut(to_one, to_two, far_sum)[:2]
    branch_got = hop(to_one, 1), hop(to_two, 2)
    messages = [unit_sums((z + k) % n) for k in range(n)]
    far_half, branch_got, *messages = cut(far_half, branch_got, *messages)
    sums = [messages[0].astype(F32), 0.0]
    moved = [ring(messages[k], k) for k in range(1, n)]

    def my_half(x, which, axis):
        return lax.dynamic_index_in_dim(x, which, axis, keepdims=False)

    def for_member(stacked, r, axis):
        return lax.dynamic_index_in_dim(stacked, p ^ r, axis, keepdims=False)

    def attention_back(own_half, far_half, branch_got):
        grad_normed_ffn = (summed(*own_half) + far_half.astype(F32)).astype(BF).astype(F32)
        grad_middle = out_cotangent.astype(F32) + norm_back(
            grad_normed_ffn, unit_second, inverse_second, gain_second
        )
        branch_pieces = plane_gather(grad_middle.astype(BF))
        fast = n == g and hs % 16 == 0
        if fast:
            branch_rows = jnp.concatenate(branch_pieces, axis=0)
            out_here, out_there = call(
                functools.partial(out_sums_kernel, g, hs, mine),
                [((g, blocks * hs, mine), BF)] * 2,
                [pltpu.VMEM((mine, mine), F32)],
                "svv",
                (place, attended, branch_rows),
            )
            out_there, *branch_pieces = cut(core(out_there), *branch_pieces)
            out_sum = (out_here.astype(F32) + out_there.astype(F32)).astype(BF)
        got_one, got_two, *branch_pieces = cut(*branch_got, *branch_pieces)
        branch_sum = plane_reduce_rest(got_one, got_two, *branch_waiting)
        grad_branch, grad_packed, *normed_parts = call(
            functools.partial(attend_back_kernel, rows, mine, head),
            [((all_rows, width), BF), ((all_rows, 3 * mine), BF), *split_shapes(rows, width)],
            [pltpu.VMEM((all_rows, mine), BF)],
            "v" * 13,
            (*branch_pieces, my_out, my_qkv, queries, keys, values, cosines, sines, bias),
        )
        branch_sum, grad_packed = cut(branch_sum, grad_packed)
        if fast:
            quarters = [hop(for_member(after(out_sum, grad_packed), r, 0), r) for r in (1, 2)]
            sum_here, sum_there = call(
                functools.partial(weight_sums_kernel, g, depth, mine),
                [((g, 3 * hd, mine), BF)] * 2,
                [pltpu.VMEM((depth, 3 * mine), F32)],
                "svv",
                (place, all_normed, grad_packed),
            )
            sum_there, out_sum, *quarters = cut(sum_there, out_sum, *quarters)
            quarters.append(hop(for_member(out_sum, 3, 0), 3))
            weight_sum = (sum_here.astype(F32) + core(sum_there).astype(F32)).astype(BF)
            last_parts = call(
                functools.partial(last_parts_kernel, g, 3 * hd),
                [((3 * hd + blocks * hs, mine), BF)] * g,
                [pltpu.VMEM((g, blocks * hs, mine), BF)],
                "s" + "v" * (g + 1),
                (place, weight_sum, for_member(out_sum, 0, 0), *quarters),
            )
        else:
            out_grad = contract_rows(attended, grad_branch).astype(BF)
            out_grad = out_grad.reshape(n // g, g, 2, hs, width)
            out_sum = my_half(out_grad, c, 2).astype(F32)
            out_sum = (out_sum + core(my_half(out_grad, 1 - c, 2)).astype(F32)).astype(BF)
            out_sum = by_member(
                [for_member(out_sum, 0, 1)]
                + [hop(for_member(out_sum, r, 1), r) for r in range(1, g)]
            ).reshape(n, hs, blocks, mine)
            qkv_grad = contract_rows(all_normed, grad_packed).astype(BF).reshape(n, 2, hd, 3, mine)
            qkv_sum = my_half(qkv_grad, c, 1).astype(F32)
            qkv_sum += core(my_half(qkv_grad, 1 - c, 1)).astype(F32)
            last_part = jnp.concatenate(
                [
                    qkv_sum.astype(BF).transpose(0, 2, 1, 3).reshape(n, 3 * hd, mine),
                    out_sum.transpose(0, 2, 1, 3).reshape(n, blocks * hs, mine),
                ],
                axis=1,
            )
            last_parts = [
                lax.dynamic_index_in_dim(last_part, (z + k) % n, 0, keepdims=False) for k in range(n)
            ]
        normed_parts = cut(*normed_parts, *last_parts)[:5]
        grad_normed = plane_reduce(*normed_parts)
        unit_first, inverse_first = unit(residual)
        input_grad = (
            grad_middle + norm_back(grad_normed, unit_first, inverse_first, gain_first)
        ).astype(BF)
        return input_grad, last_parts, branch_sum

    input_grad, last_parts, branch_sum = together(
        attention_back, own_half, far_half, branch_got
    )
    cut_values = cut(*moved, *last_parts)
    moved, last_parts = cut_values[: n - 1], cut_values[n - 1 :]
    for k in range(1, n):
        sums[k % 2] += moved[k - 1].astype(F32)
    pair_sums = jnp.concatenate([v.astype(BF) for v in sums], axis=0)
    last_moved = [ring(last_parts[k], k) for k in range(1, n)]

    unit_pieces = together(plane_gather, pair_sums)
    got = cut(*unit_pieces, *last_moved)
    unit_pieces, last_moved = got[:5], got[5:]
    last_sum = last_parts[0].astype(F32) + sum(v.astype(F32) for v in last_moved)
    last_one = gather_first(last_sum.astype(BF))
    if strip % 32 == 0:
        share_gate, share_up, ffn_part = call(
            functools.partial(columns_results_kernel, n, g, depth, strip, 2 * depth + cuts * strip),
            [
                ((depth * units // 128, 128), F32),
                ((depth * units // 128, 128), F32),
                ((depth, 1), F32),
            ],
            [
                pltpu.VMEM((shares, depth, span), BF),
                pltpu.VMEM((shares, depth, span), BF),
                pltpu.SemaphoreType.DMA((2, shares)),
            ],
            "s" + "h" * 5 + "vv",
            (place, *unit_pieces, w_gate[:, 0], w_up[:, 0]),
        )
        ffn_part = ffn_part[:, 0]
    else:
        got = as_members(unit_pieces).reshape(g, 2, -1, span)
        all_units = jnp.zeros((shares, *got.shape[2:]), BF)
        for r in range(g):
            for odd in (0, 1):
                all_units = lax.dynamic_update_index_in_dim(
                    all_units, got[r, odd], (p ^ r) * 2 + (z % 2) ^ odd, 0
                )

        def columns_back(pieces):
            return (
                pieces.reshape(shares, depth, n, strip)
                .transpose(1, 2, 0, 3)
                .reshape(depth, units)
                .astype(F32)
            )

        share_gate = columns_back(all_units[:, :depth])
        share_up = columns_back(all_units[:, depth : 2 * depth])
        share_down = (
            all_units[:, 2 * depth :]
            .reshape(shares, cuts, strip, span)
            .transpose(0, 2, 1, 3)
            .reshape(units // n, width)
            .astype(F32)
        )
        ffn_part = jnp.sum(
            share_gate * w_gate[:, 0].astype(F32) + share_up * w_up[:, 0].astype(F32), axis=1
        )
    *last_one, ffn_part = cut(*last_one, ffn_part)
    last_pieces = gather_rest(last_one)
    if strip % 32 == 0:
        [share_down] = call(
            functools.partial(rows_results_kernel, n, g, depth, strip, 2 * depth + cuts * strip),
            [((units // n * width // 128, 128), F32)],
            [pltpu.VMEM((shares, cuts * strip, span), BF), pltpu.SemaphoreType.DMA((shares,))],
            "s" + "h" * 5,
            (place, *cut(*unit_pieces, ffn_part)[:5]),
        )
        *last_rest, share_down = cut(*last_pieces[3:], share_down)
        last_pieces[3:] = last_rest
    share_gain_ffn = (ffn_part + core(ffn_part)) / gain_ffn.astype(F32)
    branch_sum = summed(*branch_sum).reshape(2, 2, rows // 2, width)
    branch_ffn, branch_far = (branch_sum[:, k].reshape(rows, width) for k in (0, 1))
    branch_ffn += pair(branch_far.astype(BF)).astype(F32)
    outputs = (middle + branch_ffn.astype(BF).astype(F32)).astype(BF)
    if hs % 16 == 0:
        share_qkv, share_out, attn_part = call(
            functools.partial(attention_results_kernel, g, depth, mine),
            [((depth, 3 * width), F32), ((depth, width), F32), ((depth, 1), F32)],
            [
                pltpu.VMEM((depth, 3 * width), BF),
                pltpu.VMEM((depth, width), BF),
                pltpu.SemaphoreType.DMA((2 * (g + 1) * (3 + blocks),)),
            ],
            "s" + "h" * 10 + "v",
            (place, *last_pieces, *(core(v) for v in last_pieces), w_qkv),
        )
        attn_part = attn_part[:, 0]
    else:
        last_got = as_members(last_pieces)
        last_got = by_member([last_got[r] for r in range(g)])
        last_both = ordered(last_got, core(last_got), 0)
        share_qkv = (
            last_both[:, :, : 3 * hd]
            .reshape(2, g, 3, hd, mine)
            .transpose(0, 3, 2, 1, 4)
            .reshape(depth, 3 * width)
            .astype(F32)
        )
        share_out = (
            last_both[:, :, 3 * hd :]
            .reshape(2, g, blocks, hs, mine)
            .transpose(1, 0, 3, 2, 4)
            .reshape(depth, width)
            .astype(F32)
        )
        attn_part = jnp.sum(share_qkv * w_qkv.astype(F32), axis=1)
    share_gain_attn = attn_part / gain_attn.astype(F32)
    return (
        outputs,
        input_grad,
        share_qkv,
        share_out,
        share_gain_attn,
        share_gain_ffn,
        share_gate.reshape(depth, 1, units),
        share_up.reshape(depth, 1, units),
        share_down.reshape(units // n, 1, width),
    )


def solution(mesh):
    in_specs = (
        P(("batch", "gran", "ffn"), None),
        P(("batch", "gran", "ffn")),
        P(("batch", "gran", "ffn")),
        P("batch", None),
        P("batch", None),
        P("batch"),
        P("batch"),
        P("batch", "ffn", None),
        P("batch", "ffn", None),
        P("batch", "ffn", None),
        P(("batch", "gran", "ffn"), None),
    )
    out_specs = (
        P(("batch", "gran", "ffn"), None),
        P(("batch", "gran", "ffn"), None),
        P("batch", None),
        P("batch", None),
        P("batch"),
        P("batch"),
        P("batch", "ffn", None),
        P("batch", "ffn", None),
        P("batch", "ffn", None),
    )
    return jax.shard_map(local, mesh=mesh, in_specs=in_specs, out_specs=out_specs, check_vma=False)
```

```python
import functools
import math

import jax
import jax.numpy as jnp
from jax import lax
from jax.experimental import pallas as pl
from jax.experimental.pallas import tpu as pltpu
from jax.sharding import PartitionSpec as P

H = 12


EPSILON = 1e-06
NEG_FILL = -1e30
ROPE_BASE = 10000.0
BF = jnp.bfloat16
F32 = jnp.float32


def row_groups(seq_rows, seq_groups, kept_rows):
    labels = jnp.arange(seq_groups.shape[0], dtype=jnp.int32)
    member = (seq_rows[:, None] == labels[None, :]).astype(jnp.int32)
    group_id = jnp.sum(member * seq_groups[None, :], axis=1)
    index = jnp.arange(seq_rows.shape[0], dtype=jnp.int32)
    earlier = (group_id[None, :] == group_id[:, None]) & (index[None, :] < index[:, None])
    rank = jnp.sum(earlier.astype(jnp.int32), axis=1)
    return jnp.where(rank < kept_rows, group_id, -1)


def dot(left, right):
    return jnp.dot(left, right, preferred_element_type=F32)


def contract_rows(left, right):
    return lax.dot_general(left, right, (((0,), (0,)), ((), ())), preferred_element_type=F32)


def contract_cols(left, right):
    return lax.dot_general(left, right, (((1,), (1,)), ((), ())), preferred_element_type=F32)


def norm_back(grad_normed, unit_rows, inverse_rms, gain):
    scaled = grad_normed * gain
    return inverse_rms * (scaled - unit_rows * jnp.mean(scaled * unit_rows, axis=-1, keepdims=True))


def first_rows(values, count, width):
    return jnp.pad(values.astype(BF)[None, :], ((0, count - 1), (0, width - values.shape[0])))


def after(value, *others):
    return lax.optimization_barrier((value, *others))[0]


def small_cost():
    return pl.CostEstimate(flops=1, bytes_accessed=1, transcendentals=0)


def call(kernel, outs, scratch=(), ins=(), operands=(), out="v", spare=8):
    held = [v for k, v in zip(ins, operands) if k == "v"]
    held += [jax.ShapeDtypeStruct(*v) for v in outs if out == "v"]
    held += [v for v in scratch if v.dtype in (BF, F32)]
    limit = sum(math.prod(v.shape) * v.dtype.itemsize for v in held) + spare * 2**20
    kinds = {
        "v": pl.BlockSpec(memory_space=pltpu.VMEM),
        "h": pl.BlockSpec(memory_space=pl.ANY),
        "s": pl.BlockSpec(memory_space=pltpu.SMEM),
    }
    return pl.pallas_call(
        kernel,
        out_shape=[jax.ShapeDtypeStruct(shape, dtype) for shape, dtype in outs],
        in_specs=[kinds[k] for k in ins],
        out_specs=[kinds[out]] * len(outs),
        scratch_shapes=list(scratch),
        compiler_params=pltpu.CompilerParams(vmem_limit_bytes=limit),
        cost_estimate=small_cost(),
    )(*operands)


def split_parts(value, rows, to_one, to_two, own, two_low, one_high):
    half = rows // 2
    to_one[:half] = value[rows : rows + half].astype(BF)
    to_one[half:] = value[3 * rows : 3 * rows + half].astype(BF)
    to_two[:half] = value[2 * rows + half : 3 * rows].astype(BF)
    to_two[half:] = value[3 * rows + half :].astype(BF)
    own[...] = value[:rows]
    two_low[...] = value[2 * rows : 2 * rows + half].astype(BF)
    one_high[...] = value[rows + half : 2 * rows].astype(BF)


def split_shapes(rows, width):
    half = rows // 2
    return [
        ((rows, width), BF),
        ((rows, width), BF),
        ((rows, width), F32),
        ((half, width), BF),
        ((half, width), BF),
    ]


def reduce_first_kernel(got_one, got_two, own, two_low, one_high, to_two, to_one, total):
    half = two_low.shape[0]
    to_two[...] = (two_low[...].astype(F32) + got_one[half:].astype(F32)).astype(BF)
    to_one[...] = (one_high[...].astype(F32) + got_two[half:].astype(F32)).astype(BF)
    total[:half] = own[:half].astype(F32) + got_one[:half].astype(F32)
    total[half:] = own[half:].astype(F32) + got_two[:half].astype(F32)


def attend_kernel(n, rows, depth, mine, head, place, freq, *refs):
    tokens, refs = refs[:5], refs[5:]
    here, there, refs = refs[:n], refs[n : 2 * n], refs[2 * n :]
    normed, weight, queries, keys, values, attended, cosines, sines, bias, gains = refs[:10]
    gain_rows, unit_rows, sems = refs[10:]
    z, c = place[0], place[2]
    hd = depth // 2
    width = n * depth
    copies = []
    for s in range(n):
        plane = lax.rem(z - s + n, n)
        for which, pieces in ((c, here), (1 - c, there)):
            start = pl.multiple_of(plane * depth + which * hd, 8)
            for k in range(3):
                copies.append(
                    pltpu.make_async_copy(
                        pieces[s].at[pl.ds(k * hd, hd), :],
                        weight.at[pl.ds(start, hd), pl.ds(k * mine, mine)],
                        sems.at[len(copies)],
                    )
                )
        copies.append(
            pltpu.make_async_copy(
                here[s].at[pl.ds(here[s].shape[0] - 16, 16), :], gain_rows.at[plane], sems.at[len(copies)]
            )
        )
    for copy in copies:
        copy.start()

    half = rows // 2
    third = tokens[3].shape[0]
    spans = [(tokens[0], 0, 0, rows), (tokens[1], 0, rows, rows), (tokens[2], 0, 2 * rows, rows)]
    spans += [(tokens[3], 0, 3 * rows, third), (tokens[4], 0, 3 * rows + third, rows - third)]
    for ref, low, at, count in spans:
        x = ref[low : low + count, :].astype(F32)
        inverse = lax.rsqrt(jnp.mean(x * x, axis=-1, keepdims=True) + EPSILON)
        unit_rows[at : at + count] = x * inverse

    row = lax.broadcasted_iota(jnp.int32, (rows, rows), 0)
    col = lax.broadcasted_iota(jnp.int32, (rows, rows), 1)
    lane = lax.broadcasted_iota(jnp.int32, (rows, head), 1)
    sign = jnp.where(lane < head // 2, -1.0, 1.0)
    for b in range(4):
        ref, low = (tokens[b], rows) if b < 3 else (tokens[4], rows - third)
        ids = ref[low : low + 8, :rows].astype(F32)[:1]
        ids_row = jnp.broadcast_to(ids, (rows, rows))
        ids_col = jnp.sum(jnp.where(row == col, ids_row, 0.0), axis=1, keepdims=True)
        before = jnp.sum(jnp.where(ids_row < ids_col, 1.0, 0.0), axis=1, keepdims=True)
        positions = row[:, :1].astype(F32) - before
        angles = positions * freq[:1, :]
        cosines[b * rows : (b + 1) * rows] = jnp.cos(angles)
        sines[b * rows : (b + 1) * rows] = jnp.sin(angles) * sign
        bias[b * rows : (b + 1) * rows] = jnp.where(
            (ids_row == ids_col) & (row >= col), 0.0, NEG_FILL
        )

    for copy in copies:
        copy.wait()
    for k in range(n):
        block = slice(k * depth, (k + 1) * depth)
        both = gain_rows[k].astype(F32)
        gains[0:8, block] = jnp.broadcast_to(both[0:1, :depth], (8, depth))
        gains[8:16, block] = jnp.broadcast_to(both[8:9, :depth], (8, depth))
    normed[...] = (unit_rows[...] * gains[0:1, :]).astype(BF)
    x = normed[...]
    cos, sin = cosines[...], sines[...]
    scale = 1.0 / math.sqrt(head)
    for k, out in enumerate((queries, keys, values)):
        packed = dot(x, weight[:, k * mine : (k + 1) * mine])
        for h in range(mine // head):
            part = packed[:, h * head : (h + 1) * head]
            if k < 2:
                part = part * cos + pltpu.roll(part, head // 2, 1) * sin
            if k == 0:
                part = part * scale
            out[:, h * head : (h + 1) * head] = part.astype(BF)
    for b in range(4):
        for h in range(mine // head):
            here_rows, here_cols = slice(b * rows, (b + 1) * rows), slice(h * head, (h + 1) * head)
            scores = contract_cols(queries[here_rows, here_cols], keys[here_rows, here_cols])
            probs = softmax(scores + bias[here_rows])
            attended[here_rows, here_cols] = dot(
                probs.astype(BF), values[here_rows, here_cols]
            ).astype(BF)


def softmax(scores):
    exponent = jnp.exp(scores - jnp.max(scores, axis=-1, keepdims=True))
    return exponent / jnp.sum(exponent, axis=-1, keepdims=True)


def project_kernel(rows, attended, out, *parts):
    split_parts(dot(attended[...], out[...]), rows, *parts)


def attend_back_kernel(rows, mine, head, *refs):
    grads, refs = refs[:5], refs[5:]
    out, weight, queries, keys, values, cosines, sines, bias = refs[:8]
    branch, packed, *parts = refs[8:-1]
    attended_grad = refs[-1]
    third = grads[3].shape[0]
    at = 0
    for ref in grads:
        branch[at : at + ref.shape[0]] = ref[...]
        at += ref.shape[0]
    del third
    attended_grad[...] = contract_cols(branch[...], out[...]).astype(BF)
    scale = 1.0 / math.sqrt(head)
    for b in range(4):
        r = slice(b * rows, (b + 1) * rows)
        cos, sin = cosines[r], sines[r]
        for h in range(mine // head):
            cols = slice(h * head, (h + 1) * head)
            q, k, v, grad = queries[r, cols], keys[r, cols], values[r, cols], attended_grad[r, cols]
            probs = softmax(contract_cols(q, k) + bias[r])
            grad_probs = contract_cols(grad, v)
            grad_scores = probs * (
                grad_probs - jnp.sum(probs * grad_probs, axis=-1, keepdims=True)
            )
            grad_scores = grad_scores.astype(BF)
            grad_q = dot(grad_scores, k).astype(BF).astype(F32) * scale
            grad_k = contract_rows(grad_scores, q).astype(BF).astype(F32)
            grad_v = contract_rows(probs.astype(BF), grad)
            for j, part in enumerate((grad_q, grad_k, grad_v)):
                if j < 2:
                    part = part * cos - pltpu.roll(part, head // 2, 1) * sin
                packed[r, j * mine + h * head : j * mine + (h + 1) * head] = part.astype(BF)
    split_parts(contract_cols(packed[...], weight[...]), rows, *parts)


def first_part_kernel(depth, mine, members, place, w_qkv, w_out, gains, out, sems):
    p, c = place[1], place[2]
    hd, hs = depth // 2, depth // members // 2
    width = w_out.shape[1]
    moves = []
    for k in range(3):
        column = pl.multiple_of(k * width + p * mine, 128)
        moves.append((w_qkv.at[pl.ds(c * hd, hd), pl.ds(column, mine)], k * hd, hd))
    top = pl.multiple_of((p * 2 + c) * hs, 8)
    for k in range(width // mine):
        block = w_out.at[pl.ds(top, hs), pl.ds(k * mine, mine)]
        moves.append((block, 3 * hd + k * hs, hs))
    moves.append((gains, out.shape[0] - 16, 16))
    copies = [
        pltpu.make_async_copy(source, out.at[pl.ds(at, count), :], sems.at[i])
        for i, (source, at, count) in enumerate(moves)
    ]
    for copy in copies:
        copy.start()
    for copy in copies:
        copy.wait()


def out_weight_kernel(n, members, hs, mine, place, *refs):
    pieces, out, sems = refs[:members], refs[members], refs[members + 1]
    p = place[1]
    copies = []
    for r in range(members):
        for j in range(n // members):
            for half in range(2):
                top = pl.multiple_of(((j * members + (p ^ r)) * 2 + half) * hs, 8)
                for k in range(out.shape[1] // mine):
                    copies.append(
                        pltpu.make_async_copy(
                            pieces[r].at[j, half, pl.ds(k * hs, hs), :],
                            out.at[pl.ds(top, hs), pl.ds(k * mine, mine)],
                            sems.at[len(copies)],
                        )
                    )
    for copy in copies:
        copy.start()
    for copy in copies:
        copy.wait()


def strips_of(tile, strip):
    at, out = 0, []
    while at < 128:
        share, first = divmod(tile * 128 + at, strip)
        count = min(strip - first, 128 - at)
        out.append((share, first, at, count))
        at += count
    return out


def fetch_shares(members, rows, low, count, place, pieces, target, sems):
    z, p = place[0], place[1]
    copies = []
    for r in range(members):
        for odd in range(2):
            share = (p ^ r) * 2 + (lax.rem(z, 2) ^ odd)
            ref, top = (pieces[r], odd * rows + low) if r < 3 else (pieces[3 + odd], low)
            copy = pltpu.make_async_copy(
                ref.at[pl.ds(top, count), :], target.at[share], sems.at[len(copies)]
            )
            copy.start()
            copies.append(copy)
    return copies


def columns_results_kernel(n, members, depth, strip, rows, place, *refs):
    pieces, w_gate, w_up = refs[:5], refs[5], refs[6]
    gate, up, gain, held_gate, held_up, sems = refs[7:]
    shares = 2 * members
    copies = [
        fetch_shares(members, rows, k * depth, depth, place, pieces, held, sems.at[k])
        for k, held in enumerate((held_gate, held_up))
    ]
    lanes = lax.broadcasted_iota(jnp.int32, (depth, 128), 1)
    row_tiles = n * shares * strip // 128
    total = jnp.zeros((depth, 128), F32)
    for which, (out, held, weight) in enumerate(
        ((gate, held_gate, w_gate), (up, held_up, w_up))
    ):
        for copy in copies[which]:
            copy.wait()
        for k in range(n):
            for tile in range(shares * strip // 128):
                made = jnp.zeros((depth, 128), F32)
                for share, first, lane, count in strips_of(tile, strip):
                    column = k * strip + first
                    while count > 0:
                        source, offset = divmod(column, 128)
                        some = min(count, 128 - offset)
                        value = held[share, :, source * 128 : (source + 1) * 128].astype(F32)
                        if lane != offset:
                            value = pltpu.roll(value, (lane - offset) % 128, 1)
                        made = jnp.where((lanes >= lane) & (lanes < lane + some), value, made)
                        column, lane, count = column + some, lane + some, count - some
                at = k * (shares * strip // 128) + tile
                out[pl.ds(at, depth, stride=row_tiles), :] = made
                total += made * weight[:, at * 128 : (at + 1) * 128].astype(F32)
    gain[...] = jnp.sum(total, axis=1, keepdims=True)


def rows_results_kernel(n, members, depth, strip, rows, place, *refs):
    pieces, down, held, sems = refs[:5], refs[5], refs[6], refs[7]
    span, cuts = n * strip, (rows - 2 * depth) // strip
    copies = fetch_shares(members, rows, 2 * depth, cuts * strip, place, pieces, held, sems)
    for copy in copies:
        copy.wait()
    wide = cuts * span // 128
    for share in range(2 * members):
        for k in range(cuts):
            for tile in range(span // 128):
                block = slice(k * strip, (k + 1) * strip), slice(tile * 128, (tile + 1) * 128)
                start = share * strip * wide + k * (span // 128) + tile
                down[pl.ds(start, strip, stride=wide), :] = held[(share, *block)].astype(F32)


def attention_results_kernel(members, depth, mine, place, *refs):
    here, there, w_qkv = refs[:5], refs[5:10], refs[10]
    qkv, out, gain, held, held_out, sems = refs[11:]
    p, c = place[1], place[2]
    hd, hs = depth // 2, depth // members // 2
    width = held_out.shape[1]
    blocks = width // mine
    copies = []

    def add(source, target):
        copies.append(pltpu.make_async_copy(source, target, sems.at[len(copies)]))

    def place_rows(ref, first, low, count, r, half):
        for k in range(3):
            top, end = max(low, k * hd), min(low + count, (k + 1) * hd)
            if top < end:
                add(
                    ref.at[pl.ds(first + top - low, end - top), :],
                    held.at[
                        pl.ds(pl.multiple_of(half * hd + top - k * hd, 8), end - top),
                        pl.ds(pl.multiple_of(k * width + (p ^ r) * mine, 128), mine),
                    ],
                )
        for k in range(blocks):
            base = 3 * hd + k * hs
            top, end = max(low, base), min(low + count, base + hs)
            if top < end:
                add(
                    ref.at[pl.ds(first + top - low, end - top), :],
                    held_out.at[
                        pl.ds(pl.multiple_of(((p ^ r) * 2 + half) * hs + top - base, 8), end - top),
                        pl.ds(k * mine, mine),
                    ],
                )

    rows = 3 * hd + blocks * hs
    for half, pieces in ((c, here), (1 - c, there)):
        for r in range(3):
            place_rows(pieces[r], 0, 0, rows, r, half)
        third = pieces[3].shape[0]
        place_rows(pieces[3], 0, 0, third, 3, half)
        place_rows(pieces[4], 0, third, rows - third, 3, half)
    for copy in copies:
        copy.start()
    for copy in copies:
        copy.wait()
    total = jnp.zeros((depth, 128), F32)
    for tile in range(3 * width // 128):
        cols = slice(tile * 128, (tile + 1) * 128)
        value = held[:, cols].astype(F32)
        qkv[:, cols] = value
        total += value * w_qkv[:, cols].astype(F32)
    gain[...] = jnp.sum(total, axis=1, keepdims=True)
    out[...] = held_out[...].astype(F32)


def out_sums_kernel(members, hs, mine, place, attended, branch, mine_out, theirs_out, held):
    c = place[2]
    for k in range(branch.shape[1] // mine):
        cols = slice(k * mine, (k + 1) * mine)
        held[...] = contract_rows(attended[...], branch[:, cols])
        for out, half in ((mine_out, c), (theirs_out, 1 - c)):
            for quarter in range(members):
                start = pl.multiple_of((quarter * 2 + half) * hs, 8)
                value = held[pl.ds(start, hs), :]
                out[quarter, k * hs : (k + 1) * hs, :] = value.astype(BF)


def weight_sums_kernel(members, depth, mine, place, normed, packed, mine_out, theirs_out, held):
    c = place[2]
    hd = depth // 2
    for plane in range(members):
        block = slice(plane * depth, (plane + 1) * depth)
        held[...] = contract_rows(normed[:, block], packed[...])
        for out, half in ((mine_out, c), (theirs_out, 1 - c)):
            start = pl.multiple_of(half * hd, 8)
            for k in range(3):
                value = held[pl.ds(start, hd), k * mine : (k + 1) * mine]
                out[plane, k * hd : (k + 1) * hd, :] = value.astype(BF)


def last_parts_kernel(members, low, place, *refs):
    sums, quarters, outs, held = refs[0], refs[1 : members + 1], refs[members + 1 : -1], refs[-1]
    z, p = place[0], place[1]
    for r in range(members):
        held[r] = quarters[r][...]
    for k in range(members):
        plane = lax.rem(z + k, members)
        outs[k][:low] = sums[plane]
        outs[k][low:] = held[p ^ plane]


def feed_forward_kernel(n, members, depth, strip, rows, e, place, unit_index, *refs):
    pieces, all_grads, refs = refs[:5], refs[5], refs[6:]
    here, there, refs = refs[:n], refs[n : 2 * n], refs[2 * n :]
    outs, scratch = refs[:14], refs[14:28]
    splits, (x, cot, hidden, grads_two) = scratch[:10], scratch[10:]
    gate, up, down, codes, in_sems, out_sems = refs[28:]
    z, p = place[0], place[1]
    span = n * strip
    units = span * 2 * members
    started, finishing = [], []

    def fetch(source, target):
        copy = pltpu.make_async_copy(source, target, in_sems.at[len(started)])
        copy.start()
        started.append(copy)

    def flush(index):
        copy = pltpu.make_async_copy(scratch[index], outs[index], out_sems.at[index])
        copy.start()
        finishing.append(copy)

    at = 0
    for ref in pieces:
        fetch(ref, x.at[pl.ds(at, ref.shape[0]), :])
        at += ref.shape[0]
    for s in range(n):
        plane = lax.rem(z - s + n, n)
        top = pl.multiple_of(plane * depth, 8)
        for half, parts in enumerate((here, there)):
            columns = pl.ds(half * span, span)
            fetch(parts[s].at[pl.ds(0, depth), :], gate.at[pl.ds(top, depth), columns])
            fetch(parts[s].at[pl.ds(depth, depth), :], up.at[pl.ds(top, depth), columns])
    first = len(started)
    for r in range(members):
        fetch(all_grads.at[p ^ r, e, pl.ds(0, rows), :], cot.at[pl.ds(r * rows, rows), :])
        fetch(all_grads.at[p ^ r, e, pl.ds(rows, 16), pl.ds(0, rows)], codes.at[r])
    for s in range(n):
        plane = lax.rem(z - s + n, n)
        for half, parts in enumerate((here, there)):
            start = pl.multiple_of(half * span + plane * strip, 8)
            for j in range(down.shape[1] // span):
                fetch(
                    parts[s].at[pl.ds(2 * depth + j * strip, strip), :],
                    down.at[pl.ds(start, strip), pl.ds(j * span, span)],
                )
    for copy in started[:first]:
        copy.wait()
    flush(10)
    row = lax.broadcasted_iota(jnp.int32, (rows, rows), 0)
    col = lax.broadcasted_iota(jnp.int32, (rows, rows), 1)

    gate_pre = dot(x[...], gate[...])
    lifted = dot(x[...], up[...])
    sigmoid = jax.nn.sigmoid(gate_pre)
    activated = gate_pre * sigmoid
    for copy in started[first:]:
        copy.wait()
    flush(11)
    limits = []
    for r in range(members):
        line = jnp.broadcast_to(codes[r].astype(F32)[:1], (rows, rows))
        code = jnp.sum(jnp.where(row == col, line, 0.0), axis=1, keepdims=True)
        limits.append(
            sum(jnp.where(code == k, float(units >> (members - 1 - k)), 0.0) for k in range(members))
        )
    live = unit_index[:1, :] < jnp.concatenate(limits, axis=0)
    hidden[...] = jnp.where(live, activated * lifted, 0.0).astype(BF)
    grad_hidden = jnp.where(live, contract_cols(cot[...], down[...]), 0.0)
    wide = 2 * span
    grads_two[:, :wide] = (
        grad_hidden * lifted * sigmoid * (1.0 + gate_pre * (1.0 - sigmoid))
    ).astype(BF)
    grads_two[:, wide:] = (grad_hidden * activated).astype(BF)
    flush(12)
    flush(13)
    grads = contract_cols(grads_two[:, :wide], gate[...])
    grads += contract_cols(grads_two[:, wide:], up[...])
    split_parts(grads, rows, *splits[:5])
    for index in range(5):
        flush(index)
    split_parts(dot(hidden[...], down[...]), rows, *splits[5:])
    for index in range(5, 10):
        flush(index)
    for copy in finishing:
        copy.wait()


def unit_sums_kernel(n, depth, strip, *refs):
    given, outs, held = refs[:8], refs[8:10], refs[10:18]
    sums, in_sems, out_sems = refs[18:20], refs[20], refs[21]
    parts = held[:4], held[4:]
    span = n * strip
    fetched = [
        pltpu.make_async_copy(given[i], held[i], in_sems.at[i]) for i in (0, 3, 4, 7, 1, 2, 5, 6)
    ]
    for copy in fetched:
        copy.start()
    for copy in fetched[:4]:
        copy.wait()
    finishing = []

    def flush(half, plane, low, count):
        place = (plane, pl.ds(low, count), slice(None))
        copy = pltpu.make_async_copy(
            sums[half].at[place], outs[half].at[place], out_sems.at[len(finishing)]
        )
        copy.start()
        finishing.append(copy)

    for plane in range(n):
        block = slice(plane * depth, (plane + 1) * depth)
        made = sum(contract_rows(x[:, block], grads[...]) for x, _, _, grads in parts)
        for half in range(2):
            for k in range(2):
                low = (2 * k + half) * span
                value = made[:, low : low + span].astype(BF)
                sums[half][plane, k * depth : (k + 1) * depth, :] = value
            flush(half, plane, 0, 2 * depth)
    for copy in fetched[4:]:
        copy.wait()
    cuts = held[1].shape[1] // span
    for j in range(cuts):
        cols = slice(j * span, (j + 1) * span)
        made = sum(contract_rows(hidden[...], cot[:, cols]) for _, cot, hidden, _ in parts)
        made = made.astype(BF)
        for half in range(2):
            for plane in range(n):
                low, at = half * span + plane * strip, 2 * depth + j * strip
                sums[half][plane, at : at + strip, :] = made[low : low + strip]
    for half in range(2):
        for plane in range(n):
            flush(half, plane, 2 * depth, cuts * strip)
    for copy in finishing:
        copy.wait()


def move(kernel, outs, copies, operands, ins):
    kinds = {"h": pl.BlockSpec(memory_space=pl.ANY), "s": pl.BlockSpec(memory_space=pltpu.SMEM)}
    return pl.pallas_call(
        kernel,
        out_shape=[jax.ShapeDtypeStruct(shape, BF) for shape in outs],
        in_specs=[kinds[k] for k in ins],
        out_specs=[pl.BlockSpec(memory_space=pltpu.VMEM)] * len(outs),
        scratch_shapes=[pltpu.SemaphoreType.DMA((copies,))],
        compiler_params=pltpu.CompilerParams(vmem_limit_bytes=56 * 2**20),
        cost_estimate=small_cost(),
    )(*operands)


def local(
    tokens,
    seq_ids,
    granularity,
    w_qkv,
    w_out,
    gain_attn,
    gain_ffn,
    w_gate,
    w_up,
    w_down,
    out_cotangent,
):
    n = lax.axis_size("batch")
    g = lax.axis_size("gran")
    z = lax.axis_index("batch")
    p = lax.axis_index("gran")
    c = lax.axis_index("ffn")
    rows, width = tokens.shape
    head = width // H
    heads = H // g
    mine = heads * head
    depth = w_qkv.shape[0]
    units = w_gate.shape[2]
    capacity = max(2, (5 * rows + 4 * n * g - 1) // (4 * n * g))

    def hop(x, r):
        return lax.ppermute(x, "gran", [(i, i ^ r) for i in range(g)])

    def pair(x):
        return lax.ppermute(x, "batch", [(i, i ^ 1) for i in range(n)])

    def core(x):
        return lax.ppermute(x, "ffn", [(0, 1), (1, 0)])

    def ring(x, s):
        return lax.ppermute(x, "batch", [(i, (i + s) % n) for i in range(n)])

    def gather_first(x):
        return [x, hop(x, 1), hop(x, 2)]

    def gather_rest(pieces):
        half = pieces[0].shape[0] // 32 * 16 or pieces[0].shape[0] // 2
        return [*pieces, hop(pieces[1][:half], 2), hop(pieces[2][half:], 1)]

    def plane_gather(x):
        return gather_rest(gather_first(x))

    def as_members(pieces):
        return jnp.concatenate(pieces, axis=0).reshape(g, *pieces[0].shape)

    def split_rows(x):
        half = x.shape[1] // 2
        return (
            jnp.concatenate([x[1, :half], x[3, :half]], axis=0),
            jnp.concatenate([x[2, half:], x[3, half:]], axis=0),
            x[0],
            x[2, :half],
            x[1, half:],
        )

    def plane_reduce(to_one, to_two, own, two_low, one_high):
        return summed(*plane_reduce_rest(hop(to_one, 1), hop(to_two, 2), own, two_low, one_high))

    def plane_reduce_rest(got_one, got_two, own, two_low, one_high):
        half, columns = two_low.shape
        two_low, one_high, total = call(
            reduce_first_kernel,
            [((half, columns), BF), ((half, columns), BF), ((2 * half, columns), F32)],
            (),
            "v" * 5,
            (got_one, got_two, own, two_low, one_high),
        )
        return total, hop(two_low, 2), hop(one_high, 1)

    def summed(total, low, high):
        return total + jnp.concatenate([low, high], axis=0).astype(F32)

    def by_member(pieces):
        out = jnp.zeros((g, *pieces[0].shape), pieces[0].dtype)
        for r in range(g):
            out = lax.dynamic_update_index_in_dim(out, pieces[r], p ^ r, 0)
        return out

    def ordered(here, there, axis):
        return jnp.stack(
            [jnp.where(c == 0, here, there), jnp.where(c == 0, there, here)], axis=axis
        )

    def cut(*values):
        return lax.optimization_barrier(values)

    def together(body, *operands):
        made = jax.eval_shape(body, *operands)
        return lax.cond(
            seq_ids[0] >= 0,
            body,
            lambda *given: jax.tree.map(lambda v: jnp.zeros(v.shape, v.dtype), made),
            *operands,
        )

    place = jnp.stack([z, p, c]).astype(jnp.int32)
    hd, sub = depth // 2, depth // g
    hs, blocks = sub // 2, width // mine
    gain_part = jnp.concatenate(
        [first_rows(gain_attn, 8, mine), first_rows(gain_ffn, 8, mine)], axis=0
    )
    token_part = jnp.concatenate([tokens, first_rows(seq_ids, 16, width)], axis=0)
    codes = row_groups(seq_ids, granularity, capacity * n)
    grad_part = jnp.concatenate([out_cotangent, first_rows(codes, 16, width)], axis=0)
    if hs % 8 == 0:
        [first_part] = move(
            functools.partial(first_part_kernel, depth, mine, g),
            [(3 * hd + blocks * hs + 16, mine)],
            blocks + 4,
            (place, w_qkv, w_out, gain_part),
            "shhh",
        )
    else:
        out_part = lax.dynamic_slice(w_out, ((p * 2 + c) * hs, 0), (hs, width))
        first_part = jnp.concatenate(
            [
                lax.dynamic_slice(w_qkv, (c * hd, k * width + p * mine), (hd, mine))
                for k in range(3)
            ]
            + [out_part[:, k * mine : (k + 1) * mine] for k in range(blocks)]
            + [gain_part],
            axis=0,
        )
    shares = 2 * g
    strip = units // n // shares
    share = p * 2 + z % 2
    span = n * strip
    cuts = width // span

    def columns(w, odd):
        return lax.dynamic_index_in_dim(
            w.reshape(depth, n, shares, strip), share ^ odd, 2, keepdims=False
        ).reshape(depth, span)

    def second_part(odd):
        rows_down = lax.dynamic_index_in_dim(
            w_down.reshape(shares, strip, width), share ^ odd, 0, keepdims=False
        )
        return jnp.concatenate(
            [columns(w_gate, odd), columns(w_up, odd)]
            + [rows_down[:, k * span : (k + 1) * span] for k in range(cuts)],
            axis=0,
        )

    first_moved = [ring(first_part, k) for k in range(1, n)]

    def rows_out(first_part, token_part, grad_part):
        token_pieces = plane_gather(token_part)
        first_part, grad_part, *token_pieces = cut(first_part, grad_part, *token_pieces)
        grad_both = jnp.stack([grad_part, pair(grad_part)])
        return token_pieces, core(first_part), grad_both, second_part(0), second_part(1)

    token_pieces, own_far, grad_both, even_part, odd_part = together(
        rows_out, first_part, token_part, grad_part
    )
    even_part, odd_part, own_far, grad_both, *first_moved = cut(
        even_part, odd_part, own_far, grad_both, *first_moved
    )
    all_grads = lax.all_gather(grad_both, "gran", axis=0)
    first_pieces = [first_part, *first_moved]
    second_odd = {k: ring(odd_part, k) for k in range(1, n, 2)}

    all_rows = g * rows

    def unit(values):
        inverse = lax.rsqrt(jnp.mean(values * values, axis=-1, keepdims=True) + EPSILON)
        return values * inverse, inverse

    def attention(token_pieces, first_pieces, own_far):
        first_far = [own_far, *(core(v) for v in first_pieces[1:])]
        frequencies = ROPE_BASE ** (-(2.0 * jnp.arange(head // 2, dtype=F32)) / head)
        frequencies = jnp.broadcast_to(jnp.concatenate([frequencies, frequencies]), (8, head))
        all_normed, my_qkv, queries, keys, values, attended, cosines, sines, bias, gains = call(
            functools.partial(attend_kernel, n, rows, depth, mine, head),
            [
                ((all_rows, width), BF),
                ((width, 3 * mine), BF),
                ((all_rows, mine), BF),
                ((all_rows, mine), BF),
                ((all_rows, mine), BF),
                ((all_rows, mine), BF),
                ((all_rows, head), F32),
                ((all_rows, head), F32),
                ((all_rows, rows), F32),
                ((16, width), F32),
            ],
            [
                pltpu.VMEM((n, 16, mine), BF),
                pltpu.VMEM((all_rows, width), F32),
                pltpu.SemaphoreType.DMA((7 * n,)),
            ],
            "sv" + "v" * 5 + "h" * (2 * n),
            (place, frequencies, *token_pieces, *first_pieces, *first_far),
        )

        low, high = 3 * hd, 3 * hd + blocks * hs
        out_here = jnp.stack([v[low:high] for v in first_pieces])
        out_there = jnp.stack([v[low:high] for v in first_far])

        def out_part_for(r):
            picked = [
                ordered(*(lax.dynamic_index_in_dim(v, s, 0, keepdims=False) for v in (out_here, out_there)), 0)
                for s in [(z - (p ^ r) * (n // g) - j) % n for j in range(n // g)]
            ]
            return jnp.stack(picked)

        out_pieces = [out_part_for(0)] + [hop(out_part_for(r), r) for r in range(1, g)]
        if hs % 8 == 0:
            [my_out] = move(
                functools.partial(out_weight_kernel, n, g, hs, mine),
                [(mine, width)],
                n * 2 * blocks,
                (place, *out_pieces),
                "s" + "h" * g,
            )
        else:
            my_out = by_member(out_pieces).reshape(g, n // g, 2, blocks, hs, mine)
            my_out = my_out.transpose(1, 0, 2, 4, 3, 5).reshape(mine, width)
        attn_parts = call(
            functools.partial(project_kernel, rows),
            split_shapes(rows, width),
            (),
            "vv",
            (attended, my_out),
        )

        kept = (all_normed, my_qkv, my_out, queries, keys, values, attended, cosines, sines, bias)
        return kept, gains, attn_parts

    kept, gains, attn_parts = together(attention, token_pieces, first_pieces, own_far)
    even_part, *got = cut(even_part, *attn_parts, *second_odd.values())
    attn_parts, second_odd = got[:5], dict(zip(second_odd, got[5:]))
    second_even = {k: ring(even_part, k) for k in range(2, n, 2)}

    def attention_end(attn_parts, even_part, odd_parts):
        to_one, to_two, *waiting = attn_parts
        got_one, got_two, even_part, *odd_far = cut(
            hop(to_one, 1), hop(to_two, 2), even_part, *(core(v) for v in odd_parts)
        )
        reduced, own_far = cut(plane_reduce_rest(got_one, got_two, *waiting), core(even_part))
        middle = tokens.astype(F32) + summed(*reduced)
        unit_second, inverse_second = unit(middle)
        normed_ffn = (unit_second * gains[8:9]).astype(BF)
        far_rows = pair(normed_ffn)
        own_pieces = plane_gather(normed_ffn)
        return middle, unit_second, inverse_second, own_pieces, gather_first(far_rows), own_far, odd_far

    middle, unit_second, inverse_second, own_pieces, far_pieces, own_far, odd_far = together(
        attention_end, attn_parts, even_part, list(second_odd.values())
    )
    all_normed, my_qkv, my_out, queries, keys, values, attended, cosines, sines, bias = kept
    gain_first, gain_second = gains[0:1], gains[8:9]
    residual = tokens.astype(F32)
    *got, all_grads = cut(*own_pieces, *far_pieces, *second_even.values(), all_grads)
    own_pieces, far_pieces, second_even = got[:5], got[5:8], dict(zip(second_even, got[8:]))
    odd_far = dict(zip(second_odd, odd_far))
    even_far = {k: core(v) for k, v in second_even.items()}
    second_here = {0: even_part, **second_odd, **second_even}
    second_far = {0: own_far, **odd_far, **even_far}
    second_here = [second_here[k] for k in range(n)]
    second_far = [second_far[k] for k in range(n)]

    index = jnp.arange(2 * span, dtype=jnp.int32) % span
    unit_index = (index // strip) * (strip * shares) + share * strip + index % strip
    fast_units = strip % 16 == 0

    def feed_forward(e, row_pieces):
        if fast_units:
            shapes = split_shapes(rows, width) * 2
            shapes += [((all_rows, width), BF)] * 2
            shapes += [((all_rows, 2 * span), BF), ((all_rows, 4 * span), BF)]
            got = call(
                functools.partial(feed_forward_kernel, n, g, depth, strip, rows, e),
                shapes,
                [pltpu.VMEM(*v) for v in shapes]
                + [
                    pltpu.VMEM((width, 2 * span), BF),
                    pltpu.VMEM((width, 2 * span), BF),
                    pltpu.VMEM((2 * span, width), BF),
                    pltpu.VMEM((g, 16, rows), BF),
                    pltpu.SemaphoreType.DMA((5 + 2 * n * (2 + cuts) + 2 * g,)),
                    pltpu.SemaphoreType.DMA((14,)),
                ],
                "sv" + "h" * (6 + 2 * n),
                (
                    place,
                    jnp.broadcast_to(unit_index.astype(F32), (8, 2 * span)),
                    *row_pieces,
                    all_grads,
                    *second_here,
                    *second_far,
                ),
                out="h",
                spare=16,
            )
            return got[:5], got[5:10], got[10:]
        group_rows = jnp.concatenate(row_pieces, axis=0)
        stacks = []
        for pieces in (second_here, second_far):
            out = jnp.zeros((n, *pieces[0].shape), BF)
            for k in range(n):
                out = lax.dynamic_update_index_in_dim(out, pieces[k], (z - k) % n, 0)
            stacks.append(out)
        gate_matrix, up_matrix = (
            jnp.concatenate(
                [v[:, k * depth : (k + 1) * depth].reshape(width, span) for v in stacks], axis=1
            )
            for k in (0, 1)
        )
        down_matrix = jnp.concatenate(
            [v[:, 2 * depth :].reshape(n, cuts, strip, span).transpose(0, 2, 1, 3) for v in stacks],
            axis=0,
        ).reshape(2 * span, width)
        grad_got = jnp.stack(
            [lax.dynamic_index_in_dim(all_grads, p ^ r, 0, keepdims=False)[e] for r in range(g)]
        )
        group_grads = grad_got[:, :rows].reshape(all_rows, width)
        group_codes = grad_got[:, rows, :rows].reshape(all_rows, 1).astype(jnp.int32)
        group_limits = jnp.where(
            group_codes < 0, 0, jnp.right_shift(jnp.int32(units), jnp.minimum(3 - group_codes, 3))
        )
        live = unit_index[None, :] < group_limits
        gate_pre = dot(group_rows, gate_matrix)
        lifted = dot(group_rows, up_matrix)
        sigmoid_gate = jax.nn.sigmoid(gate_pre)
        activated = gate_pre * sigmoid_gate
        hidden = jnp.where(live, (activated * lifted).astype(BF), jnp.zeros((), BF))
        grad_hidden = jnp.where(live, contract_cols(group_grads, down_matrix), 0.0)
        grad_gate = (
            grad_hidden * lifted * sigmoid_gate * (1.0 + gate_pre * (1.0 - sigmoid_gate))
        ).astype(BF)
        grad_lifted = (grad_hidden * activated).astype(BF)
        partial_input = (
            contract_cols(grad_gate, gate_matrix) + contract_cols(grad_lifted, up_matrix)
        ).astype(BF)
        partial_ffn = dot(hidden, down_matrix).astype(BF)
        return (
            list(split_rows(partial_input.reshape(g, rows, width))),
            list(split_rows(partial_ffn.reshape(g, rows, width))),
            [group_rows, group_grads, hidden, jnp.concatenate([grad_gate, grad_lifted], axis=1)],
        )

    def unit_grads(own, far):
        if fast_units:
            return call(
                functools.partial(unit_sums_kernel, n, depth, strip),
                [((n, 2 * depth + cuts * strip, span), BF)] * 2,
                [pltpu.VMEM(v.shape, BF) for v in (*own, *far)]
                + [pltpu.VMEM((n, 2 * depth + cuts * strip, span), BF)] * 2
                + [pltpu.SemaphoreType.DMA((8,)), pltpu.SemaphoreType.DMA((4 * n,))],
                "h" * 8,
                (*own, *far),
                out="h",
                spare=16,
            )
        group_rows, group_grads, hidden, grads_two = (
            jnp.concatenate([v, w], axis=0) for v, w in zip(own, far)
        )

        def half_grads(half):
            low = slice(half * span, (half + 1) * span)
            made = contract_rows(hidden[:, low], group_grads).astype(BF)
            made = made.reshape(n, strip, cuts, span).transpose(0, 2, 1, 3)
            return jnp.concatenate(
                [
                    contract_rows(group_rows, v[:, low]).astype(BF).reshape(n, depth, span)
                    for v in (grads_two[:, : 2 * span], grads_two[:, 2 * span :])
                ]
                + [made.reshape(n, cuts * strip, span)],
                axis=1,
            )

        return [half_grads(0), half_grads(1)]

    far_pieces = gather_rest(list(far_pieces))
    own_out = together(functools.partial(feed_forward, 0), own_pieces)
    (own_input, own_ffn, own_saved), far_pieces = cut(own_out, far_pieces)
    to_one, to_two, *own_waiting = own_input
    own_got, (far_input, far_ffn, far_saved) = cut(
        (hop(to_one, 1), hop(to_two, 2)), together(functools.partial(feed_forward, 1), far_pieces)
    )
    to_one, to_two, *far_waiting = far_input
    own_half, far_got, (sums_here, sums_there) = cut(
        plane_reduce_rest(*own_got, *own_waiting),
        (hop(to_one, 1), hop(to_two, 2)),
        together(unit_grads, own_saved, far_saved),
    )
    far_sum, far_sums = cut(plane_reduce_rest(*far_got, *far_waiting), core(sums_there))
    far_sum = summed(*far_sum)

    def unit_sums(k):
        here, there = (
            lax.dynamic_index_in_dim(v, k, 0, keepdims=False).astype(F32)
            for v in (sums_here, far_sums)
        )
        return (here + there).astype(BF)

    def mixed(own, far):
        half = own.shape[0] // 2
        return jnp.concatenate([own[:half], far[:half], own[half:], far[half:]], axis=0)

    far_half = pair(far_sum.astype(BF))
    to_one, to_two, branch_own = (mixed(v, w) for v, w in zip(own_ffn[:3], far_ffn[:3]))
    branch_waiting = [branch_own] + [
        jnp.concatenate([v, w], axis=0) for v, w in zip(own_ffn[3:], far_ffn[3:])
    ]
    to_one, to_two = cut(to_one, to_two, far_sum)[:2]
    branch_got = hop(to_one, 1), hop(to_two, 2)
    messages = [unit_sums((z + k) % n) for k in range(n)]
    far_half, *messages = cut(far_half, *messages)
    sums = [messages[0].astype(F32), 0.0]
    moved = [ring(messages[k], k) for k in range(1, n)]

    def my_half(x, which, axis):
        return lax.dynamic_index_in_dim(x, which, axis, keepdims=False)

    def for_member(stacked, r, axis):
        return lax.dynamic_index_in_dim(stacked, p ^ r, axis, keepdims=False)

    def attention_back(own_half, far_half, branch_got):
        grad_normed_ffn = (summed(*own_half) + far_half.astype(F32)).astype(BF).astype(F32)
        grad_middle = out_cotangent.astype(F32) + norm_back(
            grad_normed_ffn, unit_second, inverse_second, gain_second
        )
        branch_pieces = plane_gather(grad_middle.astype(BF))
        fast = n == g and hs % 16 == 0
        if fast:
            branch_rows = jnp.concatenate(branch_pieces, axis=0)
            out_here, out_there = call(
                functools.partial(out_sums_kernel, g, hs, mine),
                [((g, blocks * hs, mine), BF)] * 2,
                [pltpu.VMEM((mine, mine), F32)],
                "svv",
                (place, attended, branch_rows),
            )
            out_there, *branch_pieces = cut(core(out_there), *branch_pieces)
            out_sum = (out_here.astype(F32) + out_there.astype(F32)).astype(BF)
        got_one, got_two, *branch_pieces = cut(*branch_got, *branch_pieces)
        branch_sum = plane_reduce_rest(got_one, got_two, *branch_waiting)
        grad_branch, grad_packed, *normed_parts = call(
            functools.partial(attend_back_kernel, rows, mine, head),
            [((all_rows, width), BF), ((all_rows, 3 * mine), BF), *split_shapes(rows, width)],
            [pltpu.VMEM((all_rows, mine), BF)],
            "v" * 13,
            (*branch_pieces, my_out, my_qkv, queries, keys, values, cosines, sines, bias),
        )
        branch_sum, grad_packed = cut(branch_sum, grad_packed)
        if fast:
            quarters = [hop(for_member(after(out_sum, grad_packed), r, 0), r) for r in (1, 2)]
            sum_here, sum_there = call(
                functools.partial(weight_sums_kernel, g, depth, mine),
                [((g, 3 * hd, mine), BF)] * 2,
                [pltpu.VMEM((depth, 3 * mine), F32)],
                "svv",
                (place, all_normed, grad_packed),
            )
            sum_there, out_sum, *quarters = cut(sum_there, out_sum, *quarters)
            quarters.append(hop(for_member(out_sum, 3, 0), 3))
            weight_sum = (sum_here.astype(F32) + core(sum_there).astype(F32)).astype(BF)
            last_parts = call(
                functools.partial(last_parts_kernel, g, 3 * hd),
                [((3 * hd + blocks * hs, mine), BF)] * g,
                [pltpu.VMEM((g, blocks * hs, mine), BF)],
                "s" + "v" * (g + 1),
                (place, weight_sum, for_member(out_sum, 0, 0), *quarters),
            )
        else:
            out_grad = contract_rows(attended, grad_branch).astype(BF)
            out_grad = out_grad.reshape(n // g, g, 2, hs, width)
            out_sum = my_half(out_grad, c, 2).astype(F32)
            out_sum = (out_sum + core(my_half(out_grad, 1 - c, 2)).astype(F32)).astype(BF)
            out_sum = by_member(
                [for_member(out_sum, 0, 1)]
                + [hop(for_member(out_sum, r, 1), r) for r in range(1, g)]
            ).reshape(n, hs, blocks, mine)
            qkv_grad = contract_rows(all_normed, grad_packed).astype(BF).reshape(n, 2, hd, 3, mine)
            qkv_sum = my_half(qkv_grad, c, 1).astype(F32)
            qkv_sum += core(my_half(qkv_grad, 1 - c, 1)).astype(F32)
            last_part = jnp.concatenate(
                [
                    qkv_sum.astype(BF).transpose(0, 2, 1, 3).reshape(n, 3 * hd, mine),
                    out_sum.transpose(0, 2, 1, 3).reshape(n, blocks * hs, mine),
                ],
                axis=1,
            )
            last_parts = [
                lax.dynamic_index_in_dim(last_part, (z + k) % n, 0, keepdims=False) for k in range(n)
            ]
        normed_parts = cut(*normed_parts, *last_parts)[:5]
        grad_normed = plane_reduce(*normed_parts)
        unit_first, inverse_first = unit(residual)
        input_grad = (
            grad_middle + norm_back(grad_normed, unit_first, inverse_first, gain_first)
        ).astype(BF)
        return input_grad, last_parts, branch_sum

    input_grad, last_parts, branch_sum = together(
        attention_back, own_half, far_half, branch_got
    )
    cut_values = cut(*moved, *last_parts)
    moved, last_parts = cut_values[: n - 1], cut_values[n - 1 :]
    for k in range(1, n):
        sums[k % 2] += moved[k - 1].astype(F32)
    pair_sums = jnp.concatenate([v.astype(BF) for v in sums], axis=0)
    last_moved = [ring(last_parts[k], k) for k in range(1, n)]

    unit_pieces = together(plane_gather, pair_sums)
    got = cut(*unit_pieces, *last_moved)
    unit_pieces, last_moved = got[:5], got[5:]
    last_sum = last_parts[0].astype(F32) + sum(v.astype(F32) for v in last_moved)
    last_one = gather_first(last_sum.astype(BF))
    if strip % 32 == 0:
        share_gate, share_up, ffn_part = call(
            functools.partial(columns_results_kernel, n, g, depth, strip, 2 * depth + cuts * strip),
            [
                ((depth * units // 128, 128), F32),
                ((depth * units // 128, 128), F32),
                ((depth, 1), F32),
            ],
            [
                pltpu.VMEM((shares, depth, span), BF),
                pltpu.VMEM((shares, depth, span), BF),
                pltpu.SemaphoreType.DMA((2, shares)),
            ],
            "s" + "h" * 5 + "vv",
            (place, *unit_pieces, w_gate[:, 0], w_up[:, 0]),
        )
        ffn_part = ffn_part[:, 0]
    else:
        got = as_members(unit_pieces).reshape(g, 2, -1, span)
        all_units = jnp.zeros((shares, *got.shape[2:]), BF)
        for r in range(g):
            for odd in (0, 1):
                all_units = lax.dynamic_update_index_in_dim(
                    all_units, got[r, odd], (p ^ r) * 2 + (z % 2) ^ odd, 0
                )

        def columns_back(pieces):
            return (
                pieces.reshape(shares, depth, n, strip)
                .transpose(1, 2, 0, 3)
                .reshape(depth, units)
                .astype(F32)
            )

        share_gate = columns_back(all_units[:, :depth])
        share_up = columns_back(all_units[:, depth : 2 * depth])
        share_down = (
            all_units[:, 2 * depth :]
            .reshape(shares, cuts, strip, span)
            .transpose(0, 2, 1, 3)
            .reshape(units // n, width)
            .astype(F32)
        )
        ffn_part = jnp.sum(
            share_gate * w_gate[:, 0].astype(F32) + share_up * w_up[:, 0].astype(F32), axis=1
        )
    *last_one, ffn_part = cut(*last_one, ffn_part)
    last_pieces = gather_rest(last_one)
    if strip % 32 == 0:
        [share_down] = call(
            functools.partial(rows_results_kernel, n, g, depth, strip, 2 * depth + cuts * strip),
            [((units // n * width // 128, 128), F32)],
            [pltpu.VMEM((shares, cuts * strip, span), BF), pltpu.SemaphoreType.DMA((shares,))],
            "s" + "h" * 5,
            (place, *cut(*unit_pieces, ffn_part)[:5]),
        )
        *last_rest, share_down = cut(*last_pieces[3:], share_down)
        last_pieces[3:] = last_rest
    share_gain_ffn = (ffn_part + core(ffn_part)) / gain_ffn.astype(F32)
    branch_sum = summed(*branch_sum).reshape(2, 2, rows // 2, width)
    branch_ffn, branch_far = (branch_sum[:, k].reshape(rows, width) for k in (0, 1))
    branch_ffn += pair(branch_far.astype(BF)).astype(F32)
    outputs = (middle + branch_ffn.astype(BF).astype(F32)).astype(BF)
    if hs % 16 == 0:
        share_qkv, share_out, attn_part = call(
            functools.partial(attention_results_kernel, g, depth, mine),
            [((depth, 3 * width), F32), ((depth, width), F32), ((depth, 1), F32)],
            [
                pltpu.VMEM((depth, 3 * width), BF),
                pltpu.VMEM((depth, width), BF),
                pltpu.SemaphoreType.DMA((2 * (g + 1) * (3 + blocks),)),
            ],
            "s" + "h" * 10 + "v",
            (place, *last_pieces, *(core(v) for v in last_pieces), w_qkv),
        )
        attn_part = attn_part[:, 0]
    else:
        last_got = as_members(last_pieces)
        last_got = by_member([last_got[r] for r in range(g)])
        last_both = ordered(last_got, core(last_got), 0)
        share_qkv = (
            last_both[:, :, : 3 * hd]
            .reshape(2, g, 3, hd, mine)
            .transpose(0, 3, 2, 1, 4)
            .reshape(depth, 3 * width)
            .astype(F32)
        )
        share_out = (
            last_both[:, :, 3 * hd :]
            .reshape(2, g, blocks, hs, mine)
            .transpose(1, 0, 3, 2, 4)
            .reshape(depth, width)
            .astype(F32)
        )
        attn_part = jnp.sum(share_qkv * w_qkv.astype(F32), axis=1)
    share_gain_attn = attn_part / gain_attn.astype(F32)
    return (
        outputs,
        input_grad,
        share_qkv,
        share_out,
        share_gain_attn,
        share_gain_ffn,
        share_gate.reshape(depth, 1, units),
        share_up.reshape(depth, 1, units),
        share_down.reshape(units // n, 1, width),
    )


def solution(mesh):
    in_specs = (
        P(("batch", "gran", "ffn"), None),
        P(("batch", "gran", "ffn")),
        P(("batch", "gran", "ffn")),
        P("batch", None),
        P("batch", None),
        P("batch"),
        P("batch"),
        P("batch", "ffn", None),
        P("batch", "ffn", None),
        P("batch", "ffn", None),
        P(("batch", "gran", "ffn"), None),
    )
    out_specs = (
        P(("batch", "gran", "ffn"), None),
        P(("batch", "gran", "ffn"), None),
        P("batch", None),
        P("batch", None),
        P("batch"),
        P("batch"),
        P("batch", "ffn", None),
        P("batch", "ffn", None),
        P("batch", "ffn", None),
    )
    return jax.shard_map(local, mesh=mesh, in_specs=in_specs, out_specs=out_specs, check_vma=False)
```

```python
import functools
import math

import jax
import jax.numpy as jnp
from jax import lax
from jax.experimental import pallas as pl
from jax.experimental.pallas import tpu as pltpu
from jax.sharding import PartitionSpec as P

H = 12


EPSILON = 1e-06
NEG_FILL = -1e30
ROPE_BASE = 10000.0
BF = jnp.bfloat16
F32 = jnp.float32


def row_groups(seq_rows, seq_groups, kept_rows):
    labels = jnp.arange(seq_groups.shape[0], dtype=jnp.int32)
    member = (seq_rows[:, None] == labels[None, :]).astype(jnp.int32)
    group_id = jnp.sum(member * seq_groups[None, :], axis=1)
    index = jnp.arange(seq_rows.shape[0], dtype=jnp.int32)
    earlier = (group_id[None, :] == group_id[:, None]) & (index[None, :] < index[:, None])
    rank = jnp.sum(earlier.astype(jnp.int32), axis=1)
    return jnp.where(rank < kept_rows, group_id, -1)


def dot(left, right):
    return jnp.dot(left, right, preferred_element_type=F32)


def contract_rows(left, right):
    return lax.dot_general(left, right, (((0,), (0,)), ((), ())), preferred_element_type=F32)


def contract_cols(left, right):
    return lax.dot_general(left, right, (((1,), (1,)), ((), ())), preferred_element_type=F32)


def norm_back(grad_normed, unit_rows, inverse_rms, gain):
    scaled = grad_normed * gain
    return inverse_rms * (scaled - unit_rows * jnp.mean(scaled * unit_rows, axis=-1, keepdims=True))


def first_rows(values, count, width):
    return jnp.pad(values.astype(BF)[None, :], ((0, count - 1), (0, width - values.shape[0])))


def after(value, *others):
    return lax.optimization_barrier((value, *others))[0]


def small_cost():
    return pl.CostEstimate(flops=1, bytes_accessed=1, transcendentals=0)


def call(kernel, outs, scratch=(), ins=(), operands=(), out="v", spare=8):
    held = [v for k, v in zip(ins, operands) if k == "v"]
    held += [jax.ShapeDtypeStruct(*v) for v in outs if out == "v"]
    held += [v for v in scratch if v.dtype in (BF, F32)]
    limit = sum(math.prod(v.shape) * v.dtype.itemsize for v in held) + spare * 2**20
    kinds = {
        "v": pl.BlockSpec(memory_space=pltpu.VMEM),
        "h": pl.BlockSpec(memory_space=pl.ANY),
        "s": pl.BlockSpec(memory_space=pltpu.SMEM),
    }
    return pl.pallas_call(
        kernel,
        out_shape=[jax.ShapeDtypeStruct(shape, dtype) for shape, dtype in outs],
        in_specs=[kinds[k] for k in ins],
        out_specs=[kinds[out]] * len(outs),
        scratch_shapes=list(scratch),
        compiler_params=pltpu.CompilerParams(vmem_limit_bytes=limit),
        cost_estimate=small_cost(),
    )(*operands)


def split_parts(value, rows, to_one, to_two, own, two_low, one_high):
    half = rows // 2
    to_one[:half] = value[rows : rows + half].astype(BF)
    to_one[half:] = value[3 * rows : 3 * rows + half].astype(BF)
    to_two[:half] = value[2 * rows + half : 3 * rows].astype(BF)
    to_two[half:] = value[3 * rows + half :].astype(BF)
    own[...] = value[:rows]
    two_low[...] = value[2 * rows : 2 * rows + half].astype(BF)
    one_high[...] = value[rows + half : 2 * rows].astype(BF)


def split_shapes(rows, width):
    half = rows // 2
    return [
        ((rows, width), BF),
        ((rows, width), BF),
        ((rows, width), F32),
        ((half, width), BF),
        ((half, width), BF),
    ]


def reduce_first_kernel(got_one, got_two, own, two_low, one_high, to_two, to_one, total):
    half = two_low.shape[0]
    to_two[...] = (two_low[...].astype(F32) + got_one[half:].astype(F32)).astype(BF)
    to_one[...] = (one_high[...].astype(F32) + got_two[half:].astype(F32)).astype(BF)
    total[:half] = own[:half].astype(F32) + got_one[:half].astype(F32)
    total[half:] = own[half:].astype(F32) + got_two[:half].astype(F32)


def attend_kernel(n, rows, depth, mine, head, place, freq, *refs):
    tokens, refs = refs[:5], refs[5:]
    here, there, refs = refs[:n], refs[n : 2 * n], refs[2 * n :]
    normed, weight, queries, keys, values, attended, cosines, sines, bias, gains = refs[:10]
    gain_rows, unit_rows, sems = refs[10:]
    z, c = place[0], place[2]
    hd = depth // 2
    width = n * depth
    copies = []
    for s in range(n):
        plane = lax.rem(z - s + n, n)
        for which, pieces in ((c, here), (1 - c, there)):
            start = pl.multiple_of(plane * depth + which * hd, 8)
            for k in range(3):
                copies.append(
                    pltpu.make_async_copy(
                        pieces[s].at[pl.ds(k * hd, hd), :],
                        weight.at[pl.ds(start, hd), pl.ds(k * mine, mine)],
                        sems.at[len(copies)],
                    )
                )
        copies.append(
            pltpu.make_async_copy(
                here[s].at[pl.ds(here[s].shape[0] - 16, 16), :], gain_rows.at[plane], sems.at[len(copies)]
            )
        )
    for copy in copies:
        copy.start()

    half = rows // 2
    third = tokens[3].shape[0]
    spans = [(tokens[0], 0, 0, rows), (tokens[1], 0, rows, rows), (tokens[2], 0, 2 * rows, rows)]
    spans += [(tokens[3], 0, 3 * rows, third), (tokens[4], 0, 3 * rows + third, rows - third)]
    for ref, low, at, count in spans:
        x = ref[low : low + count, :].astype(F32)
        inverse = lax.rsqrt(jnp.mean(x * x, axis=-1, keepdims=True) + EPSILON)
        unit_rows[at : at + count] = x * inverse

    row = lax.broadcasted_iota(jnp.int32, (rows, rows), 0)
    col = lax.broadcasted_iota(jnp.int32, (rows, rows), 1)
    lane = lax.broadcasted_iota(jnp.int32, (rows, head), 1)
    sign = jnp.where(lane < head // 2, -1.0, 1.0)
    for b in range(4):
        ref, low = (tokens[b], rows) if b < 3 else (tokens[4], rows - third)
        ids = ref[low : low + 8, :rows].astype(F32)[:1]
        ids_row = jnp.broadcast_to(ids, (rows, rows))
        ids_col = jnp.sum(jnp.where(row == col, ids_row, 0.0), axis=1, keepdims=True)
        before = jnp.sum(jnp.where(ids_row < ids_col, 1.0, 0.0), axis=1, keepdims=True)
        positions = row[:, :1].astype(F32) - before
        angles = positions * freq[:1, :]
        cosines[b * rows : (b + 1) * rows] = jnp.cos(angles)
        sines[b * rows : (b + 1) * rows] = jnp.sin(angles) * sign
        bias[b * rows : (b + 1) * rows] = jnp.where(
            (ids_row == ids_col) & (row >= col), 0.0, NEG_FILL
        )

    for copy in copies:
        copy.wait()
    for k in range(n):
        block = slice(k * depth, (k + 1) * depth)
        both = gain_rows[k].astype(F32)
        gains[0:8, block] = jnp.broadcast_to(both[0:1, :depth], (8, depth))
        gains[8:16, block] = jnp.broadcast_to(both[8:9, :depth], (8, depth))
    normed[...] = (unit_rows[...] * gains[0:1, :]).astype(BF)
    x = normed[...]
    cos, sin = cosines[...], sines[...]
    scale = 1.0 / math.sqrt(head)
    for k, out in enumerate((queries, keys, values)):
        packed = dot(x, weight[:, k * mine : (k + 1) * mine])
        for h in range(mine // head):
            part = packed[:, h * head : (h + 1) * head]
            if k < 2:
                part = part * cos + pltpu.roll(part, head // 2, 1) * sin
            if k == 0:
                part = part * scale
            out[:, h * head : (h + 1) * head] = part.astype(BF)
    for b in range(4):
        for h in range(mine // head):
            here_rows, here_cols = slice(b * rows, (b + 1) * rows), slice(h * head, (h + 1) * head)
            scores = contract_cols(queries[here_rows, here_cols], keys[here_rows, here_cols])
            probs = softmax(scores + bias[here_rows])
            attended[here_rows, here_cols] = dot(
                probs.astype(BF), values[here_rows, here_cols]
            ).astype(BF)


def softmax(scores):
    exponent = jnp.exp(scores - jnp.max(scores, axis=-1, keepdims=True))
    return exponent / jnp.sum(exponent, axis=-1, keepdims=True)


def project_kernel(rows, attended, out, *parts):
    split_parts(dot(attended[...], out[...]), rows, *parts)


def attend_back_kernel(rows, mine, head, *refs):
    grads, refs = refs[:5], refs[5:]
    out, weight, queries, keys, values, cosines, sines, bias = refs[:8]
    branch, packed, *parts = refs[8:-1]
    attended_grad = refs[-1]
    third = grads[3].shape[0]
    at = 0
    for ref in grads:
        branch[at : at + ref.shape[0]] = ref[...]
        at += ref.shape[0]
    del third
    attended_grad[...] = contract_cols(branch[...], out[...]).astype(BF)
    scale = 1.0 / math.sqrt(head)
    for b in range(4):
        r = slice(b * rows, (b + 1) * rows)
        cos, sin = cosines[r], sines[r]
        for h in range(mine // head):
            cols = slice(h * head, (h + 1) * head)
            q, k, v, grad = queries[r, cols], keys[r, cols], values[r, cols], attended_grad[r, cols]
            probs = softmax(contract_cols(q, k) + bias[r])
            grad_probs = contract_cols(grad, v)
            grad_scores = probs * (
                grad_probs - jnp.sum(probs * grad_probs, axis=-1, keepdims=True)
            )
            grad_scores = grad_scores.astype(BF)
            grad_q = dot(grad_scores, k).astype(BF).astype(F32) * scale
            grad_k = contract_rows(grad_scores, q).astype(BF).astype(F32)
            grad_v = contract_rows(probs.astype(BF), grad)
            for j, part in enumerate((grad_q, grad_k, grad_v)):
                if j < 2:
                    part = part * cos - pltpu.roll(part, head // 2, 1) * sin
                packed[r, j * mine + h * head : j * mine + (h + 1) * head] = part.astype(BF)
    split_parts(contract_cols(packed[...], weight[...]), rows, *parts)


def first_part_kernel(depth, mine, members, place, w_qkv, w_out, gains, out, sems):
    p, c = place[1], place[2]
    hd, hs = depth // 2, depth // members // 2
    width = w_out.shape[1]
    moves = []
    for k in range(3):
        column = pl.multiple_of(k * width + p * mine, 128)
        moves.append((w_qkv.at[pl.ds(c * hd, hd), pl.ds(column, mine)], k * hd, hd))
    top = pl.multiple_of((p * 2 + c) * hs, 8)
    for k in range(width // mine):
        block = w_out.at[pl.ds(top, hs), pl.ds(k * mine, mine)]
        moves.append((block, 3 * hd + k * hs, hs))
    moves.append((gains, out.shape[0] - 16, 16))
    copies = [
        pltpu.make_async_copy(source, out.at[pl.ds(at, count), :], sems.at[i])
        for i, (source, at, count) in enumerate(moves)
    ]
    for copy in copies:
        copy.start()
    for copy in copies:
        copy.wait()


def out_weight_kernel(n, members, hs, mine, place, *refs):
    pieces, out, sems = refs[:members], refs[members], refs[members + 1]
    p = place[1]
    copies = []
    for r in range(members):
        for j in range(n // members):
            for half in range(2):
                top = pl.multiple_of(((j * members + (p ^ r)) * 2 + half) * hs, 8)
                for k in range(out.shape[1] // mine):
                    copies.append(
                        pltpu.make_async_copy(
                            pieces[r].at[j, half, pl.ds(k * hs, hs), :],
                            out.at[pl.ds(top, hs), pl.ds(k * mine, mine)],
                            sems.at[len(copies)],
                        )
                    )
    for copy in copies:
        copy.start()
    for copy in copies:
        copy.wait()


def strips_of(tile, strip):
    at, out = 0, []
    while at < 128:
        share, first = divmod(tile * 128 + at, strip)
        count = min(strip - first, 128 - at)
        out.append((share, first, at, count))
        at += count
    return out


def fetch_shares(members, rows, low, count, place, pieces, target, sems):
    z, p = place[0], place[1]
    copies = []
    for r in range(members):
        for odd in range(2):
            share = (p ^ r) * 2 + (lax.rem(z, 2) ^ odd)
            ref, top = (pieces[r], odd * rows + low) if r < 3 else (pieces[3 + odd], low)
            copy = pltpu.make_async_copy(
                ref.at[pl.ds(top, count), :], target.at[share], sems.at[len(copies)]
            )
            copy.start()
            copies.append(copy)
    return copies


def columns_results_kernel(n, members, depth, strip, rows, place, *refs):
    pieces, w_gate, w_up = refs[:5], refs[5], refs[6]
    gate, up, gain, held_gate, held_up, sems = refs[7:]
    shares = 2 * members
    copies = [
        fetch_shares(members, rows, k * depth, depth, place, pieces, held, sems.at[k])
        for k, held in enumerate((held_gate, held_up))
    ]
    lanes = lax.broadcasted_iota(jnp.int32, (depth, 128), 1)
    row_tiles = n * shares * strip // 128
    total = jnp.zeros((depth, 128), F32)
    for which, (out, held, weight) in enumerate(
        ((gate, held_gate, w_gate), (up, held_up, w_up))
    ):
        for copy in copies[which]:
            copy.wait()
        for k in range(n):
            for tile in range(shares * strip // 128):
                made = jnp.zeros((depth, 128), F32)
                for share, first, lane, count in strips_of(tile, strip):
                    column = k * strip + first
                    while count > 0:
                        source, offset = divmod(column, 128)
                        some = min(count, 128 - offset)
                        value = held[share, :, source * 128 : (source + 1) * 128].astype(F32)
                        if lane != offset:
                            value = pltpu.roll(value, (lane - offset) % 128, 1)
                        made = jnp.where((lanes >= lane) & (lanes < lane + some), value, made)
                        column, lane, count = column + some, lane + some, count - some
                at = k * (shares * strip // 128) + tile
                out[pl.ds(at, depth, stride=row_tiles), :] = made
                total += made * weight[:, at * 128 : (at + 1) * 128].astype(F32)
    gain[...] = jnp.sum(total, axis=1, keepdims=True)


def rows_results_kernel(n, members, depth, strip, rows, place, *refs):
    pieces, down, held, sems = refs[:5], refs[5], refs[6], refs[7]
    span, cuts = n * strip, (rows - 2 * depth) // strip
    copies = fetch_shares(members, rows, 2 * depth, cuts * strip, place, pieces, held, sems)
    for copy in copies:
        copy.wait()
    wide = cuts * span // 128
    for share in range(2 * members):
        for k in range(cuts):
            for tile in range(span // 128):
                block = slice(k * strip, (k + 1) * strip), slice(tile * 128, (tile + 1) * 128)
                start = share * strip * wide + k * (span // 128) + tile
                down[pl.ds(start, strip, stride=wide), :] = held[(share, *block)].astype(F32)


def attention_results_kernel(members, depth, mine, place, *refs):
    here, there, w_qkv = refs[:5], refs[5:10], refs[10]
    qkv, out, gain, held, held_out, sems = refs[11:]
    p, c = place[1], place[2]
    hd, hs = depth // 2, depth // members // 2
    width = held_out.shape[1]
    blocks = width // mine
    copies = []

    def add(source, target):
        copies.append(pltpu.make_async_copy(source, target, sems.at[len(copies)]))

    def place_rows(ref, first, low, count, r, half):
        for k in range(3):
            top, end = max(low, k * hd), min(low + count, (k + 1) * hd)
            if top < end:
                add(
                    ref.at[pl.ds(first + top - low, end - top), :],
                    held.at[
                        pl.ds(pl.multiple_of(half * hd + top - k * hd, 8), end - top),
                        pl.ds(pl.multiple_of(k * width + (p ^ r) * mine, 128), mine),
                    ],
                )
        for k in range(blocks):
            base = 3 * hd + k * hs
            top, end = max(low, base), min(low + count, base + hs)
            if top < end:
                add(
                    ref.at[pl.ds(first + top - low, end - top), :],
                    held_out.at[
                        pl.ds(pl.multiple_of(((p ^ r) * 2 + half) * hs + top - base, 8), end - top),
                        pl.ds(k * mine, mine),
                    ],
                )

    rows = 3 * hd + blocks * hs
    for half, pieces in ((c, here), (1 - c, there)):
        for r in range(3):
            place_rows(pieces[r], 0, 0, rows, r, half)
        third = pieces[3].shape[0]
        place_rows(pieces[3], 0, 0, third, 3, half)
        place_rows(pieces[4], 0, third, rows - third, 3, half)
    for copy in copies:
        copy.start()
    for copy in copies:
        copy.wait()
    total = jnp.zeros((depth, 128), F32)
    for tile in range(3 * width // 128):
        cols = slice(tile * 128, (tile + 1) * 128)
        value = held[:, cols].astype(F32)
        qkv[:, cols] = value
        total += value * w_qkv[:, cols].astype(F32)
    gain[...] = jnp.sum(total, axis=1, keepdims=True)
    out[...] = held_out[...].astype(F32)


def out_sums_kernel(members, hs, mine, place, attended, branch, mine_out, theirs_out, held):
    c = place[2]
    for k in range(branch.shape[1] // mine):
        cols = slice(k * mine, (k + 1) * mine)
        held[...] = contract_rows(attended[...], branch[:, cols])
        for out, half in ((mine_out, c), (theirs_out, 1 - c)):
            for quarter in range(members):
                start = pl.multiple_of((quarter * 2 + half) * hs, 8)
                value = held[pl.ds(start, hs), :]
                out[quarter, k * hs : (k + 1) * hs, :] = value.astype(BF)


def weight_sums_kernel(members, depth, mine, place, normed, packed, mine_out, theirs_out, held):
    c = place[2]
    hd = depth // 2
    for plane in range(members):
        block = slice(plane * depth, (plane + 1) * depth)
        held[...] = contract_rows(normed[:, block], packed[...])
        for out, half in ((mine_out, c), (theirs_out, 1 - c)):
            start = pl.multiple_of(half * hd, 8)
            for k in range(3):
                value = held[pl.ds(start, hd), k * mine : (k + 1) * mine]
                out[plane, k * hd : (k + 1) * hd, :] = value.astype(BF)


def last_parts_kernel(members, low, place, *refs):
    sums, quarters, outs, held = refs[0], refs[1 : members + 1], refs[members + 1 : -1], refs[-1]
    z, p = place[0], place[1]
    for r in range(members):
        held[r] = quarters[r][...]
    for k in range(members):
        plane = lax.rem(z + k, members)
        outs[k][:low] = sums[plane]
        outs[k][low:] = held[p ^ plane]


def feed_forward_kernel(n, members, depth, strip, rows, e, place, unit_index, *refs):
    pieces, all_grads, refs = refs[:5], refs[5], refs[6:]
    here, there, refs = refs[:n], refs[n : 2 * n], refs[2 * n :]
    outs, scratch = refs[:14], refs[14:28]
    splits, (x, cot, hidden, grads_two) = scratch[:10], scratch[10:]
    gate, up, down, codes, in_sems, out_sems = refs[28:]
    z, p = place[0], place[1]
    span = n * strip
    units = span * 2 * members
    started, finishing = [], []

    def fetch(source, target):
        copy = pltpu.make_async_copy(source, target, in_sems.at[len(started)])
        copy.start()
        started.append(copy)

    def flush(index):
        copy = pltpu.make_async_copy(scratch[index], outs[index], out_sems.at[index])
        copy.start()
        finishing.append(copy)

    at = 0
    for ref in pieces:
        fetch(ref, x.at[pl.ds(at, ref.shape[0]), :])
        at += ref.shape[0]
    for s in range(n):
        plane = lax.rem(z - s + n, n)
        top = pl.multiple_of(plane * depth, 8)
        for half, parts in enumerate((here, there)):
            columns = pl.ds(half * span, span)
            fetch(parts[s].at[pl.ds(0, depth), :], gate.at[pl.ds(top, depth), columns])
            fetch(parts[s].at[pl.ds(depth, depth), :], up.at[pl.ds(top, depth), columns])
    first = len(started)
    for r in range(members):
        fetch(all_grads.at[p ^ r, e, pl.ds(0, rows), :], cot.at[pl.ds(r * rows, rows), :])
        fetch(all_grads.at[p ^ r, e, pl.ds(rows, 16), pl.ds(0, rows)], codes.at[r])
    for s in range(n):
        plane = lax.rem(z - s + n, n)
        for half, parts in enumerate((here, there)):
            start = pl.multiple_of(half * span + plane * strip, 8)
            for j in range(down.shape[1] // span):
                fetch(
                    parts[s].at[pl.ds(2 * depth + j * strip, strip), :],
                    down.at[pl.ds(start, strip), pl.ds(j * span, span)],
                )
    for copy in started[:first]:
        copy.wait()
    flush(10)
    row = lax.broadcasted_iota(jnp.int32, (rows, rows), 0)
    col = lax.broadcasted_iota(jnp.int32, (rows, rows), 1)

    gate_pre = dot(x[...], gate[...])
    lifted = dot(x[...], up[...])
    sigmoid = jax.nn.sigmoid(gate_pre)
    activated = gate_pre * sigmoid
    for copy in started[first:]:
        copy.wait()
    flush(11)
    limits = []
    for r in range(members):
        line = jnp.broadcast_to(codes[r].astype(F32)[:1], (rows, rows))
        code = jnp.sum(jnp.where(row == col, line, 0.0), axis=1, keepdims=True)
        limits.append(
            sum(jnp.where(code == k, float(units >> (members - 1 - k)), 0.0) for k in range(members))
        )
    live = unit_index[:1, :] < jnp.concatenate(limits, axis=0)
    hidden[...] = jnp.where(live, activated * lifted, 0.0).astype(BF)
    grad_hidden = jnp.where(live, contract_cols(cot[...], down[...]), 0.0)
    wide = 2 * span
    grads_two[:, :wide] = (
        grad_hidden * lifted * sigmoid * (1.0 + gate_pre * (1.0 - sigmoid))
    ).astype(BF)
    grads_two[:, wide:] = (grad_hidden * activated).astype(BF)
    flush(12)
    flush(13)
    grads = contract_cols(grads_two[:, :wide], gate[...])
    grads += contract_cols(grads_two[:, wide:], up[...])
    split_parts(grads, rows, *splits[:5])
    for index in range(5):
        flush(index)
    split_parts(dot(hidden[...], down[...]), rows, *splits[5:])
    for index in range(5, 10):
        flush(index)
    for copy in finishing:
        copy.wait()


def unit_sums_kernel(n, depth, strip, *refs):
    given, outs, held = refs[:8], refs[8:10], refs[10:18]
    sums, in_sems, out_sems = refs[18:20], refs[20], refs[21]
    parts = held[:4], held[4:]
    span = n * strip
    fetched = [
        pltpu.make_async_copy(given[i], held[i], in_sems.at[i]) for i in (0, 3, 4, 7, 1, 2, 5, 6)
    ]
    for copy in fetched:
        copy.start()
    for copy in fetched[:4]:
        copy.wait()
    finishing = []

    def flush(half, plane, low, count):
        place = (plane, pl.ds(low, count), slice(None))
        copy = pltpu.make_async_copy(
            sums[half].at[place], outs[half].at[place], out_sems.at[len(finishing)]
        )
        copy.start()
        finishing.append(copy)

    for plane in range(n):
        block = slice(plane * depth, (plane + 1) * depth)
        made = sum(contract_rows(x[:, block], grads[...]) for x, _, _, grads in parts)
        for half in range(2):
            for k in range(2):
                low = (2 * k + half) * span
                value = made[:, low : low + span].astype(BF)
                sums[half][plane, k * depth : (k + 1) * depth, :] = value
            flush(half, plane, 0, 2 * depth)
    for copy in fetched[4:]:
        copy.wait()
    cuts = held[1].shape[1] // span
    for j in range(cuts):
        cols = slice(j * span, (j + 1) * span)
        made = sum(contract_rows(hidden[...], cot[:, cols]) for _, cot, hidden, _ in parts)
        made = made.astype(BF)
        for half in range(2):
            for plane in range(n):
                low, at = half * span + plane * strip, 2 * depth + j * strip
                sums[half][plane, at : at + strip, :] = made[low : low + strip]
    for half in range(2):
        for plane in range(n):
            flush(half, plane, 2 * depth, cuts * strip)
    for copy in finishing:
        copy.wait()


def move(kernel, outs, copies, operands, ins):
    kinds = {"h": pl.BlockSpec(memory_space=pl.ANY), "s": pl.BlockSpec(memory_space=pltpu.SMEM)}
    return pl.pallas_call(
        kernel,
        out_shape=[jax.ShapeDtypeStruct(shape, BF) for shape in outs],
        in_specs=[kinds[k] for k in ins],
        out_specs=[pl.BlockSpec(memory_space=pltpu.VMEM)] * len(outs),
        scratch_shapes=[pltpu.SemaphoreType.DMA((copies,))],
        compiler_params=pltpu.CompilerParams(vmem_limit_bytes=56 * 2**20),
        cost_estimate=small_cost(),
    )(*operands)


def local(
    tokens,
    seq_ids,
    granularity,
    w_qkv,
    w_out,
    gain_attn,
    gain_ffn,
    w_gate,
    w_up,
    w_down,
    out_cotangent,
):
    n = lax.axis_size("batch")
    g = lax.axis_size("gran")
    z = lax.axis_index("batch")
    p = lax.axis_index("gran")
    c = lax.axis_index("ffn")
    rows, width = tokens.shape
    head = width // H
    heads = H // g
    mine = heads * head
    depth = w_qkv.shape[0]
    units = w_gate.shape[2]
    capacity = max(2, (5 * rows + 4 * n * g - 1) // (4 * n * g))

    def hop(x, r):
        return lax.ppermute(x, "gran", [(i, i ^ r) for i in range(g)])

    def pair(x):
        return lax.ppermute(x, "batch", [(i, i ^ 1) for i in range(n)])

    def core(x):
        return lax.ppermute(x, "ffn", [(0, 1), (1, 0)])

    def ring(x, s):
        return lax.ppermute(x, "batch", [(i, (i + s) % n) for i in range(n)])

    def gather_first(x):
        return [x, hop(x, 1), hop(x, 2)]

    def gather_rest(pieces):
        half = pieces[0].shape[0] // 32 * 16 or pieces[0].shape[0] // 2
        return [*pieces, hop(pieces[1][:half], 2), hop(pieces[2][half:], 1)]

    def plane_gather(x):
        return gather_rest(gather_first(x))

    def as_members(pieces):
        return jnp.concatenate(pieces, axis=0).reshape(g, *pieces[0].shape)

    def split_rows(x):
        half = x.shape[1] // 2
        return (
            jnp.concatenate([x[1, :half], x[3, :half]], axis=0),
            jnp.concatenate([x[2, half:], x[3, half:]], axis=0),
            x[0],
            x[2, :half],
            x[1, half:],
        )

    def plane_reduce(to_one, to_two, own, two_low, one_high):
        return summed(*plane_reduce_rest(hop(to_one, 1), hop(to_two, 2), own, two_low, one_high))

    def plane_reduce_rest(got_one, got_two, own, two_low, one_high):
        half, columns = two_low.shape
        two_low, one_high, total = call(
            reduce_first_kernel,
            [((half, columns), BF), ((half, columns), BF), ((2 * half, columns), F32)],
            (),
            "v" * 5,
            (got_one, got_two, own, two_low, one_high),
        )
        return total, hop(two_low, 2), hop(one_high, 1)

    def summed(total, low, high):
        return total + jnp.concatenate([low, high], axis=0).astype(F32)

    def by_member(pieces):
        out = jnp.zeros((g, *pieces[0].shape), pieces[0].dtype)
        for r in range(g):
            out = lax.dynamic_update_index_in_dim(out, pieces[r], p ^ r, 0)
        return out

    def ordered(here, there, axis):
        return jnp.stack(
            [jnp.where(c == 0, here, there), jnp.where(c == 0, there, here)], axis=axis
        )

    def cut(*values):
        return lax.optimization_barrier(values)

    def together(body, *operands):
        made = jax.eval_shape(body, *operands)
        return lax.cond(
            seq_ids[0] >= 0,
            body,
            lambda *given: jax.tree.map(lambda v: jnp.zeros(v.shape, v.dtype), made),
            *operands,
        )

    place = jnp.stack([z, p, c]).astype(jnp.int32)
    hd, sub = depth // 2, depth // g
    hs, blocks = sub // 2, width // mine
    gain_part = jnp.concatenate(
        [first_rows(gain_attn, 8, mine), first_rows(gain_ffn, 8, mine)], axis=0
    )
    token_part = jnp.concatenate([tokens, first_rows(seq_ids, 16, width)], axis=0)
    codes = row_groups(seq_ids, granularity, capacity * n)
    grad_part = jnp.concatenate([out_cotangent, first_rows(codes, 16, width)], axis=0)
    if hs % 8 == 0:
        [first_part] = move(
            functools.partial(first_part_kernel, depth, mine, g),
            [(3 * hd + blocks * hs + 16, mine)],
            blocks + 4,
            (place, w_qkv, w_out, gain_part),
            "shhh",
        )
    else:
        out_part = lax.dynamic_slice(w_out, ((p * 2 + c) * hs, 0), (hs, width))
        first_part = jnp.concatenate(
            [
                lax.dynamic_slice(w_qkv, (c * hd, k * width + p * mine), (hd, mine))
                for k in range(3)
            ]
            + [out_part[:, k * mine : (k + 1) * mine] for k in range(blocks)]
            + [gain_part],
            axis=0,
        )
    shares = 2 * g
    strip = units // n // shares
    share = p * 2 + z % 2
    span = n * strip
    cuts = width // span

    def columns(w, odd):
        return lax.dynamic_index_in_dim(
            w.reshape(depth, n, shares, strip), share ^ odd, 2, keepdims=False
        ).reshape(depth, span)

    def second_part(odd):
        rows_down = lax.dynamic_index_in_dim(
            w_down.reshape(shares, strip, width), share ^ odd, 0, keepdims=False
        )
        return jnp.concatenate(
            [columns(w_gate, odd), columns(w_up, odd)]
            + [rows_down[:, k * span : (k + 1) * span] for k in range(cuts)],
            axis=0,
        )

    first_moved = [ring(first_part, k) for k in range(1, n)]

    def rows_out(first_part, token_part, grad_part):
        token_pieces = plane_gather(token_part)
        first_part, grad_part, *token_pieces = cut(first_part, grad_part, *token_pieces)
        grad_both = jnp.stack([grad_part, pair(grad_part)])
        return token_pieces, core(first_part), grad_both, second_part(0), second_part(1)

    token_pieces, own_far, grad_both, even_part, odd_part = together(
        rows_out, first_part, token_part, grad_part
    )
    even_part, odd_part, own_far, grad_both, *first_moved = cut(
        even_part, odd_part, own_far, grad_both, *first_moved
    )
    all_grads = lax.all_gather(grad_both, "gran", axis=0)
    first_pieces = [first_part, *first_moved]
    second_odd = {k: ring(odd_part, k) for k in range(1, n, 2)}

    all_rows = g * rows

    def unit(values):
        inverse = lax.rsqrt(jnp.mean(values * values, axis=-1, keepdims=True) + EPSILON)
        return values * inverse, inverse

    def attention(token_pieces, first_pieces, own_far):
        first_far = [own_far, *(core(v) for v in first_pieces[1:])]
        frequencies = ROPE_BASE ** (-(2.0 * jnp.arange(head // 2, dtype=F32)) / head)
        frequencies = jnp.broadcast_to(jnp.concatenate([frequencies, frequencies]), (8, head))
        all_normed, my_qkv, queries, keys, values, attended, cosines, sines, bias, gains = call(
            functools.partial(attend_kernel, n, rows, depth, mine, head),
            [
                ((all_rows, width), BF),
                ((width, 3 * mine), BF),
                ((all_rows, mine), BF),
                ((all_rows, mine), BF),
                ((all_rows, mine), BF),
                ((all_rows, mine), BF),
                ((all_rows, head), F32),
                ((all_rows, head), F32),
                ((all_rows, rows), F32),
                ((16, width), F32),
            ],
            [
                pltpu.VMEM((n, 16, mine), BF),
                pltpu.VMEM((all_rows, width), F32),
                pltpu.SemaphoreType.DMA((7 * n,)),
            ],
            "sv" + "v" * 5 + "h" * (2 * n),
            (place, frequencies, *token_pieces, *first_pieces, *first_far),
        )

        low, high = 3 * hd, 3 * hd + blocks * hs
        out_here = jnp.stack([v[low:high] for v in first_pieces])
        out_there = jnp.stack([v[low:high] for v in first_far])

        def out_part_for(r):
            picked = [
                ordered(*(lax.dynamic_index_in_dim(v, s, 0, keepdims=False) for v in (out_here, out_there)), 0)
                for s in [(z - (p ^ r) * (n // g) - j) % n for j in range(n // g)]
            ]
            return jnp.stack(picked)

        out_pieces = [out_part_for(0)] + [hop(out_part_for(r), r) for r in range(1, g)]
        if hs % 8 == 0:
            [my_out] = move(
                functools.partial(out_weight_kernel, n, g, hs, mine),
                [(mine, width)],
                n * 2 * blocks,
                (place, *out_pieces),
                "s" + "h" * g,
            )
        else:
            my_out = by_member(out_pieces).reshape(g, n // g, 2, blocks, hs, mine)
            my_out = my_out.transpose(1, 0, 2, 4, 3, 5).reshape(mine, width)
        attn_parts = call(
            functools.partial(project_kernel, rows),
            split_shapes(rows, width),
            (),
            "vv",
            (attended, my_out),
        )

        kept = (all_normed, my_qkv, my_out, queries, keys, values, attended, cosines, sines, bias)
        return kept, gains, attn_parts

    kept, gains, attn_parts = together(attention, token_pieces, first_pieces, own_far)
    even_part, *got = cut(even_part, *attn_parts, *second_odd.values())
    attn_parts, second_odd = got[:5], dict(zip(second_odd, got[5:]))
    second_even = {k: ring(even_part, k) for k in range(2, n, 2)}

    def attention_end(attn_parts, even_part, odd_parts):
        to_one, to_two, *waiting = attn_parts
        got_one, got_two, even_part, *odd_far = cut(
            hop(to_one, 1), hop(to_two, 2), even_part, *(core(v) for v in odd_parts)
        )
        reduced, own_far = cut(plane_reduce_rest(got_one, got_two, *waiting), core(even_part))
        middle = tokens.astype(F32) + summed(*reduced)
        unit_second, inverse_second = unit(middle)
        normed_ffn = (unit_second * gains[8:9]).astype(BF)
        far_rows = pair(normed_ffn)
        own_pieces = plane_gather(normed_ffn)
        return middle, unit_second, inverse_second, own_pieces, gather_first(far_rows), own_far, odd_far

    middle, unit_second, inverse_second, own_pieces, far_pieces, own_far, odd_far = together(
        attention_end, attn_parts, even_part, list(second_odd.values())
    )
    all_normed, my_qkv, my_out, queries, keys, values, attended, cosines, sines, bias = kept
    gain_first, gain_second = gains[0:1], gains[8:9]
    residual = tokens.astype(F32)
    *got, all_grads = cut(*own_pieces, *far_pieces, *second_even.values(), all_grads)
    own_pieces, far_pieces, second_even = got[:5], got[5:8], dict(zip(second_even, got[8:]))
    odd_far = dict(zip(second_odd, odd_far))
    even_far = {k: core(v) for k, v in second_even.items()}
    second_here = {0: even_part, **second_odd, **second_even}
    second_far = {0: own_far, **odd_far, **even_far}
    second_here = [second_here[k] for k in range(n)]
    second_far = [second_far[k] for k in range(n)]

    index = jnp.arange(2 * span, dtype=jnp.int32) % span
    unit_index = (index // strip) * (strip * shares) + share * strip + index % strip
    fast_units = strip % 16 == 0

    def feed_forward(e, row_pieces):
        if fast_units:
            shapes = split_shapes(rows, width) * 2
            shapes += [((all_rows, width), BF)] * 2
            shapes += [((all_rows, 2 * span), BF), ((all_rows, 4 * span), BF)]
            got = call(
                functools.partial(feed_forward_kernel, n, g, depth, strip, rows, e),
                shapes,
                [pltpu.VMEM(*v) for v in shapes]
                + [
                    pltpu.VMEM((width, 2 * span), BF),
                    pltpu.VMEM((width, 2 * span), BF),
                    pltpu.VMEM((2 * span, width), BF),
                    pltpu.VMEM((g, 16, rows), BF),
                    pltpu.SemaphoreType.DMA((5 + 2 * n * (2 + cuts) + 2 * g,)),
                    pltpu.SemaphoreType.DMA((14,)),
                ],
                "sv" + "h" * (6 + 2 * n),
                (
                    place,
                    jnp.broadcast_to(unit_index.astype(F32), (8, 2 * span)),
                    *row_pieces,
                    all_grads,
                    *second_here,
                    *second_far,
                ),
                out="h",
                spare=16,
            )
            return got[:5], got[5:10], got[10:]
        group_rows = jnp.concatenate(row_pieces, axis=0)
        stacks = []
        for pieces in (second_here, second_far):
            out = jnp.zeros((n, *pieces[0].shape), BF)
            for k in range(n):
                out = lax.dynamic_update_index_in_dim(out, pieces[k], (z - k) % n, 0)
            stacks.append(out)
        gate_matrix, up_matrix = (
            jnp.concatenate(
                [v[:, k * depth : (k + 1) * depth].reshape(width, span) for v in stacks], axis=1
            )
            for k in (0, 1)
        )
        down_matrix = jnp.concatenate(
            [v[:, 2 * depth :].reshape(n, cuts, strip, span).transpose(0, 2, 1, 3) for v in stacks],
            axis=0,
        ).reshape(2 * span, width)
        grad_got = jnp.stack(
            [lax.dynamic_index_in_dim(all_grads, p ^ r, 0, keepdims=False)[e] for r in range(g)]
        )
        group_grads = grad_got[:, :rows].reshape(all_rows, width)
        group_codes = grad_got[:, rows, :rows].reshape(all_rows, 1).astype(jnp.int32)
        group_limits = jnp.where(
            group_codes < 0, 0, jnp.right_shift(jnp.int32(units), jnp.minimum(3 - group_codes, 3))
        )
        live = unit_index[None, :] < group_limits
        gate_pre = dot(group_rows, gate_matrix)
        lifted = dot(group_rows, up_matrix)
        sigmoid_gate = jax.nn.sigmoid(gate_pre)
        activated = gate_pre * sigmoid_gate
        hidden = jnp.where(live, (activated * lifted).astype(BF), jnp.zeros((), BF))
        grad_hidden = jnp.where(live, contract_cols(group_grads, down_matrix), 0.0)
        grad_gate = (
            grad_hidden * lifted * sigmoid_gate * (1.0 + gate_pre * (1.0 - sigmoid_gate))
        ).astype(BF)
        grad_lifted = (grad_hidden * activated).astype(BF)
        partial_input = (
            contract_cols(grad_gate, gate_matrix) + contract_cols(grad_lifted, up_matrix)
        ).astype(BF)
        partial_ffn = dot(hidden, down_matrix).astype(BF)
        return (
            list(split_rows(partial_input.reshape(g, rows, width))),
            list(split_rows(partial_ffn.reshape(g, rows, width))),
            [group_rows, group_grads, hidden, jnp.concatenate([grad_gate, grad_lifted], axis=1)],
        )

    def unit_grads(own, far):
        if fast_units:
            return call(
                functools.partial(unit_sums_kernel, n, depth, strip),
                [((n, 2 * depth + cuts * strip, span), BF)] * 2,
                [pltpu.VMEM(v.shape, BF) for v in (*own, *far)]
                + [pltpu.VMEM((n, 2 * depth + cuts * strip, span), BF)] * 2
                + [pltpu.SemaphoreType.DMA((8,)), pltpu.SemaphoreType.DMA((4 * n,))],
                "h" * 8,
                (*own, *far),
                out="h",
                spare=16,
            )
        group_rows, group_grads, hidden, grads_two = (
            jnp.concatenate([v, w], axis=0) for v, w in zip(own, far)
        )

        def half_grads(half):
            low = slice(half * span, (half + 1) * span)
            made = contract_rows(hidden[:, low], group_grads).astype(BF)
            made = made.reshape(n, strip, cuts, span).transpose(0, 2, 1, 3)
            return jnp.concatenate(
                [
                    contract_rows(group_rows, v[:, low]).astype(BF).reshape(n, depth, span)
                    for v in (grads_two[:, : 2 * span], grads_two[:, 2 * span :])
                ]
                + [made.reshape(n, cuts * strip, span)],
                axis=1,
            )

        return [half_grads(0), half_grads(1)]

    far_pieces = gather_rest(list(far_pieces))
    own_out = together(functools.partial(feed_forward, 0), own_pieces)
    (own_input, own_ffn, own_saved), far_pieces = cut(own_out, far_pieces)
    to_one, to_two, *own_waiting = own_input
    own_got, (far_input, far_ffn, far_saved) = cut(
        (hop(to_one, 1), hop(to_two, 2)), together(functools.partial(feed_forward, 1), far_pieces)
    )
    to_one, to_two, *far_waiting = far_input
    own_half, far_got, (sums_here, sums_there) = cut(
        plane_reduce_rest(*own_got, *own_waiting),
        (hop(to_one, 1), hop(to_two, 2)),
        together(unit_grads, own_saved, far_saved),
    )
    far_sum, far_sums = cut(plane_reduce_rest(*far_got, *far_waiting), core(sums_there))
    far_sum = summed(*far_sum)

    def unit_sums(k):
        here, there = (
            lax.dynamic_index_in_dim(v, k, 0, keepdims=False).astype(F32)
            for v in (sums_here, far_sums)
        )
        return (here + there).astype(BF)

    def mixed(own, far):
        half = own.shape[0] // 2
        return jnp.concatenate([own[:half], far[:half], own[half:], far[half:]], axis=0)

    far_half = pair(far_sum.astype(BF))
    to_one, to_two, branch_own = (mixed(v, w) for v, w in zip(own_ffn[:3], far_ffn[:3]))
    branch_waiting = [branch_own] + [
        jnp.concatenate([v, w], axis=0) for v, w in zip(own_ffn[3:], far_ffn[3:])
    ]
    to_one, to_two = cut(to_one, to_two, far_sum)[:2]
    branch_got = hop(to_one, 1), hop(to_two, 2)
    messages = [unit_sums((z + k) % n) for k in range(n)]
    far_half, *messages = cut(far_half, *messages)
    sums = [messages[0].astype(F32), 0.0]
    moved = [ring(messages[k], k) for k in range(1, n)]

    def my_half(x, which, axis):
        return lax.dynamic_index_in_dim(x, which, axis, keepdims=False)

    def for_member(stacked, r, axis):
        return lax.dynamic_index_in_dim(stacked, p ^ r, axis, keepdims=False)

    def attention_back(own_half, far_half, branch_got):
        grad_normed_ffn = (summed(*own_half) + far_half.astype(F32)).astype(BF).astype(F32)
        grad_middle = out_cotangent.astype(F32) + norm_back(
            grad_normed_ffn, unit_second, inverse_second, gain_second
        )
        branch_pieces = plane_gather(grad_middle.astype(BF))
        fast = n == g and hs % 16 == 0
        if fast:
            branch_rows = jnp.concatenate(branch_pieces, axis=0)
            out_here, out_there = call(
                functools.partial(out_sums_kernel, g, hs, mine),
                [((g, blocks * hs, mine), BF)] * 2,
                [pltpu.VMEM((mine, mine), F32)],
                "svv",
                (place, attended, branch_rows),
            )
            out_there, *branch_pieces = cut(core(out_there), *branch_pieces)
            out_sum = (out_here.astype(F32) + out_there.astype(F32)).astype(BF)
        got_one, got_two, *branch_pieces = cut(*branch_got, *branch_pieces)
        branch_sum = plane_reduce_rest(got_one, got_two, *branch_waiting)
        grad_branch, grad_packed, *normed_parts = call(
            functools.partial(attend_back_kernel, rows, mine, head),
            [((all_rows, width), BF), ((all_rows, 3 * mine), BF), *split_shapes(rows, width)],
            [pltpu.VMEM((all_rows, mine), BF)],
            "v" * 13,
            (*branch_pieces, my_out, my_qkv, queries, keys, values, cosines, sines, bias),
        )
        branch_sum, grad_packed = cut(branch_sum, grad_packed)
        if fast:
            quarters = [hop(for_member(after(out_sum, grad_packed), r, 0), r) for r in (1, 2)]
            sum_here, sum_there = call(
                functools.partial(weight_sums_kernel, g, depth, mine),
                [((g, 3 * hd, mine), BF)] * 2,
                [pltpu.VMEM((depth, 3 * mine), F32)],
                "svv",
                (place, all_normed, grad_packed),
            )
            sum_there, out_sum, *quarters = cut(sum_there, out_sum, *quarters)
            quarters.append(hop(for_member(out_sum, 3, 0), 3))
            weight_sum = (sum_here.astype(F32) + core(sum_there).astype(F32)).astype(BF)
            last_parts = call(
                functools.partial(last_parts_kernel, g, 3 * hd),
                [((3 * hd + blocks * hs, mine), BF)] * g,
                [pltpu.VMEM((g, blocks * hs, mine), BF)],
                "s" + "v" * (g + 1),
                (place, weight_sum, for_member(out_sum, 0, 0), *quarters),
            )
        else:
            out_grad = contract_rows(attended, grad_branch).astype(BF)
            out_grad = out_grad.reshape(n // g, g, 2, hs, width)
            out_sum = my_half(out_grad, c, 2).astype(F32)
            out_sum = (out_sum + core(my_half(out_grad, 1 - c, 2)).astype(F32)).astype(BF)
            out_sum = by_member(
                [for_member(out_sum, 0, 1)]
                + [hop(for_member(out_sum, r, 1), r) for r in range(1, g)]
            ).reshape(n, hs, blocks, mine)
            qkv_grad = contract_rows(all_normed, grad_packed).astype(BF).reshape(n, 2, hd, 3, mine)
            qkv_sum = my_half(qkv_grad, c, 1).astype(F32)
            qkv_sum += core(my_half(qkv_grad, 1 - c, 1)).astype(F32)
            last_part = jnp.concatenate(
                [
                    qkv_sum.astype(BF).transpose(0, 2, 1, 3).reshape(n, 3 * hd, mine),
                    out_sum.transpose(0, 2, 1, 3).reshape(n, blocks * hs, mine),
                ],
                axis=1,
            )
            last_parts = [
                lax.dynamic_index_in_dim(last_part, (z + k) % n, 0, keepdims=False) for k in range(n)
            ]
        normed_parts = cut(*normed_parts, *last_parts)[:5]
        to_one, to_two, *waiting = normed_parts
        normed_sum = plane_reduce_rest(hop(to_one, 1), hop(to_two, 2), *waiting)
        return grad_middle, normed_sum, last_parts, branch_sum

    grad_middle, normed_sum, last_parts, branch_sum = together(
        attention_back, own_half, far_half, branch_got
    )
    cut_values = cut(*moved, *last_parts)
    moved, last_parts = cut_values[: n - 1], cut_values[n - 1 :]
    for k in range(1, n):
        sums[k % 2] += moved[k - 1].astype(F32)
    pair_sums = jnp.concatenate([v.astype(BF) for v in sums], axis=0)
    last_moved = [ring(last_parts[k], k) for k in range(1, n)]

    def rows_done(pair_sums, branch_sum, normed_sum):
        unit_pieces = plane_gather(pair_sums)
        unit_first, inverse_first = unit(residual)
        input_grad = grad_middle + norm_back(
            summed(*normed_sum), unit_first, inverse_first, gain_first
        )
        branch = summed(*branch_sum).reshape(2, 2, rows // 2, width)
        branch_ffn, branch_far = (branch[:, k].reshape(rows, width) for k in (0, 1))
        return unit_pieces, input_grad.astype(BF), branch_ffn, branch_far.astype(BF)

    unit_pieces, input_grad, branch_ffn, branch_far = together(
        rows_done, pair_sums, branch_sum, normed_sum
    )
    got = cut(*unit_pieces, *last_moved)
    unit_pieces, last_moved = got[:5], got[5:]
    last_sum = last_parts[0].astype(F32) + sum(v.astype(F32) for v in last_moved)
    last_one = gather_first(last_sum.astype(BF))
    if strip % 32 == 0:
        share_gate, share_up, ffn_part = call(
            functools.partial(columns_results_kernel, n, g, depth, strip, 2 * depth + cuts * strip),
            [
                ((depth * units // 128, 128), F32),
                ((depth * units // 128, 128), F32),
                ((depth, 1), F32),
            ],
            [
                pltpu.VMEM((shares, depth, span), BF),
                pltpu.VMEM((shares, depth, span), BF),
                pltpu.SemaphoreType.DMA((2, shares)),
            ],
            "s" + "h" * 5 + "vv",
            (place, *unit_pieces, w_gate[:, 0], w_up[:, 0]),
        )
        ffn_part = ffn_part[:, 0]
    else:
        got = as_members(unit_pieces).reshape(g, 2, -1, span)
        all_units = jnp.zeros((shares, *got.shape[2:]), BF)
        for r in range(g):
            for odd in (0, 1):
                all_units = lax.dynamic_update_index_in_dim(
                    all_units, got[r, odd], (p ^ r) * 2 + (z % 2) ^ odd, 0
                )

        def columns_back(pieces):
            return (
                pieces.reshape(shares, depth, n, strip)
                .transpose(1, 2, 0, 3)
                .reshape(depth, units)
                .astype(F32)
            )

        share_gate = columns_back(all_units[:, :depth])
        share_up = columns_back(all_units[:, depth : 2 * depth])
        share_down = (
            all_units[:, 2 * depth :]
            .reshape(shares, cuts, strip, span)
            .transpose(0, 2, 1, 3)
            .reshape(units // n, width)
            .astype(F32)
        )
        ffn_part = jnp.sum(
            share_gate * w_gate[:, 0].astype(F32) + share_up * w_up[:, 0].astype(F32), axis=1
        )
    *last_one, ffn_part = cut(*last_one, ffn_part)
    last_pieces = gather_rest(last_one)
    if strip % 32 == 0:
        [share_down] = call(
            functools.partial(rows_results_kernel, n, g, depth, strip, 2 * depth + cuts * strip),
            [((units // n * width // 128, 128), F32)],
            [pltpu.VMEM((shares, cuts * strip, span), BF), pltpu.SemaphoreType.DMA((shares,))],
            "s" + "h" * 5,
            (place, *cut(*unit_pieces, ffn_part)[:5]),
        )
        *last_rest, share_down = cut(*last_pieces[3:], share_down)
        last_pieces[3:] = last_rest
    share_gain_ffn = (ffn_part + core(ffn_part)) / gain_ffn.astype(F32)
    branch_ffn += pair(branch_far).astype(F32)
    outputs = (middle + branch_ffn.astype(BF).astype(F32)).astype(BF)
    if hs % 16 == 0:
        share_qkv, share_out, attn_part = call(
            functools.partial(attention_results_kernel, g, depth, mine),
            [((depth, 3 * width), F32), ((depth, width), F32), ((depth, 1), F32)],
            [
                pltpu.VMEM((depth, 3 * width), BF),
                pltpu.VMEM((depth, width), BF),
                pltpu.SemaphoreType.DMA((2 * (g + 1) * (3 + blocks),)),
            ],
            "s" + "h" * 10 + "v",
            (place, *last_pieces, *(core(v) for v in last_pieces), w_qkv),
        )
        attn_part = attn_part[:, 0]
    else:
        last_got = as_members(last_pieces)
        last_got = by_member([last_got[r] for r in range(g)])
        last_both = ordered(last_got, core(last_got), 0)
        share_qkv = (
            last_both[:, :, : 3 * hd]
            .reshape(2, g, 3, hd, mine)
            .transpose(0, 3, 2, 1, 4)
            .reshape(depth, 3 * width)
            .astype(F32)
        )
        share_out = (
            last_both[:, :, 3 * hd :]
            .reshape(2, g, blocks, hs, mine)
            .transpose(1, 0, 3, 2, 4)
            .reshape(depth, width)
            .astype(F32)
        )
        attn_part = jnp.sum(share_qkv * w_qkv.astype(F32), axis=1)
    share_gain_attn = attn_part / gain_attn.astype(F32)
    return (
        outputs,
        input_grad,
        share_qkv,
        share_out,
        share_gain_attn,
        share_gain_ffn,
        share_gate.reshape(depth, 1, units),
        share_up.reshape(depth, 1, units),
        share_down.reshape(units // n, 1, width),
    )


def solution(mesh):
    in_specs = (
        P(("batch", "gran", "ffn"), None),
        P(("batch", "gran", "ffn")),
        P(("batch", "gran", "ffn")),
        P("batch", None),
        P("batch", None),
        P("batch"),
        P("batch"),
        P("batch", "ffn", None),
        P("batch", "ffn", None),
        P("batch", "ffn", None),
        P(("batch", "gran", "ffn"), None),
    )
    out_specs = (
        P(("batch", "gran", "ffn"), None),
        P(("batch", "gran", "ffn"), None),
        P("batch", None),
        P("batch", None),
        P("batch"),
        P("batch"),
        P("batch", "ffn", None),
        P("batch", "ffn", None),
        P("batch", "ffn", None),
    )
    return jax.shard_map(local, mesh=mesh, in_specs=in_specs, out_specs=out_specs, check_vma=False)
```
